32 devices in a mesh: chan: 16 (over z, y, core), tm: 2 (over x).
Axes of the slice: x: 2, y: 2, z: 4, core: 2. Of those that a mesh axis runs over, the one named last changes fastest.
Arguments:
- samples: bfloat16 [256, 4096], P('chan', 'tm'), may hold values from -6 to 6
- fir_taps: float32 [96], replicated, may hold values from -0.625 to 0.625
- plan: int32 [4], replicated, may hold values from 1 to 15, as said below
Outputs:
- self_corr: float32 [256, 16, 129], P(('chan', 'tm'))
- pair_corr: float32 [4, 256, 16, 129], P(None, ('chan', 'tm'))
The draws below stay inside these ranges and needn't reach their ends.
Inputs may be any that keep to these rules, and one draw needn't show every extreme that they name: Round r pairs block g with block g XOR plan[r]; the masks of the rounds are distinct, and the values 1 and 15 both occur.
All inputs are finite; a program needn't handle non-finite values.
Results may differ from the reference program's by a relative error of at most 0.0043.
Values may be sent and summed in bfloat16 or wider, within the bound.
No kernel may reach another device: no remote copies, remote signals or barrier semaphores. Data moves between devices by JAX's collectives and lax.ppermute only.
A program may use at most 128 MiB of HBM per device.

```python
import math
import jax
import jax.numpy as jnp
from jax import lax

CH_DEV = 16
SEG = 1024
TAPS = 96
LAGS = 129
ROUNDS = 4
HALF = 513
CHANNELS = 256
SEGMENTS = 4
TIME = 4096
N_CHAN = 16


def draw_plan(key, part):
    key = jax.random.fold_in(key, 11)
    key_masks, key_order = jax.random.split(key)
    inner_masks = jax.random.permutation(key_masks, N_CHAN - 3)[:ROUNDS - 2] + 2
    all_masks = jnp.concatenate([jnp.array([1, N_CHAN - 1], jnp.int32), inner_masks.astype(jnp.int32)])
    return jax.random.permutation(key_order, all_masks).astype(jnp.int32)


def block_scale(stream_key, shape, pieces, low, top_value):
    factor_of = 1.0
    for axis_at, parts in pieces:
        draws = jax.random.uniform(jax.random.fold_in(jax.random.fold_in(stream_key, 6), axis_at), (parts,), jnp.float32, low / len(pieces), top_value / len(pieces))
        factor_of = factor_of * jnp.repeat(jnp.exp(draws), shape[axis_at] // parts).reshape((-1,) + (1,) * (len(shape) - 1 - axis_at))
    return factor_of


def bell_draw(stream_key, dims, spread, bound, cuts=(), held_as=jnp.bfloat16):
    loudness = block_scale(stream_key, dims, cuts, -0.22, 0.18) if cuts else 1.0
    result = jax.random.normal(stream_key, dims, jnp.float32) * spread * loudness
    return jnp.minimum(jnp.maximum(result, -bound), bound).astype(held_as)


def setup_inputs(seed: int = 0) -> dict:
    key_of = jax.random.split(jax.random.key(seed), 4)
    samples = bell_draw(key_of[0], (CHANNELS, TIME), 1.0, 6.0, ((0, 16), (1, 2)))
    fir_taps = bell_draw(key_of[1], (TAPS,), TAPS ** -0.5, 0.625, (), jnp.float32)
    plan = draw_plan(jax.random.fold_in(key_of[3], 71), 0)
    return {"samples": samples, "fir_taps": fir_taps, "plan": plan}


def dft_matrix(length, half):
    sample_index = jnp.arange(length, dtype=jnp.int32)[:, None]
    freq_index = jnp.arange(half, dtype=jnp.int32)[None, :]
    angles = 2.0 * math.pi / length * (sample_index * freq_index % length).astype(jnp.float32)
    return jnp.concatenate([jnp.cos(angles), -jnp.sin(angles)], axis=1)

def fir_filter(extended, fir_taps, length):
    rim_width = fir_taps.shape[0] - 1
    widened = extended.astype(jnp.float32)
    summed = jnp.zeros((extended.shape[0], length), jnp.float32)
    for tap_index in range(rim_width + 1):
        begin = rim_width - tap_index
        summed = summed + fir_taps[tap_index] * widened[:, begin:begin + length]
    return summed

def whiten(filtered, matrix):
    spectrum = jnp.dot(filtered, matrix, precision=lax.Precision.HIGHEST, preferred_element_type=jnp.float32)
    half = matrix.shape[1] // 2
    real_part = spectrum[:, :half]
    imag_part = spectrum[:, half:]
    energy = real_part * real_part + imag_part * imag_part
    water_level = 0.1 * lax.optimization_barrier(jnp.mean(energy, axis=1, keepdims=True))
    inverse_amp = lax.rsqrt(energy + water_level + 1e-06)
    return jnp.concatenate([real_part * inverse_amp, imag_part * inverse_amp], axis=1).astype(jnp.bfloat16)

def rotate(spectra, lag_count):
    half = spectra.shape[-1] // 2
    length = 2 * (half - 1)
    lag_value = jnp.arange(lag_count, dtype=jnp.int32) - lag_count // 2
    freq_index = jnp.arange(half, dtype=jnp.int32)
    angles = 2.0 * math.pi / length * (lag_value[:, None] * freq_index[None, :] % length).astype(jnp.float32)
    edges = (freq_index == 0) | (freq_index == half - 1)
    weight = jnp.where(edges, 1.0, 2.0).astype(jnp.float32) / length
    cosine = jnp.cos(angles) * weight
    sinus = jnp.sin(angles) * weight
    real_part = spectra[..., :half].astype(jnp.float32)[..., None, :]
    imag_part = spectra[..., half:].astype(jnp.float32)[..., None, :]
    rot_real = real_part * cosine - imag_part * sinus
    rot_imag = imag_part * cosine + real_part * sinus
    return jnp.concatenate([rot_real, rot_imag], axis=-1).astype(jnp.bfloat16)

def correlate_stack(rotated, partner):
    return jnp.einsum('talk,tbk->abl', rotated.astype(jnp.float32), partner.astype(jnp.float32), precision=lax.Precision.HIGHEST)

def reference(samples, fir_taps, plan):
    leading = jnp.zeros((CHANNELS, TAPS - 1), jnp.bfloat16)
    filtered = fir_filter(jnp.concatenate([leading, samples], axis=1), fir_taps, TIME)
    segments = filtered.reshape(CHANNELS, SEGMENTS, SEG).transpose(1, 0, 2).reshape(SEGMENTS * CHANNELS, SEG)
    spectra = whiten(segments, dft_matrix(SEG, HALF))
    spectra = spectra.reshape(SEGMENTS, N_CHAN, CH_DEV, 2 * HALF).transpose(1, 0, 2, 3)

    def per_block(block_index):
        own_spectra = spectra[block_index]
        rotated = rotate(own_spectra, LAGS)
        self_term = correlate_stack(rotated, own_spectra)
        pair_terms = []
        for round_index in range(ROUNDS):
            partner_index = jnp.bitwise_xor(block_index, plan[round_index]).astype(jnp.int32)
            pair_terms.append(correlate_stack(rotated, spectra[partner_index]))
        return (self_term, jnp.stack(pair_terms))
    self_all, pair_all = lax.map(per_block, jnp.arange(N_CHAN, dtype=jnp.int32))
    self_corr = self_all.reshape(CHANNELS, CH_DEV, LAGS)
    pair_corr = pair_all.transpose(1, 0, 2, 3, 4).reshape(ROUNDS, CHANNELS, CH_DEV, LAGS)
    return (self_corr, pair_corr)
```

```python
import functools
import math

import jax
import jax.numpy as jnp
import ml_dtypes
import numpy as np
from jax import lax
from jax.experimental import pallas as pl
from jax.experimental.pallas import tpu as pltpu
from jax.sharding import PartitionSpec as P

SEGS_DEV = 2
LAGS = 129
ROUNDS = 4
LANE = 128


def split_table(table):
    high = table.astype(ml_dtypes.bfloat16)
    low = (table - high.astype(np.float64)).astype(ml_dtypes.bfloat16)
    return high, low


def tables(length):
    half = length // 2
    quarter = length // 4
    sample = np.arange(half)[:, None]

    def columns(freqs):
        angle = 2.0 * math.pi / length * (sample * freqs[None, :] % length)
        return np.cos(angle), -np.sin(angle)

    even = 2 * np.arange(quarter)
    odd = even + 1
    even_re, even_im = columns(even)
    even_im[:, 0] = 1.0 - 2.0 * (np.arange(half) % 2)
    odd_re, odd_im = columns(odd)
    even_table = np.concatenate([even_re, even_im], axis=1)
    odd_table = np.concatenate([odd_re, odd_im], axis=1)

    freqs = np.concatenate([even, odd])[:, None]
    lag = (np.arange(LAGS) - LAGS // 2)[None, :]
    angle = 2.0 * math.pi / length * (lag * freqs % length)
    weight = np.where(freqs == 0, 1.0, 2.0) / length
    lag_cos = weight * np.cos(angle)
    lag_sin = weight * np.sin(angle)
    lag_sin[0] = (1.0 - 2.0 * (np.abs(lag[0]) % 2)) / length
    lag_table = np.zeros((length, 2 * LANE))
    lag_table[:, :LAGS] = np.concatenate([lag_cos, lag_sin], axis=0)
    return (
        *split_table(even_table),
        *split_table(odd_table),
        lag_table.astype(ml_dtypes.bfloat16),
    )


def dot(left, right):
    return jnp.dot(left, right, preferred_element_type=jnp.float32)


def correlate_kernel(
    parts,
    info,
    own,
    part_0,
    part_1,
    part_2,
    part_3,
    taps,
    even_hi,
    even_lo,
    odd_hi,
    odd_lo,
    lag_table,
    mine,
    others,
    sums,
    diffs,
    real_ref,
    imag_ref,
    left_ref,
    cross,
    result,
):
    blocks = (own, part_0, part_1, part_2, part_3)
    chans = own.shape[0]
    rows_blk = SEGS_DEV * chans
    rows = rows_blk * len(blocks)
    half = even_hi.shape[0]
    quarter = half // 2
    pieces = half // LANE

    base = jnp.broadcast_to(taps[...], (2 * LANE, 2 * LANE))
    toeplitz = pltpu.roll(base, LANE, 1, stride=1, stride_axis=0)[:, :LANE]
    toep_hi = toeplitz.astype(jnp.bfloat16)
    toep_lo = (toeplitz - toep_hi.astype(jnp.float32)).astype(jnp.bfloat16)
    toep = jnp.concatenate([toep_hi, toep_lo], axis=1)

    for q, block in enumerate(blocks):
        windows = jnp.concatenate(
            [block[:, LANE * k : LANE * (k + 2)] for k in range(2 * pieces * SEGS_DEV)], axis=0
        )
        both = dot(windows, toep)
        filtered = both[:, :LANE] + both[:, LANE:]
        for s in range(SEGS_DEV):
            row = q * rows_blk + s * chans
            for k in range(pieces):
                lo = (s * 2 * pieces + k) * chans
                hi = lo + pieces * chans
                first, second = filtered[lo : lo + chans], filtered[hi : hi + chans]
                for ref, value in ((sums, first + second), (diffs, first - second)):
                    high = value.astype(jnp.bfloat16)
                    low = (value - high.astype(jnp.float32)).astype(jnp.bfloat16)
                    ref[row : row + chans, LANE * k : LANE * (k + 1)] = high
                    ref[rows + row : rows + row + chans, LANE * k : LANE * (k + 1)] = low

    def transform(values, table_hi, table_lo):
        main = dot(values[...], table_hi[...])
        return main[:rows] + main[rows:] + dot(values[:rows, :], table_lo[...])

    even = transform(sums, even_hi, even_lo)
    odd = transform(diffs, odd_hi, odd_lo)
    real = jnp.concatenate([even[:, :quarter], odd[:, :quarter]], axis=1)
    imag = jnp.concatenate([even[:, quarter:], odd[:, quarter:]], axis=1)
    edge = lax.broadcasted_iota(jnp.int32, real.shape, 1) == 0
    real_sq = real * real
    imag_sq = imag * imag
    level = 0.1 / (half + 1) * jnp.sum(real_sq + imag_sq, axis=1, keepdims=True) + 1e-06
    inv_real = lax.rsqrt(real_sq + jnp.where(edge, 0.0, imag_sq) + level)
    inv_imag = jnp.where(edge, lax.rsqrt(imag_sq + level), inv_real)
    real = (real * inv_real).astype(jnp.bfloat16).astype(jnp.float32)
    imag = (imag * inv_imag).astype(jnp.bfloat16).astype(jnp.float32)
    real_ref[...] = real
    imag_ref[...] = imag
    lefts = (real, jnp.where(edge, 0.0, imag), jnp.where(edge, imag, real))
    for a in range(chans):
        for s in range(SEGS_DEV):
            row = s * chans + a
            for j, value in enumerate(lefts):
                at = SEGS_DEV * j + s
                left_ref[a, at : at + 1, :] = value[row : row + 1]

    out_rows = chans * len(blocks)

    @pl.loop(0, chans)
    def _(a):
        at = pl.multiple_of(a * out_rows, out_rows)
        for c in range(pieces):
            cols = slice(LANE * c, LANE * (c + 1))
            left = [
                jnp.broadcast_to(left_ref[a, j : j + 1, cols], (chans, LANE))
                for j in range(3 * SEGS_DEV)
            ]
            for q in range(len(blocks)):
                cos_part = sin_part = 0.0
                for s in range(SEGS_DEV):
                    row_b = slice(q * rows_blk + s * chans, q * rows_blk + (s + 1) * chans)
                    re_b, im_b = real_ref[row_b, cols], imag_ref[row_b, cols]
                    re_a, im_a, x_a = (left[SEGS_DEV * j + s] for j in range(3))
                    cos_part += re_a * re_b + im_a * im_b
                    sin_part += x_a * im_b - im_a * re_b
                at_q = pl.ds(at + q * chans, chans)
                cross[at_q, cols] = cos_part.astype(jnp.bfloat16)
                cross[at_q, half + LANE * c : half + LANE * (c + 1)] = sin_part.astype(jnp.bfloat16)

    result[...] = dot(cross[...], lag_table[...])

    place = info[0]
    share = chans // parts
    for j in range(parts):
        owner = lax.rem(place + j, parts)

        @pl.loop(0, share)
        def _(i, j=j, owner=owner):
            at = pl.multiple_of((owner * share + i) * out_rows, out_rows)
            for q in range(len(blocks)):
                slot = 0 if q == 0 else info[q]
                value = result[pl.ds(at + q * chans, chans), :LAGS]
                if j == 0:
                    mine[slot, i] = value
                else:
                    others[j - 1, slot, i] = value.astype(jnp.bfloat16)


def correlate(info, own, partners, fir_taps, parts):
    chans = own.shape[0]
    length = (own.shape[1] - LANE) // SEGS_DEV
    half = length // 2
    sets = ROUNDS + 1
    rows = sets * SEGS_DEV * chans
    taps = jnp.pad(fir_taps, (0, 2 * LANE - fir_taps.shape[0]))[None]
    vmem = pl.BlockSpec(memory_space=pltpu.VMEM)
    smem = pl.BlockSpec(memory_space=pltpu.SMEM)
    share = chans // parts
    return pl.pallas_call(
        functools.partial(correlate_kernel, parts),
        out_shape=(
            jax.ShapeDtypeStruct((sets, share, chans, LAGS), jnp.float32),
            jax.ShapeDtypeStruct((parts - 1, sets, share, chans, LAGS), jnp.bfloat16),
        ),
        in_specs=[smem] + [vmem] * 11,
        out_specs=(vmem, vmem),
        scratch_shapes=[
            pltpu.VMEM((2 * rows, half), jnp.bfloat16),
            pltpu.VMEM((2 * rows, half), jnp.bfloat16),
            pltpu.VMEM((rows, half), jnp.float32),
            pltpu.VMEM((rows, half), jnp.float32),
            pltpu.VMEM((chans, 3 * SEGS_DEV, half), jnp.float32),
            pltpu.VMEM((sets * chans * chans, length), jnp.bfloat16),
            pltpu.VMEM((sets * chans * chans, 2 * LANE), jnp.float32),
        ],
        compiler_params=pltpu.CompilerParams(vmem_limit_bytes=32 * 1024 * 1024),
    )(info, own, *partners, taps, *tables(length))


def from_partner(block, axis, mask):
    count = lax.axis_size(axis)
    return lax.ppermute(block, axis, [(i, i ^ mask) for i in range(count)])


def on_device(samples, fir_taps, plan):
    chan_count = lax.axis_size("chan")
    parts = lax.axis_size("tm")
    tail = samples[:, samples.shape[1] - LANE :]
    before = lax.ppermute(tail, "tm", [(i, i + 1) for i in range(parts - 1)])
    own = jnp.concatenate([before, samples], axis=1)

    fixed_masks = (1, chan_count - 1)
    free_masks = range(2, chan_count - 1)
    masks = [plan[r] for r in range(ROUNDS)]
    seen = jnp.int32(0)
    slots = [jnp.int32(0)] * ROUNDS
    free = [jnp.int32(0)] * 2
    for r, mask in enumerate(masks):
        is_first, is_last = mask == fixed_masks[0], mask == fixed_masks[1]
        is_free = ~(is_first | is_last)
        takes = [is_first, is_last, is_free & (seen == 0), is_free & (seen == 1)]
        slots = [jnp.where(take, r + 1, slot) for take, slot in zip(takes, slots)]
        free = [jnp.where(take, mask, old) for take, old in zip(takes[2:], free)]
        seen = seen + is_free.astype(jnp.int32)

    partners = [from_partner(own, "chan", mask) for mask in fixed_masks]
    routes = [functools.partial(from_partner, axis="chan", mask=mask) for mask in free_masks]
    for mask in free:
        partners.append(lax.switch(mask - free_masks[0], routes, own))

    info = jnp.stack([lax.axis_index("tm").astype(jnp.int32), *slots])
    mine, others = correlate(info, own, partners, fir_taps, parts)
    total = mine
    for j in range(1, parts):
        route = [(i, (i + j) % parts) for i in range(parts)]
        total = total + lax.ppermute(others[j - 1], "tm", route).astype(jnp.float32)
    return total[0], total[1:]


def solution(mesh):
    in_specs = (P("chan", "tm"), P(), P())
    out_specs = (P(("chan", "tm"), None, None), P(None, ("chan", "tm"), None, None))
    return jax.shard_map(
        on_device, mesh=mesh, in_specs=in_specs, out_specs=out_specs, check_vma=False
    )
```

```python
import functools
import math

import jax
import jax.numpy as jnp
import ml_dtypes
import numpy as np
from jax import lax
from jax.experimental import pallas as pl
from jax.experimental.pallas import tpu as pltpu
from jax.sharding import PartitionSpec as P

SEGS_DEV = 2
LAGS = 129
ROUNDS = 4
LANE = 128
MAX_BRANCHES = 128


def split_table(table):
    high = table.astype(ml_dtypes.bfloat16)
    low = (table - high.astype(np.float64)).astype(ml_dtypes.bfloat16)
    return high, low


def tables(length):
    half = length // 2
    quarter = length // 4
    sample = np.arange(half)[:, None]

    def columns(freqs):
        angle = 2.0 * math.pi / length * (sample * freqs[None, :] % length)
        return np.cos(angle), -np.sin(angle)

    even = 2 * np.arange(quarter)
    odd = even + 1
    even_re, even_im = columns(even)
    even_im[:, 0] = 1.0 - 2.0 * (np.arange(half) % 2)
    odd_re, odd_im = columns(odd)
    even_table = np.concatenate([even_re, even_im], axis=1)
    odd_table = np.concatenate([odd_re, odd_im], axis=1)

    freqs = np.concatenate([even, odd])[:, None]
    lag = (np.arange(LAGS) - LAGS // 2)[None, :]
    angle = 2.0 * math.pi / length * (lag * freqs % length)
    weight = np.where(freqs == 0, 1.0, 2.0) / length
    lag_cos = weight * np.cos(angle)
    lag_sin = weight * np.sin(angle)
    lag_sin[0] = (1.0 - 2.0 * (np.abs(lag[0]) % 2)) / length
    lag_table = np.zeros((length, 2 * LANE))
    lag_table[:, :LAGS] = np.concatenate([lag_cos, lag_sin], axis=0)
    return (
        *split_table(even_table),
        *split_table(odd_table),
        lag_table.astype(ml_dtypes.bfloat16),
    )


def dot(left, right):
    return jnp.dot(left, right, preferred_element_type=jnp.float32)


def correlate_kernel(parts, last_mask, plan, taps, *refs):
    sets = ROUNDS + 1
    pieces, refs = refs[: sets * parts], refs[sets * parts :]
    tables_hbm, refs = refs[:5], refs[5:]
    self_out, pair_out = refs[:2]
    piece_vmem, tables_vmem, refs = refs[2], refs[3:8], refs[8:]
    base_ref, sums, diffs, real_ref, imag_ref, left_ref, cross, result, piece_sems, table_sems = refs

    chans, width = pieces[0].shape
    half = tables_hbm[0].shape[0]
    quarter = half // 2
    tiles = half // LANE
    rows_piece = SEGS_DEV * chans
    rows_blk = parts * rows_piece
    rows = sets * rows_blk
    share = chans // parts
    place = lax.axis_index("tm")

    piece_copies = [
        pltpu.make_async_copy(piece, piece_vmem.at[i], piece_sems.at[i])
        for i, piece in enumerate(pieces)
    ]
    table_copies = [
        pltpu.make_async_copy(table, table_vmem, table_sems.at[i])
        for i, (table, table_vmem) in enumerate(zip(tables_hbm, tables_vmem))
    ]
    for copy in piece_copies + table_copies:
        copy.start()
    even_hi, even_lo, odd_hi, odd_lo, lag_table = tables_vmem

    base_ref[...] = jnp.zeros_like(base_ref)
    base_ref[0:1, : taps.shape[1]] = taps[...]
    base = jnp.broadcast_to(base_ref[0:1], (2 * LANE, 2 * LANE))
    toeplitz = pltpu.roll(base, LANE, 1, stride=1, stride_axis=0)[:, :LANE]
    toep_hi = toeplitz.astype(jnp.bfloat16)
    toep_lo = (toeplitz - toep_hi.astype(jnp.float32)).astype(jnp.bfloat16)
    toep = jnp.concatenate([toep_hi, toep_lo], axis=1)

    for q in range(sets):
        for j in range(parts):
            piece_copies[q * parts + j].wait()
        for j in range(parts):
            piece = piece_vmem[q * parts + j]
            tail = piece_vmem[q * parts + (j + 1) % parts, :, width - LANE :]
            is_first = lax.rem(place + parts - j, parts) == 0
            tail = (tail.astype(jnp.float32) * jnp.where(is_first, 0.0, 1.0)).astype(jnp.bfloat16)
            windows = [jnp.concatenate([tail, piece[:, :LANE]], axis=1)]
            windows += [piece[:, LANE * (k - 1) : LANE * (k + 1)] for k in range(1, width // LANE)]
            both = dot(jnp.concatenate(windows, axis=0), toep)
            filtered = both[:, :LANE] + both[:, LANE:]
            for s in range(SEGS_DEV):
                row = q * rows_blk + j * rows_piece + s * chans
                for k in range(tiles):
                    lo = (s * 2 * tiles + k) * chans
                    hi = lo + tiles * chans
                    first, second = filtered[lo : lo + chans], filtered[hi : hi + chans]
                    for ref, value in ((sums, first + second), (diffs, first - second)):
                        high = value.astype(jnp.bfloat16)
                        low = (value - high.astype(jnp.float32)).astype(jnp.bfloat16)
                        ref[row : row + chans, LANE * k : LANE * (k + 1)] = high
                        ref[rows + row : rows + row + chans, LANE * k : LANE * (k + 1)] = low

    for copy in table_copies:
        copy.wait()

    def transform(values, table_hi, table_lo):
        main = dot(values[...], table_hi[...])
        return main[:rows] + main[rows:] + dot(values[:rows, :], table_lo[...])

    even = transform(sums, even_hi, even_lo)
    odd = transform(diffs, odd_hi, odd_lo)
    real = jnp.concatenate([even[:, :quarter], odd[:, :quarter]], axis=1)
    imag = jnp.concatenate([even[:, quarter:], odd[:, quarter:]], axis=1)
    edge = lax.broadcasted_iota(jnp.int32, real.shape, 1) == 0
    real_sq = real * real
    imag_sq = imag * imag
    level = 0.1 / (half + 1) * jnp.sum(real_sq + imag_sq, axis=1, keepdims=True) + 1e-06
    inv_real = lax.rsqrt(real_sq + jnp.where(edge, 0.0, imag_sq) + level)
    inv_imag = jnp.where(edge, lax.rsqrt(imag_sq + level), inv_real)
    real_ref[...] = (real * inv_real).astype(jnp.bfloat16).astype(jnp.float32)
    imag_ref[...] = (imag * inv_imag).astype(jnp.bfloat16).astype(jnp.float32)

    def picked(ref, s):
        value = ref[s * chans : s * chans + share, :]
        for owner in range(1, parts):
            at = s * chans + owner * share
            value = jnp.where(place == owner, ref[at : at + share, :], value)
        return value

    segs = parts * SEGS_DEV
    edge_row = lax.broadcasted_iota(jnp.int32, (share, half), 1) == 0
    for s in range(segs):
        real_s, imag_s = picked(real_ref, s), picked(imag_ref, s)
        lefts = (real_s, jnp.where(edge_row, 0.0, imag_s), jnp.where(edge_row, imag_s, real_s))
        for j, value in enumerate(lefts):
            for a in range(share):
                left_ref[a, segs * j + s : segs * j + s + 1, :] = value[a : a + 1]

    out_rows = chans * sets

    @pl.loop(0, share)
    def _(a):
        at = pl.multiple_of(a * out_rows, out_rows)
        for c in range(tiles):
            cols = slice(LANE * c, LANE * (c + 1))
            left = [
                jnp.broadcast_to(left_ref[a, j : j + 1, cols], (chans, LANE))
                for j in range(3 * segs)
            ]
            for q in range(sets):
                cos_part = sin_part = 0.0
                for s in range(segs):
                    row_b = slice(q * rows_blk + s * chans, q * rows_blk + (s + 1) * chans)
                    re_b, im_b = real_ref[row_b, cols], imag_ref[row_b, cols]
                    re_a, im_a, x_a = (left[segs * j + s] for j in range(3))
                    cos_part += re_a * re_b + im_a * im_b
                    sin_part += x_a * im_b - im_a * re_b
                at_q = pl.ds(at + q * chans, chans)
                cross[at_q, cols] = cos_part.astype(jnp.bfloat16)
                cross[at_q, half + LANE * c : half + LANE * (c + 1)] = sin_part.astype(jnp.bfloat16)

    result[...] = dot(cross[...], lag_table[...])

    masks = [plan[r] for r in range(ROUNDS)]
    free = [(mask != 1) & (mask != last_mask) for mask in masks]
    least = functools.reduce(
        jnp.minimum, [jnp.where(ok, mask, last_mask) for ok, mask in zip(free, masks)]
    )

    def slot_of(hits):
        return sum(jnp.where(hit, r, 0) for r, hit in enumerate(hits))

    slots = [
        slot_of([mask == 1 for mask in masks]),
        slot_of([mask == last_mask for mask in masks]),
        slot_of([mask == least for mask in masks]),
        slot_of([ok & (mask != least) for ok, mask in zip(free, masks)]),
    ]
    for a in range(share):
        for q in range(sets):
            at = (a * sets + q) * chans
            value = result[at : at + chans, :LAGS]
            if q == 0:
                self_out[a] = value
            else:
                pair_out[slots[q - 1], a] = value


def correlate(plan, fir_taps, pieces, parts, last_mask):
    chans, width = pieces[0].shape
    length = width // SEGS_DEV
    half = length // 2
    sets = ROUNDS + 1
    rows = sets * parts * SEGS_DEV * chans
    share = chans // parts
    table_list = tables(length)
    vmem = pl.BlockSpec(memory_space=pltpu.VMEM)
    smem = pl.BlockSpec(memory_space=pltpu.SMEM)
    hbm = pl.BlockSpec(memory_space=pl.ANY)
    return pl.pallas_call(
        functools.partial(correlate_kernel, parts, last_mask),
        out_shape=(
            jax.ShapeDtypeStruct((share, chans, LAGS), jnp.float32),
            jax.ShapeDtypeStruct((ROUNDS, share, chans, LAGS), jnp.float32),
        ),
        in_specs=[smem, vmem] + [hbm] * (len(pieces) + len(table_list)),
        out_specs=(vmem, vmem),
        scratch_shapes=[
            pltpu.VMEM((len(pieces), chans, width), jnp.bfloat16),
            *[pltpu.VMEM(table.shape, jnp.bfloat16) for table in table_list],
            pltpu.VMEM((8, 2 * LANE), jnp.float32),
            pltpu.VMEM((2 * rows, half), jnp.bfloat16),
            pltpu.VMEM((2 * rows, half), jnp.bfloat16),
            pltpu.VMEM((rows, half), jnp.float32),
            pltpu.VMEM((rows, half), jnp.float32),
            pltpu.VMEM((share, 3 * parts * SEGS_DEV, half), jnp.float32),
            pltpu.VMEM((share * sets * chans, length), jnp.bfloat16),
            pltpu.VMEM((share * sets * chans, 2 * LANE), jnp.float32),
            pltpu.SemaphoreType.DMA((len(pieces),)),
            pltpu.SemaphoreType.DMA((len(table_list),)),
        ],
        compiler_params=pltpu.CompilerParams(vmem_limit_bytes=60 * 1024 * 1024),
    )(plan, fir_taps[None], *pieces, *table_list)


def from_block(samples, mask):
    chan_count, parts = lax.axis_size("chan"), lax.axis_size("tm")
    pieces = []
    for shift in range(parts):
        route = [
            (g * parts + t, (g ^ mask) * parts + (t + shift) % parts)
            for g in range(chan_count)
            for t in range(parts)
        ]
        same = mask == 0 and shift == 0
        pieces.append(samples if same else lax.ppermute(samples, ("chan", "tm"), route))
    return pieces


def from_free_blocks(samples, plan, free_masks, fixed_masks):
    first = free_masks[0]
    is_free = functools.reduce(jnp.logical_and, [plan != mask for mask in fixed_masks])
    pairs = [(low, high) for high in free_masks for low in free_masks if low < high]
    if len(pairs) <= MAX_BRANCHES:
        low, high = plan[:, None] - first, plan[None, :] - first
        is_pair = is_free[:, None] & is_free[None, :] & (low < high)
        branch = jnp.sum(jnp.where(is_pair, high * (high - 1) // 2 + low, 0))

        def route(low, high, x):
            return from_block(x, low) + from_block(x, high)

        return lax.switch(branch, [functools.partial(route, *pair) for pair in pairs], samples)
    routes = [functools.partial(from_block, mask=mask) for mask in free_masks]
    low = jnp.min(jnp.where(is_free, plan, free_masks[-1]))
    high = jnp.max(jnp.where(is_free, plan, first))
    return sum((lax.switch(mask - first, routes, samples) for mask in (low, high)), [])


def on_device(samples, fir_taps, plan):
    chan_count, parts = lax.axis_size("chan"), lax.axis_size("tm")
    fixed_masks = (1, chan_count - 1)
    free_masks = range(2, chan_count - 1)
    pieces = sum((from_block(samples, mask) for mask in (0, *fixed_masks)), [])
    pieces += from_free_blocks(samples, plan, free_masks, fixed_masks)
    return correlate(plan, fir_taps, pieces, parts, chan_count - 1)


def solution(mesh):
    in_specs = (P("chan", "tm"), P(), P())
    out_specs = (P(("chan", "tm"), None, None), P(None, ("chan", "tm"), None, None))
    return jax.shard_map(
        on_device, mesh=mesh, in_specs=in_specs, out_specs=out_specs, check_vma=False
    )
```

```python
import functools
import math

import jax
import jax.numpy as jnp
import ml_dtypes
import numpy as np
from jax import lax
from jax.experimental import pallas as pl
from jax.experimental.pallas import tpu as pltpu
from jax.sharding import PartitionSpec as P

SEGS_DEV = 2
LAGS = 129
ROUNDS = 4
LANE = 128
MAX_BRANCHES = 128
TAIL_ROWS = 16


def split_table(table):
    high = table.astype(ml_dtypes.bfloat16)
    low = (table - high.astype(np.float64)).astype(ml_dtypes.bfloat16)
    return high, low


def tables(length):
    half = length // 2
    quarter = length // 4
    sample = np.arange(half)[:, None]

    def columns(freqs):
        angle = 2.0 * math.pi / length * (sample * freqs[None, :] % length)
        return np.cos(angle), -np.sin(angle)

    even = 2 * np.arange(quarter)
    odd = even + 1
    even_re, even_im = columns(even)
    even_im[:, 0] = 1.0 - 2.0 * (np.arange(half) % 2)
    odd_re, odd_im = columns(odd)
    even_table = np.concatenate([even_re, even_im], axis=1)
    odd_table = np.concatenate([odd_re, odd_im], axis=1)

    freqs = np.concatenate([even, odd])[:, None]
    lag = (np.arange(LAGS) - LAGS // 2)[None, :]
    angle = 2.0 * math.pi / length * (lag * freqs % length)
    weight = np.where(freqs == 0, 1.0, 2.0) / length
    lag_cos = weight * np.cos(angle)
    lag_sin = weight * np.sin(angle)
    lag_sin[0] = (1.0 - 2.0 * (np.abs(lag[0]) % 2)) / length
    lag_table = np.zeros((length, 2 * LANE))
    lag_table[:, :LAGS] = np.concatenate([lag_cos, lag_sin], axis=0)
    return (
        *split_table(even_table),
        *split_table(odd_table),
        lag_table.astype(ml_dtypes.bfloat16),
    )


def dot(left, right):
    return jnp.dot(left, right, preferred_element_type=jnp.float32)


def correlate_kernel(parts, taps, *refs):
    sets = ROUNDS + 1
    blocks_hbm, tables_hbm, refs = refs[:sets], refs[sets : sets + 5], refs[sets + 5 :]
    mine, others, blocks, refs = refs[0], refs[1], refs[2], refs[3:]
    tables_vmem, refs = refs[:5], refs[5:]
    base_ref, sums, diffs, real_ref, imag_ref, left_ref, cross, block_sems, table_sems = refs

    chans = blocks.shape[1]
    half = tables_hbm[0].shape[0]
    quarter = half // 2
    tiles = half // LANE
    rows_blk = SEGS_DEV * chans
    rows = sets * rows_blk
    share = chans // parts
    place = lax.axis_index("tm")

    block_copies = [
        pltpu.make_async_copy(block, blocks.at[q], block_sems.at[q])
        for q, block in enumerate(blocks_hbm)
    ]
    table_copies = [
        pltpu.make_async_copy(table, table_vmem, table_sems.at[i])
        for i, (table, table_vmem) in enumerate(zip(tables_hbm, tables_vmem))
    ]
    for copy in block_copies + table_copies:
        copy.start()
    even_hi, even_lo, odd_hi, odd_lo, lag_table = tables_vmem

    base_ref[...] = jnp.zeros_like(base_ref)
    base_ref[0:1, : taps.shape[1]] = taps[...]
    base = jnp.broadcast_to(base_ref[0:1], (2 * LANE, 2 * LANE))
    toeplitz = pltpu.roll(base, LANE, 1, stride=1, stride_axis=0)[:, :LANE]
    toep_hi = toeplitz.astype(jnp.bfloat16)
    toep_lo = (toeplitz - toep_hi.astype(jnp.float32)).astype(jnp.bfloat16)
    toep = jnp.concatenate([toep_hi, toep_lo], axis=1)

    for q in range(sets):
        block_copies[q].wait()
        windows = [
            blocks[q, :, LANE * k : LANE * (k + 2)] for k in range(2 * tiles * SEGS_DEV)
        ]
        both = dot(jnp.concatenate(windows, axis=0), toep)
        filtered = both[:, :LANE] + both[:, LANE:]
        for s in range(SEGS_DEV):
            row = q * rows_blk + s * chans
            for k in range(tiles):
                lo = (s * 2 * tiles + k) * chans
                hi = lo + tiles * chans
                first, second = filtered[lo : lo + chans], filtered[hi : hi + chans]
                for ref, value in ((sums, first + second), (diffs, first - second)):
                    high = value.astype(jnp.bfloat16)
                    low = (value - high.astype(jnp.float32)).astype(jnp.bfloat16)
                    ref[row : row + chans, LANE * k : LANE * (k + 1)] = high
                    ref[rows + row : rows + row + chans, LANE * k : LANE * (k + 1)] = low

    for copy in table_copies:
        copy.wait()

    def transform(values, table_hi, table_lo):
        main = dot(values[...], table_hi[...])
        return main[:rows] + main[rows:] + dot(values[:rows, :], table_lo[...])

    even = transform(sums, even_hi, even_lo)
    odd = transform(diffs, odd_hi, odd_lo)
    real = jnp.concatenate([even[:, :quarter], odd[:, :quarter]], axis=1)
    imag = jnp.concatenate([even[:, quarter:], odd[:, quarter:]], axis=1)
    edge = lax.broadcasted_iota(jnp.int32, real.shape, 1) == 0
    real_sq = real * real
    imag_sq = imag * imag
    level = 0.1 / (half + 1) * jnp.sum(real_sq + imag_sq, axis=1, keepdims=True) + 1e-06
    inv_real = lax.rsqrt(real_sq + jnp.where(edge, 0.0, imag_sq) + level)
    inv_imag = jnp.where(edge, lax.rsqrt(imag_sq + level), inv_real)
    real = (real * inv_real).astype(jnp.bfloat16).astype(jnp.float32)
    imag = (imag * inv_imag).astype(jnp.bfloat16).astype(jnp.float32)
    real_ref[...] = real
    imag_ref[...] = imag

    own = slice(0, rows_blk)
    lefts = (real[own], jnp.where(edge, 0.0, imag)[own], jnp.where(edge, imag, real)[own])
    for j, value in enumerate(lefts):
        for s in range(SEGS_DEV):
            at = SEGS_DEV * j + s
            for a in range(chans):
                row = s * chans + a
                left_ref[a, at : at + 1, :] = value[row : row + 1]

    set_rows = chans * sets

    @pl.loop(0, chans)
    def _(step):
        a = lax.rem(place * share + step, chans)
        at = pl.multiple_of(step * set_rows, set_rows)
        for c in range(tiles):
            cols = slice(LANE * c, LANE * (c + 1))
            left = [
                jnp.broadcast_to(left_ref[a, j : j + 1, cols], (chans, LANE))
                for j in range(3 * SEGS_DEV)
            ]
            for q in range(sets):
                cos_part = sin_part = 0.0
                for s in range(SEGS_DEV):
                    row_b = slice(q * rows_blk + s * chans, q * rows_blk + (s + 1) * chans)
                    re_b, im_b = real_ref[row_b, cols], imag_ref[row_b, cols]
                    re_a, im_a, x_a = (left[SEGS_DEV * j + s] for j in range(3))
                    cos_part += re_a * re_b + im_a * im_b
                    sin_part += x_a * im_b - im_a * re_b
                at_q = pl.ds(at + q * chans, chans)
                cross[at_q, cols] = cos_part.astype(jnp.bfloat16)
                cross[at_q, half + LANE * c : half + LANE * (c + 1)] = sin_part.astype(jnp.bfloat16)

    rows_part = share * set_rows
    chunk = share * chans
    mine[...] = dot(cross[:rows_part, :], lag_table[...])
    for j in range(1, parts):
        partial = dot(cross[rows_part * j : rows_part * (j + 1), :], lag_table[...])
        others[j - 1, :rows_part] = partial[:, :LANE].astype(jnp.bfloat16)
        on_diagonal = lax.broadcasted_iota(jnp.int32, (chunk, LANE), 0) == (
            lax.broadcasted_iota(jnp.int32, (chunk, LANE), 1)
        )
        last_rows = []
        for k in range(sets):
            column = partial[chunk * k : chunk * (k + 1), LANE : LANE + 1]
            spread = jnp.where(on_diagonal, column, 0.0)
            last_rows.append(jnp.sum(spread, axis=0, keepdims=True))
        last_rows.append(jnp.zeros((TAIL_ROWS - sets, LANE), jnp.float32))
        others[j - 1, rows_part:] = jnp.concatenate(last_rows, axis=0).astype(jnp.bfloat16)


def combine_kernel(parts, last_mask, plan, mine, *refs):
    received, (self_out, pair_out) = refs[: parts - 1], refs[parts - 1 :]
    sets = ROUNDS + 1
    share, chans, _ = self_out.shape
    chunk = share * chans
    rows_part = sets * chunk

    masks = [plan[r] for r in range(ROUNDS)]
    free = [(mask != 1) & (mask != last_mask) for mask in masks]
    least = functools.reduce(
        jnp.minimum, [jnp.where(ok, mask, last_mask) for ok, mask in zip(free, masks)]
    )

    def slot_of(hits):
        return sum(jnp.where(hit, r, 0) for r, hit in enumerate(hits))

    slots = [
        slot_of([mask == 1 for mask in masks]),
        slot_of([mask == last_mask for mask in masks]),
        slot_of([mask == least for mask in masks]),
        slot_of([ok & (mask != least) for ok, mask in zip(free, masks)]),
    ]
    on_diagonal = lax.broadcasted_iota(jnp.int32, (chunk, LANE), 0) == (
        lax.broadcasted_iota(jnp.int32, (chunk, LANE), 1)
    )
    for k in range(sets):
        rows = slice(chunk * k, chunk * (k + 1))
        main = mine[rows, :LANE]
        last = mine[rows, LANE : LANE + 1]
        for ref in received:
            main = main + ref[rows, :].astype(jnp.float32)
            row = ref[rows_part:, :].astype(jnp.float32)[k : k + 1]
            last = last + jnp.sum(jnp.where(on_diagonal, row, 0.0), axis=1, keepdims=True)
        for i in range(share):
            step, q = divmod(k * share + i, sets)
            at = slice(i * chans, (i + 1) * chans)
            out = self_out if q == 0 else pair_out.at[slots[q - 1]]
            out[step, :, :LANE] = main[at]
            out[step, :, LANE:] = last[at]


def correlate(fir_taps, blocks, parts):
    chans, width = blocks[0].shape
    length = (width - LANE) // SEGS_DEV
    half = length // 2
    sets = ROUNDS + 1
    rows = sets * SEGS_DEV * chans
    rows_part = chans // parts * sets * chans
    table_list = tables(length)
    vmem = pl.BlockSpec(memory_space=pltpu.VMEM)
    hbm = pl.BlockSpec(memory_space=pl.ANY)
    return pl.pallas_call(
        functools.partial(correlate_kernel, parts),
        out_shape=(
            jax.ShapeDtypeStruct((rows_part, 2 * LANE), jnp.float32),
            jax.ShapeDtypeStruct((parts - 1, rows_part + TAIL_ROWS, LANE), jnp.bfloat16),
        ),
        in_specs=[vmem] + [hbm] * (len(blocks) + len(table_list)),
        out_specs=(vmem, vmem),
        scratch_shapes=[
            pltpu.VMEM((sets, chans, width), jnp.bfloat16),
            *[pltpu.VMEM(table.shape, jnp.bfloat16) for table in table_list],
            pltpu.VMEM((8, 2 * LANE), jnp.float32),
            pltpu.VMEM((2 * rows, half), jnp.bfloat16),
            pltpu.VMEM((2 * rows, half), jnp.bfloat16),
            pltpu.VMEM((rows, half), jnp.float32),
            pltpu.VMEM((rows, half), jnp.float32),
            pltpu.VMEM((chans, 3 * SEGS_DEV, half), jnp.float32),
            pltpu.VMEM((sets * chans * chans, length), jnp.bfloat16),
            pltpu.SemaphoreType.DMA((sets,)),
            pltpu.SemaphoreType.DMA((len(table_list),)),
        ],
        compiler_params=pltpu.CompilerParams(vmem_limit_bytes=60 * 1024 * 1024),
    )(fir_taps[None], *blocks, *table_list)


def combine(plan, mine, received, chans, last_mask):
    parts = len(received) + 1
    share = chans // parts
    vmem = pl.BlockSpec(memory_space=pltpu.VMEM)
    smem = pl.BlockSpec(memory_space=pltpu.SMEM)
    return pl.pallas_call(
        functools.partial(combine_kernel, parts, last_mask),
        out_shape=(
            jax.ShapeDtypeStruct((share, chans, LAGS), jnp.float32),
            jax.ShapeDtypeStruct((ROUNDS, share, chans, LAGS), jnp.float32),
        ),
        in_specs=[smem] + [vmem] * parts,
        out_specs=(vmem, vmem),
        compiler_params=pltpu.CompilerParams(vmem_limit_bytes=32 * 1024 * 1024),
    )(plan, mine, *received)


def from_partner(block, mask):
    chan_count = lax.axis_size("chan")
    return lax.ppermute(block, "chan", [(g, g ^ mask) for g in range(chan_count)])


def from_partners(block, plan, free_masks, fixed_masks):
    first = free_masks[0]
    is_free = functools.reduce(jnp.logical_and, [plan != mask for mask in fixed_masks])

    def send(*masks):
        return lambda x: [from_partner(x, mask) for mask in masks]

    pairs = [(low, high) for high in free_masks for low in free_masks if low < high]
    if len(pairs) <= MAX_BRANCHES:
        low, high = plan[:, None] - first, plan[None, :] - first
        is_pair = is_free[:, None] & is_free[None, :] & (low < high)
        branch = jnp.sum(jnp.where(is_pair, high * (high - 1) // 2 + low, 0))
        return lax.switch(branch, [send(*fixed_masks, *pair) for pair in pairs], block)
    routes = [send(mask) for mask in free_masks]
    blocks = send(*fixed_masks)(block)
    low = jnp.min(jnp.where(is_free, plan, free_masks[-1]))
    high = jnp.max(jnp.where(is_free, plan, first))
    for mask in (low, high):
        blocks += lax.switch(mask - first, routes, block)
    return blocks


def on_device(samples, fir_taps, plan):
    chan_count, parts = lax.axis_size("chan"), lax.axis_size("tm")
    chans, width = samples.shape
    tail = samples[:, width - LANE :]
    before = lax.ppermute(tail, "tm", [(t, t + 1) for t in range(parts - 1)])
    own = lax.dynamic_update_slice(jnp.pad(samples, ((0, 0), (LANE, 0))), before, (0, 0))

    fixed_masks = (1, chan_count - 1)
    free_masks = range(2, chan_count - 1)
    blocks = [own, *from_partners(own, plan, free_masks, fixed_masks)]
    mine, others = correlate(fir_taps, blocks, parts)
    received = [
        lax.ppermute(others[j - 1], "tm", [(t, (t + j) % parts) for t in range(parts)])
        for j in range(1, parts)
    ]
    return combine(plan, mine, received, chans, chan_count - 1)


def solution(mesh):
    in_specs = (P("chan", "tm"), P(), P())
    out_specs = (P(("chan", "tm"), None, None), P(None, ("chan", "tm"), None, None))
    return jax.shard_map(
        on_device, mesh=mesh, in_specs=in_specs, out_specs=out_specs, check_vma=False
    )
```

```python
import functools
import math

import jax
import jax.numpy as jnp
import ml_dtypes
import numpy as np
from jax import lax
from jax.experimental import pallas as pl
from jax.experimental.pallas import tpu as pltpu
from jax.sharding import PartitionSpec as P

SEGS_DEV = 2
LAGS = 129
ROUNDS = 4
LANE = 128
MAX_BRANCHES = 128
TAIL_ROWS = 16
VMEM_LIMIT = 24 * 1024 * 1024


def split_table(table):
    high = table.astype(ml_dtypes.bfloat16)
    low = (table - high.astype(np.float64)).astype(ml_dtypes.bfloat16)
    return high, low


def tables(length):
    half = length // 2
    quarter = length // 4
    sample = np.arange(half)[:, None]

    def columns(freqs):
        angle = 2.0 * math.pi / length * (sample * freqs[None, :] % length)
        return np.cos(angle), -np.sin(angle)

    even = 2 * np.arange(quarter)
    odd = even + 1
    even_re, even_im = columns(even)
    even_im[:, 0] = 1.0 - 2.0 * (np.arange(half) % 2)
    odd_re, odd_im = columns(odd)
    even_table = np.concatenate([even_re, even_im], axis=1)
    odd_table = np.concatenate([odd_re, odd_im], axis=1)

    freqs = np.concatenate([even, odd])[:, None]
    lag = (np.arange(LAGS) - LAGS // 2)[None, :]
    angle = 2.0 * math.pi / length * (lag * freqs % length)
    weight = np.where(freqs == 0, 1.0, 2.0) / length
    lag_cos = weight * np.cos(angle)
    lag_sin = weight * np.sin(angle)
    lag_sin[0] = (1.0 - 2.0 * (np.abs(lag[0]) % 2)) / length
    lag_table = np.zeros((length, 2 * LANE))
    lag_table[:, :LAGS] = np.concatenate([lag_cos, lag_sin], axis=0)
    return (
        *split_table(even_table),
        *split_table(odd_table),
        lag_table.astype(ml_dtypes.bfloat16),
    )


def dot(left, right):
    return jnp.dot(left, right, preferred_element_type=jnp.float32)


def cross_products(count, first, last_step, left_ref, real_ref, imag_ref, cross):
    chans = left_ref.shape[0]
    half = real_ref.shape[1]
    rows_blk = SEGS_DEV * chans
    sets = real_ref.shape[0] // rows_blk
    set_rows = chans * sets

    @pl.loop(0, count)
    def _(step):
        a = lax.rem(first + step, last_step)
        at = pl.multiple_of(step * set_rows, set_rows)
        for c in range(half // LANE):
            cols = slice(LANE * c, LANE * (c + 1))
            left = [
                jnp.broadcast_to(left_ref[a, j : j + 1, cols], (chans, LANE))
                for j in range(3 * SEGS_DEV)
            ]
            for q in range(sets):
                cos_part = sin_part = 0.0
                for s in range(SEGS_DEV):
                    row_b = slice(q * rows_blk + s * chans, q * rows_blk + (s + 1) * chans)
                    re_b, im_b = real_ref[row_b, cols], imag_ref[row_b, cols]
                    re_a, im_a, x_a = (left[SEGS_DEV * j + s] for j in range(3))
                    cos_part += re_a * re_b + im_a * im_b
                    sin_part += x_a * im_b - im_a * re_b
                at_q = pl.ds(at + q * chans, chans)
                cross[at_q, cols] = cos_part.astype(jnp.bfloat16)
                cross[at_q, half + LANE * c : half + LANE * (c + 1)] = sin_part.astype(jnp.bfloat16)


def others_kernel(parts, taps, *refs):
    sets = ROUNDS + 1
    parts_hbm, tables_hbm, refs = refs[: sets + 1], refs[sets + 1 : sets + 6], refs[sets + 6 :]
    others, real_ref, imag_ref, left_ref, lag_table, blocks, refs = *refs[:6], refs[6:]
    tables_vmem, refs = (*refs[:4], lag_table), refs[4:]
    sums, diffs, cross, block_sems, table_sems = refs

    chans, width = blocks.shape[1:]
    half = tables_hbm[0].shape[0]
    quarter = half // 2
    tiles = half // LANE
    rows_blk = SEGS_DEV * chans
    rows = sets * rows_blk
    share = chans // parts
    place = lax.axis_index("tm")

    own, near, far, far_tail, low, high = parts_hbm
    places = [
        (own, blocks.at[0]),
        (near, blocks.at[1]),
        (far, blocks.at[2, :, pl.ds(LANE, width - LANE)]),
        (far_tail, blocks.at[2, :, pl.ds(0, LANE)]),
        (low, blocks.at[3]),
        (high, blocks.at[4]),
    ]
    block_copies = [
        pltpu.make_async_copy(source, target, block_sems.at[i])
        for i, (source, target) in enumerate(places)
    ]
    table_copies = [
        pltpu.make_async_copy(table, table_vmem, table_sems.at[i])
        for i, (table, table_vmem) in enumerate(zip(tables_hbm, tables_vmem))
    ]
    for copy in block_copies + table_copies:
        copy.start()
    even_hi, even_lo, odd_hi, odd_lo, _ = tables_vmem
    waits = [block_copies[0:1], block_copies[1:2], block_copies[2:4]]
    waits += [block_copies[4:5], block_copies[5:6]]

    base = jnp.broadcast_to(taps[...], (2 * LANE, 2 * LANE))
    toeplitz = pltpu.roll(base, LANE, 1, stride=1, stride_axis=0)[:, :LANE]
    toep_hi = toeplitz.astype(jnp.bfloat16)
    toep_lo = (toeplitz - toep_hi.astype(jnp.float32)).astype(jnp.bfloat16)
    toep = jnp.concatenate([toep_hi, toep_lo], axis=1)

    for q in range(sets):
        for copy in waits[q]:
            copy.wait()
        windows = [
            blocks[q, :, LANE * k : LANE * (k + 2)] for k in range(2 * tiles * SEGS_DEV)
        ]
        both = dot(jnp.concatenate(windows, axis=0), toep)
        filtered = both[:, :LANE] + both[:, LANE:]
        for s in range(SEGS_DEV):
            row = q * rows_blk + s * chans
            for k in range(tiles):
                lo = (s * 2 * tiles + k) * chans
                hi = lo + tiles * chans
                first, second = filtered[lo : lo + chans], filtered[hi : hi + chans]
                for ref, value in ((sums, first + second), (diffs, first - second)):
                    high = value.astype(jnp.bfloat16)
                    low = (value - high.astype(jnp.float32)).astype(jnp.bfloat16)
                    ref[row : row + chans, LANE * k : LANE * (k + 1)] = high
                    ref[rows + row : rows + row + chans, LANE * k : LANE * (k + 1)] = low

    for copy in table_copies:
        copy.wait()

    def transform(values, table_hi, table_lo):
        main = dot(values[...], table_hi[...])
        return main[:rows] + main[rows:] + dot(values[:rows, :], table_lo[...])

    even = transform(sums, even_hi, even_lo)
    odd = transform(diffs, odd_hi, odd_lo)
    real = jnp.concatenate([even[:, :quarter], odd[:, :quarter]], axis=1)
    imag = jnp.concatenate([even[:, quarter:], odd[:, quarter:]], axis=1)
    edge = lax.broadcasted_iota(jnp.int32, real.shape, 1) == 0
    real_sq = real * real
    imag_sq = imag * imag
    level = 0.1 / (half + 1) * jnp.sum(real_sq + imag_sq, axis=1, keepdims=True) + 1e-06
    inv_real = lax.rsqrt(real_sq + jnp.where(edge, 0.0, imag_sq) + level)
    inv_imag = jnp.where(edge, lax.rsqrt(imag_sq + level), inv_real)
    real = (real * inv_real).astype(jnp.bfloat16).astype(jnp.float32)
    imag = (imag * inv_imag).astype(jnp.bfloat16).astype(jnp.float32)
    real_ref[...] = real
    imag_ref[...] = imag

    own_rows = slice(0, rows_blk)
    lefts = (real, jnp.where(edge, 0.0, imag), jnp.where(edge, imag, real))
    for j, value in enumerate(lefts):
        value = value[own_rows]
        for s in range(SEGS_DEV):
            at = SEGS_DEV * j + s
            for a in range(chans):
                row = s * chans + a
                left_ref[a, at : at + 1, :] = value[row : row + 1]

    first_step = (place + 1) * share
    cross_products(chans - share, first_step, chans, left_ref, real_ref, imag_ref, cross)

    chunk = share * chans
    rows_part = sets * chunk
    on_diagonal = lax.broadcasted_iota(jnp.int32, (chunk, LANE), 0) == (
        lax.broadcasted_iota(jnp.int32, (chunk, LANE), 1)
    )
    for j in range(parts - 1):
        partial = dot(cross[rows_part * j : rows_part * (j + 1), :], lag_table[...])
        others[j, :rows_part] = partial[:, :LANE].astype(jnp.bfloat16)
        last_rows = []
        for k in range(sets):
            column = partial[chunk * k : chunk * (k + 1), LANE : LANE + 1]
            spread = jnp.where(on_diagonal, column, 0.0)
            last_rows.append(jnp.sum(spread, axis=0, keepdims=True))
        last_rows.append(jnp.zeros((TAIL_ROWS - sets, LANE), jnp.float32))
        others[j, rows_part:] = jnp.concatenate(last_rows, axis=0).astype(jnp.bfloat16)


def mine_kernel(parts, real_ref, imag_ref, left_ref, lag_table, mine, cross):
    chans = left_ref.shape[0]
    share = chans // parts
    first_step = lax.axis_index("tm") * share
    cross_products(share, first_step, chans, left_ref, real_ref, imag_ref, cross)
    mine[...] = dot(cross[...], lag_table[...])


def combine_kernel(parts, last_mask, plan, mine, *refs):
    received, (self_out, pair_out) = refs[: parts - 1], refs[parts - 1 :]
    sets = ROUNDS + 1
    share, chans, _ = self_out.shape
    chunk = share * chans
    rows_part = sets * chunk

    masks = [plan[r] for r in range(ROUNDS)]
    free = [(mask != 1) & (mask != last_mask) for mask in masks]
    least = functools.reduce(
        jnp.minimum, [jnp.where(ok, mask, last_mask) for ok, mask in zip(free, masks)]
    )

    def slot_of(hits):
        return sum(jnp.where(hit, r, 0) for r, hit in enumerate(hits))

    slots = [
        slot_of([mask == 1 for mask in masks]),
        slot_of([mask == last_mask for mask in masks]),
        slot_of([mask == least for mask in masks]),
        slot_of([ok & (mask != least) for ok, mask in zip(free, masks)]),
    ]
    on_diagonal = lax.broadcasted_iota(jnp.int32, (chunk, LANE), 0) == (
        lax.broadcasted_iota(jnp.int32, (chunk, LANE), 1)
    )
    for k in range(sets):
        rows = slice(chunk * k, chunk * (k + 1))
        main = mine[rows, :LANE]
        last = mine[rows, LANE : LANE + 1]
        for ref in received:
            main = main + ref[rows, :].astype(jnp.float32)
            row = ref[rows_part:, :].astype(jnp.float32)[k : k + 1]
            last = last + jnp.sum(jnp.where(on_diagonal, row, 0.0), axis=1, keepdims=True)
        for i in range(share):
            step, q = divmod(k * share + i, sets)
            at = slice(i * chans, (i + 1) * chans)
            out = self_out if q == 0 else pair_out.at[slots[q - 1]]
            out[step, :, :LANE] = main[at]
            out[step, :, LANE:] = last[at]


def correlate(taps, blocks, parts):
    chans, width = blocks[0].shape
    length = (width - LANE) // SEGS_DEV
    half = length // 2
    sets = ROUNDS + 1
    rows = sets * SEGS_DEV * chans
    rows_part = chans // parts * sets * chans
    *dft_tables, lag_table = tables(length)
    table_list = [
        pltpu.with_memory_space_constraint(jnp.asarray(table), pltpu.HBM)
        for table in (*dft_tables, lag_table)
    ]
    vmem = pl.BlockSpec(memory_space=pltpu.VMEM)
    hbm = pl.BlockSpec(memory_space=pl.ANY)
    others, *spectra = pl.pallas_call(
        functools.partial(others_kernel, parts),
        out_shape=(
            pltpu.VMEM((parts - 1, rows_part + TAIL_ROWS, LANE), jnp.bfloat16),
            pltpu.VMEM((rows, half), jnp.float32),
            pltpu.VMEM((rows, half), jnp.float32),
            pltpu.VMEM((chans, 3 * SEGS_DEV, half), jnp.float32),
            pltpu.VMEM(lag_table.shape, jnp.bfloat16),
        ),
        in_specs=[vmem] + [hbm] * (len(blocks) + len(table_list)),
        out_specs=(vmem,) * 5,
        scratch_shapes=[
            pltpu.VMEM((sets, chans, width), jnp.bfloat16),
            *[pltpu.VMEM(table.shape, jnp.bfloat16) for table in dft_tables],
            pltpu.VMEM((2 * rows, half), jnp.bfloat16),
            pltpu.VMEM((2 * rows, half), jnp.bfloat16),
            pltpu.VMEM(((parts - 1) * rows_part, length), jnp.bfloat16),
            pltpu.SemaphoreType.DMA((len(blocks),)),
            pltpu.SemaphoreType.DMA((len(table_list),)),
        ],
        compiler_params=pltpu.CompilerParams(vmem_limit_bytes=VMEM_LIMIT),
    )(taps, *blocks, *table_list)
    mine = pl.pallas_call(
        functools.partial(mine_kernel, parts),
        out_shape=pltpu.VMEM((rows_part, 2 * LANE), jnp.float32),
        in_specs=[vmem] * 4,
        out_specs=vmem,
        scratch_shapes=[pltpu.VMEM((rows_part, length), jnp.bfloat16)],
        compiler_params=pltpu.CompilerParams(vmem_limit_bytes=VMEM_LIMIT),
        cost_estimate=pl.CostEstimate(
            flops=2 * rows_part * length * 2 * LANE, bytes_accessed=0, transcendentals=0
        ),
    )(*spectra)
    return mine, others


def combine(plan, mine, received, chans, last_mask):
    parts = len(received) + 1
    share = chans // parts
    vmem = pl.BlockSpec(memory_space=pltpu.VMEM)
    smem = pl.BlockSpec(memory_space=pltpu.SMEM)
    return pl.pallas_call(
        functools.partial(combine_kernel, parts, last_mask),
        out_shape=(
            jax.ShapeDtypeStruct((share, chans, LAGS), jnp.float32),
            jax.ShapeDtypeStruct((ROUNDS, share, chans, LAGS), jnp.float32),
        ),
        in_specs=[smem] + [vmem] * parts,
        out_specs=(vmem, vmem),
        compiler_params=pltpu.CompilerParams(vmem_limit_bytes=VMEM_LIMIT),
    )(plan, mine, *received)


def from_partner(block, mask):
    chan_count = lax.axis_size("chan")
    return lax.ppermute(block, "chan", [(g, g ^ mask) for g in range(chan_count)])


def from_free_partners(plan, free_masks, fixed_masks, send):
    first = free_masks[0]
    is_free = functools.reduce(jnp.logical_and, [plan != mask for mask in fixed_masks])
    pairs = [(low, high) for high in free_masks for low in free_masks if low < high]
    if len(pairs) <= MAX_BRANCHES:
        low, high = plan[:, None] - first, plan[None, :] - first
        is_pair = is_free[:, None] & is_free[None, :] & (low < high)
        branch = jnp.sum(jnp.where(is_pair, high * (high - 1) // 2 + low, 0))
        return lax.switch(branch, [functools.partial(send, pair) for pair in pairs])
    low = jnp.min(jnp.where(is_free, plan, free_masks[-1]))
    high = jnp.max(jnp.where(is_free, plan, first))
    routes = [functools.partial(send, (mask,)) for mask in free_masks]
    *fixed, low_block = lax.switch(low - first, routes)
    return *fixed, low_block, lax.switch(high - first, routes)[-1]


def on_device(samples, fir_taps, plan):
    chan_count, parts = lax.axis_size("chan"), lax.axis_size("tm")
    chans, width = samples.shape
    near_mask, far_mask = fixed_masks = (1, chan_count - 1)
    free_masks = range(2, chan_count - 1)

    far = from_partner(samples, far_mask)
    tail = samples[:, width - LANE :]
    before = lax.ppermute(tail, "tm", [(t, t + 1) for t in range(parts - 1)])
    padded, taps = lax.optimization_barrier(
        (
            jnp.pad(samples, ((0, 0), (LANE, 0))),
            jnp.pad(fir_taps, (0, 2 * LANE - fir_taps.shape[0])),
        )
    )
    own = lax.dynamic_update_slice(padded, before, (0, 0))

    def send(masks):
        blocks = [from_partner(own, mask) for mask in masks]
        return from_partner(own, near_mask), from_partner(before, far_mask), *blocks

    near, far_tail, low, high = from_free_partners(plan, free_masks, fixed_masks, send)
    blocks = [own, near, far, far_tail, low, high]
    mine, others = correlate(taps[None], blocks, parts)
    received = [
        lax.ppermute(others[j - 1], "tm", [(t, (t + j) % parts) for t in range(parts)])
        for j in range(1, parts)
    ]
    return combine(plan, mine, received, chans, chan_count - 1)


def solution(mesh):
    in_specs = (P("chan", "tm"), P(), P())
    out_specs = (P(("chan", "tm"), None, None), P(None, ("chan", "tm"), None, None))
    return jax.shard_map(
        on_device, mesh=mesh, in_specs=in_specs, out_specs=out_specs, check_vma=False
    )
```

```python
import functools
import math

import jax
import jax.numpy as jnp
import ml_dtypes
import numpy as np
from jax import lax
from jax.experimental import pallas as pl
from jax.experimental.pallas import tpu as pltpu
from jax.sharding import PartitionSpec as P

SEGS_DEV = 2
LAGS = 129
ROUNDS = 4
LANE = 128
MAX_BRANCHES = 128
TAIL_ROWS = 16
VMEM_LIMIT = 24 * 1024 * 1024


def split_table(table):
    high = table.astype(ml_dtypes.bfloat16)
    low = (table - high.astype(np.float64)).astype(ml_dtypes.bfloat16)
    return high, low


def tables(length):
    half = length // 2
    quarter = length // 4
    sample = np.arange(half)[:, None]

    def columns(freqs):
        angle = 2.0 * math.pi / length * (sample * freqs[None, :] % length)
        return np.cos(angle), -np.sin(angle)

    even = 2 * np.arange(quarter)
    odd = even + 1
    even_re, even_im = columns(even)
    even_im[:, 0] = 1.0 - 2.0 * (np.arange(half) % 2)
    odd_re, odd_im = columns(odd)
    even_table = np.concatenate([even_re, even_im], axis=1)
    odd_table = np.concatenate([odd_re, odd_im], axis=1)

    freqs = np.concatenate([even, odd])[:, None]
    lag = (np.arange(LAGS) - LAGS // 2)[None, :]
    angle = 2.0 * math.pi / length * (lag * freqs % length)
    weight = np.where(freqs == 0, 1.0, 2.0) / length
    lag_cos = weight * np.cos(angle)
    lag_sin = weight * np.sin(angle)
    lag_sin[0] = (1.0 - 2.0 * (np.abs(lag[0]) % 2)) / length
    lag_table = np.zeros((length, 2 * LANE))
    lag_table[:, :LAGS] = np.concatenate([lag_cos, lag_sin], axis=0)
    return (
        *split_table(even_table),
        *split_table(odd_table),
        lag_table.astype(ml_dtypes.bfloat16),
    )


def dot(left, right):
    return jnp.dot(left, right, preferred_element_type=jnp.float32)


def prepare_kernel(masks, plan, taps, samples, *refs):
    tables_hbm, refs = refs[:5], refs[5:]
    branch, own, toep = refs[:3]
    tables_vmem, (own_sem, table_sems) = refs[3:8], refs[8:]
    chans, width = samples.shape
    copies = [pltpu.make_async_copy(samples, own.at[:, pl.ds(LANE, width)], own_sem)]
    copies += [
        pltpu.make_async_copy(table, table_vmem, table_sems.at[i])
        for i, (table, table_vmem) in enumerate(zip(tables_hbm, tables_vmem))
    ]
    for copy in copies:
        copy.start()
    own[:, :LANE] = jnp.zeros((chans, LANE), jnp.bfloat16)

    first, last = masks
    low, high = free_masks_of(plan, last)
    branch[0] = pair_branch(low - first, high - first)

    lane = lax.broadcasted_iota(jnp.int32, (1, 2 * LANE), 1)
    base = jnp.zeros((1, 2 * LANE), jnp.float32)
    for j in range(taps.shape[0]):
        base = jnp.where(lane == j, taps[j], base)
    base = jnp.broadcast_to(base, (2 * LANE, 2 * LANE))
    toeplitz = pltpu.roll(base, LANE, 1, stride=1, stride_axis=0)[:, :LANE]
    toep_hi = toeplitz.astype(jnp.bfloat16)
    toep_lo = (toeplitz - toep_hi.astype(jnp.float32)).astype(jnp.bfloat16)
    toep[:, :LANE] = toep_hi
    toep[:, LANE:] = toep_lo
    for copy in copies:
        copy.wait()


def free_masks_of(plan, last_mask):
    masks = [plan[r] for r in range(ROUNDS)]
    free = [(mask != 1) & (mask != last_mask) for mask in masks]
    low = functools.reduce(
        jnp.minimum, [jnp.where(ok, mask, last_mask) for ok, mask in zip(free, masks)]
    )
    high = functools.reduce(jnp.maximum, [jnp.where(ok, mask, 0) for ok, mask in zip(free, masks)])
    return low, high


def pair_branch(low, high):
    return high * (high - 1) // 2 + low


def prepare(plan, fir_taps, samples, masks):
    chans, width = samples.shape
    table_list = [
        pltpu.with_memory_space_constraint(jnp.asarray(table), pltpu.HBM)
        for table in tables(width // SEGS_DEV)
    ]
    plan, fir_taps, samples = (
        pltpu.with_memory_space_constraint(array, pltpu.HBM) for array in (plan, fir_taps, samples)
    )
    smem = pl.BlockSpec(memory_space=pltpu.SMEM)
    vmem = pl.BlockSpec(memory_space=pltpu.VMEM)
    hbm = pl.BlockSpec(memory_space=pl.ANY)
    branch, own, toep, *table_list = pl.pallas_call(
        functools.partial(prepare_kernel, masks),
        out_shape=(
            jax.ShapeDtypeStruct((1,), jnp.int32),
            pltpu.VMEM((chans, width + LANE), jnp.bfloat16),
            pltpu.VMEM((2 * LANE, 2 * LANE), jnp.bfloat16),
            *[pltpu.VMEM(table.shape, jnp.bfloat16) for table in table_list],
        ),
        in_specs=[smem, smem] + [hbm] * (1 + len(table_list)),
        out_specs=(smem,) + (vmem,) * (2 + len(table_list)),
        scratch_shapes=[
            pltpu.SemaphoreType.DMA,
            pltpu.SemaphoreType.DMA((len(table_list),)),
        ],
        compiler_params=pltpu.CompilerParams(vmem_limit_bytes=VMEM_LIMIT),
    )(plan, fir_taps, samples, *table_list)
    return branch, own, (toep, *table_list)


def cross_products(count, first, last_step, left_ref, real_ref, imag_ref, cross):
    chans = left_ref.shape[0]
    half = real_ref.shape[1]
    rows_blk = SEGS_DEV * chans
    sets = real_ref.shape[0] // rows_blk
    set_rows = chans * sets

    @pl.loop(0, count)
    def _(step):
        a = lax.rem(first + step, last_step)
        at = pl.multiple_of(step * set_rows, set_rows)
        for c in range(half // LANE):
            cols = slice(LANE * c, LANE * (c + 1))
            left = [
                jnp.broadcast_to(left_ref[a, j : j + 1, cols], (chans, LANE))
                for j in range(3 * SEGS_DEV)
            ]
            for q in range(sets):
                cos_part = sin_part = 0.0
                for s in range(SEGS_DEV):
                    row_b = slice(q * rows_blk + s * chans, q * rows_blk + (s + 1) * chans)
                    re_b, im_b = real_ref[row_b, cols], imag_ref[row_b, cols]
                    re_a, im_a, x_a = (left[SEGS_DEV * j + s] for j in range(3))
                    cos_part += re_a * re_b + im_a * im_b
                    sin_part += x_a * im_b - im_a * re_b
                at_q = pl.ds(at + q * chans, chans)
                cross[at_q, cols] = cos_part.astype(jnp.bfloat16)
                cross[at_q, half + LANE * c : half + LANE * (c + 1)] = sin_part.astype(jnp.bfloat16)


def others_kernel(parts, toep, even_hi, even_lo, odd_hi, odd_lo, lag_table, *refs):
    own, far, far_tail, *arriving = refs[:6]
    others, real_ref, imag_ref, left_ref = refs[6:10]
    arrived, sums, diffs, cross, sems = refs[10:]

    sets = ROUNDS + 1
    chans, width = far.shape
    half = even_hi.shape[0]
    quarter = half // 2
    tiles = half // LANE
    rows_blk = SEGS_DEV * chans
    rows = sets * rows_blk
    share = chans // parts
    place = lax.axis_index("tm")

    copies = [
        pltpu.make_async_copy(source, arrived.at[i], sems.at[i])
        for i, source in enumerate(arriving)
    ]
    for copy in copies:
        copy.start()

    def windows_of(q):
        if q == 2:
            inner = [far[:, LANE * k : LANE * (k + 2)] for k in range(width // LANE - 1)]
            return [jnp.concatenate([far_tail[...], far[:, :LANE]], axis=1), *inner]
        if q == 0:
            return [own[:, LANE * k : LANE * (k + 2)] for k in range(width // LANE)]
        at = (1, 3, 4).index(q)
        copies[at].wait()
        return [arrived[at, :, LANE * k : LANE * (k + 2)] for k in range(width // LANE)]

    for q in (0, 2, 1, 3, 4):
        both = dot(jnp.concatenate(windows_of(q), axis=0), toep[...])
        filtered = both[:, :LANE] + both[:, LANE:]
        for s in range(SEGS_DEV):
            row = q * rows_blk + s * chans
            for k in range(tiles):
                lo = (s * 2 * tiles + k) * chans
                hi = lo + tiles * chans
                first, second = filtered[lo : lo + chans], filtered[hi : hi + chans]
                for ref, value in ((sums, first + second), (diffs, first - second)):
                    high = value.astype(jnp.bfloat16)
                    low = (value - high.astype(jnp.float32)).astype(jnp.bfloat16)
                    ref[row : row + chans, LANE * k : LANE * (k + 1)] = high
                    ref[rows + row : rows + row + chans, LANE * k : LANE * (k + 1)] = low

    def transform(values, table_hi, table_lo):
        main = dot(values[...], table_hi[...])
        return main[:rows] + main[rows:] + dot(values[:rows, :], table_lo[...])

    even = transform(sums, even_hi, even_lo)
    odd = transform(diffs, odd_hi, odd_lo)
    real = jnp.concatenate([even[:, :quarter], odd[:, :quarter]], axis=1)
    imag = jnp.concatenate([even[:, quarter:], odd[:, quarter:]], axis=1)
    edge = lax.broadcasted_iota(jnp.int32, real.shape, 1) == 0
    real_sq = real * real
    imag_sq = imag * imag
    level = 0.1 / (half + 1) * jnp.sum(real_sq + imag_sq, axis=1, keepdims=True) + 1e-06
    inv_real = lax.rsqrt(real_sq + jnp.where(edge, 0.0, imag_sq) + level)
    inv_imag = jnp.where(edge, lax.rsqrt(imag_sq + level), inv_real)
    real = (real * inv_real).astype(jnp.bfloat16).astype(jnp.float32)
    imag = (imag * inv_imag).astype(jnp.bfloat16).astype(jnp.float32)
    real_ref[...] = real
    imag_ref[...] = imag

    own_rows = slice(0, rows_blk)
    lefts = (real, jnp.where(edge, 0.0, imag), jnp.where(edge, imag, real))
    for j, value in enumerate(lefts):
        value = value[own_rows]
        for s in range(SEGS_DEV):
            at = SEGS_DEV * j + s
            for a in range(chans):
                row = s * chans + a
                left_ref[a, at : at + 1, :] = value[row : row + 1]

    first_step = (place + 1) * share
    cross_products(chans - share, first_step, chans, left_ref, real_ref, imag_ref, cross)

    chunk = share * chans
    rows_part = sets * chunk
    on_diagonal = lax.broadcasted_iota(jnp.int32, (chunk, LANE), 0) == (
        lax.broadcasted_iota(jnp.int32, (chunk, LANE), 1)
    )
    for j in range(parts - 1):
        partial = dot(cross[rows_part * j : rows_part * (j + 1), :], lag_table[...])
        others[j, :rows_part] = partial[:, :LANE].astype(jnp.bfloat16)
        last_rows = []
        for k in range(sets):
            column = partial[chunk * k : chunk * (k + 1), LANE : LANE + 1]
            spread = jnp.where(on_diagonal, column, 0.0)
            last_rows.append(jnp.sum(spread, axis=0, keepdims=True))
        last_rows.append(jnp.zeros((TAIL_ROWS - sets, LANE), jnp.float32))
        others[j, rows_part:] = jnp.concatenate(last_rows, axis=0).astype(jnp.bfloat16)


def mine_kernel(parts, real_ref, imag_ref, left_ref, lag_table, mine, cross):
    chans = left_ref.shape[0]
    share = chans // parts
    first_step = lax.axis_index("tm") * share
    cross_products(share, first_step, chans, left_ref, real_ref, imag_ref, cross)
    mine[...] = dot(cross[...], lag_table[...])


def combine_kernel(parts, last_mask, plan, mine, *refs):
    received, (self_out, pair_out) = refs[: parts - 1], refs[parts - 1 :]
    sets = ROUNDS + 1
    share, chans, _ = self_out.shape
    chunk = share * chans
    rows_part = sets * chunk

    low, high = free_masks_of(plan, last_mask)

    def slot_of(hits):
        return sum(jnp.where(hit, r, 0) for r, hit in enumerate(hits))

    slots = [
        slot_of([plan[r] == mask for r in range(ROUNDS)]) for mask in (1, last_mask, low, high)
    ]
    on_diagonal = lax.broadcasted_iota(jnp.int32, (chunk, LANE), 0) == (
        lax.broadcasted_iota(jnp.int32, (chunk, LANE), 1)
    )
    for k in range(sets):
        rows = slice(chunk * k, chunk * (k + 1))
        main = mine[rows, :LANE]
        last = mine[rows, LANE : LANE + 1]
        for ref in received:
            main = main + ref[rows, :].astype(jnp.float32)
            row = ref[rows_part:, :].astype(jnp.float32)[k : k + 1]
            last = last + jnp.sum(jnp.where(on_diagonal, row, 0.0), axis=1, keepdims=True)
        for i in range(share):
            step, q = divmod(k * share + i, sets)
            at = slice(i * chans, (i + 1) * chans)
            out = self_out if q == 0 else pair_out.at[slots[q - 1]]
            out[step, :, :LANE] = main[at]
            out[step, :, LANE:] = last[at]


def correlate(table_list, blocks, parts):
    lag_table = table_list[-1]
    length = lag_table.shape[0]
    half = length // 2
    own, near, far, far_tail, low, high = blocks
    chans, width = own.shape
    sets = ROUNDS + 1
    rows = sets * SEGS_DEV * chans
    rows_part = chans // parts * sets * chans
    vmem = pl.BlockSpec(memory_space=pltpu.VMEM)
    hbm = pl.BlockSpec(memory_space=pl.ANY)
    others, *spectra = pl.pallas_call(
        functools.partial(others_kernel, parts),
        out_shape=(
            pltpu.VMEM((parts - 1, rows_part + TAIL_ROWS, LANE), jnp.bfloat16),
            pltpu.VMEM((rows, half), jnp.float32),
            pltpu.VMEM((rows, half), jnp.float32),
            pltpu.VMEM((chans, 3 * SEGS_DEV, half), jnp.float32),
        ),
        in_specs=[vmem] * (len(table_list) + 3) + [hbm] * 3,
        out_specs=(vmem,) * 4,
        scratch_shapes=[
            pltpu.VMEM((3, chans, width), jnp.bfloat16),
            pltpu.VMEM((2 * rows, half), jnp.bfloat16),
            pltpu.VMEM((2 * rows, half), jnp.bfloat16),
            pltpu.VMEM(((parts - 1) * rows_part, length), jnp.bfloat16),
            pltpu.SemaphoreType.DMA((3,)),
        ],
        compiler_params=pltpu.CompilerParams(vmem_limit_bytes=VMEM_LIMIT),
    )(*table_list, own, far, far_tail, near, low, high)
    mine = pl.pallas_call(
        functools.partial(mine_kernel, parts),
        out_shape=pltpu.VMEM((rows_part, 2 * LANE), jnp.float32),
        in_specs=[vmem] * 4,
        out_specs=vmem,
        scratch_shapes=[pltpu.VMEM((rows_part, length), jnp.bfloat16)],
        compiler_params=pltpu.CompilerParams(vmem_limit_bytes=VMEM_LIMIT),
        cost_estimate=pl.CostEstimate(
            flops=2 * rows_part * length * 2 * LANE, bytes_accessed=0, transcendentals=0
        ),
    )(*spectra, lag_table)
    return mine, others


def combine(plan, mine, received, chans, last_mask):
    parts = len(received) + 1
    share = chans // parts
    plan = pltpu.with_memory_space_constraint(plan, pltpu.HBM)
    vmem = pl.BlockSpec(memory_space=pltpu.VMEM)
    smem = pl.BlockSpec(memory_space=pltpu.SMEM)
    return pl.pallas_call(
        functools.partial(combine_kernel, parts, last_mask),
        out_shape=(
            jax.ShapeDtypeStruct((share, chans, LAGS), jnp.float32),
            jax.ShapeDtypeStruct((ROUNDS, share, chans, LAGS), jnp.float32),
        ),
        in_specs=[smem] + [vmem] * parts,
        out_specs=(vmem, vmem),
        compiler_params=pltpu.CompilerParams(vmem_limit_bytes=VMEM_LIMIT),
    )(plan, mine, *received)


def from_partner(block, mask):
    chan_count = lax.axis_size("chan")
    return lax.ppermute(block, "chan", [(g, g ^ mask) for g in range(chan_count)])


def on_device(samples, fir_taps, plan):
    chan_count, parts = lax.axis_size("chan"), lax.axis_size("tm")
    chans, width = samples.shape
    near_mask, far_mask = 1, chan_count - 1
    free_masks = range(2, far_mask)
    tail = samples[:, width - LANE :]

    def tail_before(mask):
        route = [
            (g * parts + t, (g ^ mask) * parts + t + 1)
            for g in range(chan_count)
            for t in range(parts - 1)
        ]
        return lax.ppermute(tail, ("chan", "tm"), route)

    far = from_partner(samples, far_mask)
    before = tail_before(0)
    far_tail = tail_before(far_mask)
    branch, padded, table_list = prepare(plan, fir_taps, samples, (free_masks[0], far_mask))
    own = lax.dynamic_update_slice(padded, before, (0, 0))

    def send(masks):
        return [from_partner(own, mask) for mask in (near_mask, *masks)]

    pairs = [(low, high) for high in free_masks for low in free_masks if low < high]
    if len(pairs) <= MAX_BRANCHES:
        routes = [functools.partial(send, pair) for pair in pairs]
        near, low, high = lax.switch(branch.reshape(()), routes)
    else:
        routes = [functools.partial(send, (mask,)) for mask in free_masks]
        near, low = lax.switch(free_masks_of(plan, far_mask)[0] - free_masks[0], routes)
        _, high = lax.switch(free_masks_of(plan, far_mask)[1] - free_masks[0], routes)

    mine, others = correlate(table_list, [own, near, far, far_tail, low, high], parts)
    received = [
        lax.ppermute(others[j - 1], "tm", [(t, (t + j) % parts) for t in range(parts)])
        for j in range(1, parts)
    ]
    return combine(plan, mine, received, chans, far_mask)


def solution(mesh):
    in_specs = (P("chan", "tm"), P(), P())
    out_specs = (P(("chan", "tm"), None, None), P(None, ("chan", "tm"), None, None))
    return jax.shard_map(
        on_device, mesh=mesh, in_specs=in_specs, out_specs=out_specs, check_vma=False
    )
```

```python
import functools
import math

import jax
import jax.numpy as jnp
import ml_dtypes
import numpy as np
from jax import lax
from jax.experimental import pallas as pl
from jax.experimental.pallas import tpu as pltpu
from jax.sharding import PartitionSpec as P

SEGS_DEV = 2
LAGS = 129
ROUNDS = 4
LANE = 128
MAX_BRANCHES = 128
OUT_GROUPS = 2
VMEM_LIMIT = 8 * 1024 * 1024
KERNEL_VMEM = 24 * 1024 * 1024
VMEM = pl.BlockSpec(memory_space=pltpu.VMEM)
SMEM = pl.BlockSpec(memory_space=pltpu.SMEM)
HBM = pl.BlockSpec(memory_space=pl.ANY)


def split_table(table):
    high = table.astype(ml_dtypes.bfloat16)
    low = (table - high.astype(np.float64)).astype(ml_dtypes.bfloat16)
    return np.concatenate([high, high, low], axis=0)


def tables(length):
    half = length // 2
    quarter = length // 4
    sample = np.arange(half)[:, None]

    def columns(freqs):
        angle = 2.0 * math.pi / length * (sample * freqs[None, :] % length)
        return np.cos(angle), -np.sin(angle)

    even = 2 * np.arange(quarter)
    odd = even + 1
    even_re, even_im = columns(even)
    even_im[:, 0] = 1.0 - 2.0 * (np.arange(half) % 2)
    odd_re, odd_im = columns(odd)
    even_table = np.concatenate([even_re, even_im], axis=1)
    odd_table = np.concatenate([odd_re, odd_im], axis=1)

    freqs = np.concatenate([even, odd])[:, None]
    lag = (np.arange(LAGS) - LAGS // 2)[None, :]
    angle = 2.0 * math.pi / length * (lag * freqs % length)
    weight = np.where(freqs == 0, 1.0, 2.0) / length
    lag_cos = weight * np.cos(angle)
    lag_sin = weight * np.sin(angle)
    lag_sin[0] = (1.0 - 2.0 * (np.abs(lag[0]) % 2)) / length
    lag_table = np.zeros((length, 2 * LANE))
    lag_table[:, :LAGS] = np.concatenate([lag_cos, lag_sin], axis=0)
    return (
        split_table(even_table),
        split_table(odd_table),
        lag_table.astype(ml_dtypes.bfloat16),
    )


def dot(left, right):
    return jnp.dot(left, right, preferred_element_type=jnp.float32)


def free_masks_of(plan, last_mask):
    masks = [plan[r] for r in range(ROUNDS)]
    free = [(mask != 1) & (mask != last_mask) for mask in masks]
    low = functools.reduce(
        jnp.minimum, [jnp.where(ok, mask, last_mask) for ok, mask in zip(free, masks)]
    )
    high = functools.reduce(jnp.maximum, [jnp.where(ok, mask, 0) for ok, mask in zip(free, masks)])
    return low, high


def prepare_kernel(last_mask, plan, taps, samples, *refs):
    tables_hbm, (branch, record, toep), refs = refs[:3], refs[3:6], refs[6:]
    tables_vmem, (own_sem, table_sems) = refs[:3], refs[3:]
    chans = samples.shape[0]
    copies = [pltpu.make_async_copy(samples, record.at[pl.ds(0, chans)], own_sem)]
    copies += [
        pltpu.make_async_copy(table, table_vmem, table_sems.at[i])
        for i, (table, table_vmem) in enumerate(zip(tables_hbm, tables_vmem))
    ]
    for copy in copies:
        copy.start()
    low, high = (mask - 2 for mask in free_masks_of(plan, last_mask))
    branch[0] = high * (high - 1) // 2 + low

    lane = lax.broadcasted_iota(jnp.int32, (1, 2 * LANE), 1)
    base = jnp.zeros((1, 2 * LANE), jnp.float32)
    for j in range(taps.shape[0]):
        base = jnp.where(lane == j, taps[j], base)
    base = jnp.broadcast_to(base, (2 * LANE, 2 * LANE))
    toeplitz = pltpu.roll(base, LANE, 1, stride=1, stride_axis=0)[:, :LANE]
    toep_hi = toeplitz.astype(jnp.bfloat16)
    toep[:, :LANE] = toep_hi
    toep[:, LANE:] = (toeplitz - toep_hi.astype(jnp.float32)).astype(jnp.bfloat16)
    for copy in copies:
        copy.wait()


def prepare(plan, fir_taps, samples, last_mask, parts):
    chans, width = samples.shape
    table_list = tables(width // SEGS_DEV)
    plan, fir_taps, samples, *table_list = (
        pltpu.with_memory_space_constraint(jnp.asarray(array), pltpu.HBM)
        for array in (plan, fir_taps, samples, *table_list)
    )
    branch, record, toep, *table_list = pl.pallas_call(
        functools.partial(prepare_kernel, last_mask),
        out_shape=(
            jax.ShapeDtypeStruct((1,), jnp.int32),
            pltpu.VMEM((parts * chans, width), jnp.bfloat16),
            pltpu.VMEM((2 * LANE, 2 * LANE), jnp.bfloat16),
            *[pltpu.VMEM(table.shape, jnp.bfloat16) for table in table_list],
        ),
        in_specs=[SMEM, SMEM] + [HBM] * (1 + len(table_list)),
        out_specs=(SMEM,) + (VMEM,) * (2 + len(table_list)),
        scratch_shapes=[
            pltpu.SemaphoreType.DMA,
            pltpu.SemaphoreType.DMA((len(table_list),)),
        ],
        compiler_params=pltpu.CompilerParams(vmem_limit_bytes=VMEM_LIMIT),
    )(plan, fir_taps, samples, *table_list)
    return branch, record, (toep, *table_list)


def add_spectra(columns_of, place, parts, shape, first_row, refs):
    chans, width = shape
    toep, sums, diffs = refs
    half = width // SEGS_DEV // 2
    tiles = half // LANE
    for piece in range(parts):
        tail = columns_of((piece + 1) % parts, width - LANE, width)
        has_before = jnp.where(lax.rem(place + parts - piece, parts) == 0, 0.0, 1.0)
        tail = (tail.astype(jnp.float32) * has_before).astype(jnp.bfloat16)
        windows = [jnp.concatenate([tail, columns_of(piece, 0, LANE)], axis=1)]
        windows += [
            columns_of(piece, LANE * (k - 1), LANE * (k + 1)) for k in range(1, width // LANE)
        ]
        both = dot(jnp.concatenate(windows, axis=0), toep[...])
        filtered = both[:, :LANE] + both[:, LANE:]
        for s in range(SEGS_DEV):
            row = first_row + (piece * SEGS_DEV + s) * chans
            for k in range(tiles):
                lo = (s * 2 * tiles + k) * chans
                hi = lo + tiles * chans
                first, second = filtered[lo : lo + chans], filtered[hi : hi + chans]
                for ref, value in ((sums, first + second), (diffs, first - second)):
                    high = value.astype(jnp.bfloat16)
                    low = (value - high.astype(jnp.float32)).astype(jnp.bfloat16)
                    for j, part in enumerate((high, low, high)):
                        at = half * j + LANE * k
                        ref[row : row + chans, at : at + LANE] = part


def whiten(sums, diffs, even_table, odd_table, real_ref, imag_ref):
    half = even_table.shape[1]
    quarter = half // 2
    even = dot(sums[...], even_table[...])
    odd = dot(diffs[...], odd_table[...])
    real = jnp.concatenate([even[:, :quarter], odd[:, :quarter]], axis=1)
    imag = jnp.concatenate([even[:, quarter:], odd[:, quarter:]], axis=1)
    edge = lax.broadcasted_iota(jnp.int32, real.shape, 1) == 0
    real_sq = real * real
    imag_sq = imag * imag
    level = 0.1 / (half + 1) * jnp.sum(real_sq + imag_sq, axis=1, keepdims=True) + 1e-06
    inv_real = lax.rsqrt(real_sq + jnp.where(edge, 0.0, imag_sq) + level)
    inv_imag = jnp.where(edge, lax.rsqrt(imag_sq + level), inv_real)
    real_ref[...] = (real * inv_real).astype(jnp.bfloat16).astype(jnp.float32)
    imag_ref[...] = (imag * inv_imag).astype(jnp.bfloat16).astype(jnp.float32)


def cross_spectra(first, count, chans, segs, left_ref, real_ref, imag_ref, cross):
    rows, half = real_ref.shape
    rows_blk = segs * chans
    sets = rows // rows_blk

    @pl.loop(0, count)
    def _(i):
        a = first + i
        at = pl.multiple_of(a * sets * chans, sets * chans)
        for c in range(half // LANE):
            cols = slice(LANE * c, LANE * (c + 1))
            left = [
                jnp.broadcast_to(left_ref[a, j : j + 1, cols], (chans, LANE))
                for j in range(3 * segs)
            ]
            for q in range(sets):
                cos_part = sin_part = 0.0
                for s in range(segs):
                    row_b = slice(q * rows_blk + s * chans, q * rows_blk + (s + 1) * chans)
                    re_b, im_b = real_ref[row_b, cols], imag_ref[row_b, cols]
                    re_a, im_a, x_a = (left[segs * j + s] for j in range(3))
                    cos_part += re_a * re_b + im_a * im_b
                    sin_part += x_a * im_b - im_a * re_b
                at_q = pl.ds(at + q * chans, chans)
                cross[at_q, cols] = cos_part.astype(jnp.bfloat16)
                cross[at_q, half + LANE * c : half + LANE * (c + 1)] = sin_part.astype(jnp.bfloat16)


def spectra_scratch(sets, parts, chans, length, share):
    rows, half = sets * parts * SEGS_DEV * chans, length // 2
    return [
        pltpu.VMEM((rows, 3 * half), jnp.bfloat16),
        pltpu.VMEM((rows, 3 * half), jnp.bfloat16),
        pltpu.VMEM((rows, half), jnp.float32),
        pltpu.VMEM((rows, half), jnp.float32),
        pltpu.VMEM((share * sets * chans, length), jnp.bfloat16),
    ]


def rows_of_block(block, chans):
    return lambda piece, lo, hi: block[piece * chans : (piece + 1) * chans, lo:hi]


def early_kernel(parts, toep, even_table, odd_table, lag_table, own, near, *refs):
    self_out, near_out, left_ref, sums, diffs, real_ref, imag_ref, cross = refs
    share, chans, _ = self_out.shape
    segs = parts * SEGS_DEV
    half = even_table.shape[1]
    place = lax.axis_index("tm")
    for q, block in enumerate((own, near)):
        columns_of = rows_of_block(block, chans)
        first_row = q * segs * chans
        shape = (chans, own.shape[1])
        add_spectra(columns_of, place, parts, shape, first_row, (toep, sums, diffs))
    whiten(sums, diffs, even_table, odd_table, real_ref, imag_ref)

    def picked(ref, s):
        value = ref[s * chans : s * chans + share, :]
        for owner in range(1, parts):
            at = s * chans + owner * share
            value = jnp.where(place == owner, ref[at : at + share, :], value)
        return value

    edge = lax.broadcasted_iota(jnp.int32, (share, half), 1) == 0
    for s in range(segs):
        real_s, imag_s = picked(real_ref, s), picked(imag_ref, s)
        lefts = (real_s, jnp.where(edge, 0.0, imag_s), jnp.where(edge, imag_s, real_s))
        for j, value in enumerate(lefts):
            for a in range(share):
                left_ref[a, segs * j + s : segs * j + s + 1, :] = value[a : a + 1]

    cross_spectra(0, share, chans, segs, left_ref, real_ref, imag_ref, cross)
    result = dot(cross[...], lag_table[...])
    for a in range(share):
        at = a * 2 * chans
        self_out[a] = result[at : at + chans, :LAGS]
        near_out[a] = result[at + chans : at + 2 * chans, :LAGS]


def far_kernel(parts, toep, even_table, odd_table, lag_table, left_ref, far, *refs):
    far_more, (far_out, *refs) = refs[: parts - 1], refs[parts - 1 :]
    sums, diffs, real_ref, imag_ref, cross = refs
    share, chans, _ = far_out.shape
    segs = parts * SEGS_DEV

    def columns_of(piece, lo, hi):
        return (far, *far_more)[piece][:, lo:hi]

    place = lax.axis_index("tm")
    add_spectra(columns_of, place, parts, far.shape, 0, (toep, sums, diffs))
    whiten(sums, diffs, even_table, odd_table, real_ref, imag_ref)
    cross_spectra(0, share, chans, segs, left_ref, real_ref, imag_ref, cross)
    result = dot(cross[...], lag_table[...])
    for a in range(share):
        far_out[a] = result[a * chans : (a + 1) * chans, :LAGS]


def late_kernel(parts, last_mask, plan, toep, even_table, odd_table, lag_table, *refs):
    near_corr, far_corr, left_hbm, low, high, pair_out = refs[:6]
    arrived, left_ref, sums, diffs, real_ref, imag_ref, cross, staged = refs[6:14]
    left_sem, free_sems, out_sems, done_sems = refs[14:]

    chans = arrived.shape[1] // parts
    share = left_ref.shape[0]
    segs = parts * SEGS_DEV
    place = lax.axis_index("tm")
    free_copies = [
        pltpu.make_async_copy(source, arrived.at[i], free_sems.at[i])
        for i, source in enumerate((low, high))
    ]
    left_copy = pltpu.make_async_copy(left_hbm, left_ref, left_sem)
    for copy in free_copies + [left_copy]:
        copy.start()

    low_mask, high_mask = free_masks_of(plan, last_mask)
    slots = [
        sum(jnp.where(plan[r] == mask, r, 0) for r in range(ROUNDS))
        for mask in (1, last_mask, low_mask, high_mask)
    ]
    done_copies = [
        pltpu.make_async_copy(corr, pair_out.at[slots[i]], done_sems.at[i])
        for i, corr in enumerate((near_corr, far_corr))
    ]
    for copy in done_copies:
        copy.start()

    for q, copy in enumerate(free_copies):
        copy.wait()
        columns_of = rows_of_block(arrived.at[q], chans)
        shape = (chans, arrived.shape[2])
        first_row = q * segs * chans
        add_spectra(columns_of, place, parts, shape, first_row, (toep, sums, diffs))
    whiten(sums, diffs, even_table, odd_table, real_ref, imag_ref)
    left_copy.wait()

    sets = len(free_copies)
    out_copies = []
    groups = OUT_GROUPS if share % OUT_GROUPS == 0 else 1
    count = share // groups
    for group in range(groups):
        first = group * count
        cross_spectra(first, count, chans, segs, left_ref, real_ref, imag_ref, cross)
        rows = slice(first * sets * chans, (first + count) * sets * chans)
        result = dot(cross[rows, :], lag_table[...])
        for i in range(count):
            for q in range(sets):
                at = (i * sets + q) * chans
                staged[q, first + i] = result[at : at + chans, :LAGS]
        for q in range(sets):
            piece = pl.ds(first, count)
            sem = out_sems.at[group * sets + q]
            out_copies.append(
                pltpu.make_async_copy(staged.at[q, piece], pair_out.at[slots[2 + q], piece], sem)
            )
            out_copies[-1].start()
    for copy in done_copies + out_copies:
        copy.wait()


def early(table_list, own, near, parts):
    chans, length = own.shape[0] // parts, own.shape[1] // SEGS_DEV
    share = chans // parts
    corr = jax.ShapeDtypeStruct((share, chans, LAGS), jnp.float32)
    left = jax.ShapeDtypeStruct((share, 3 * parts * SEGS_DEV, length // 2), jnp.float32)
    return pl.pallas_call(
        functools.partial(early_kernel, parts),
        out_shape=(corr, corr, left),
        in_specs=[VMEM] * (len(table_list) + 2),
        out_specs=(VMEM,) * 3,
        scratch_shapes=spectra_scratch(2, parts, chans, length, share),
        compiler_params=pltpu.CompilerParams(vmem_limit_bytes=KERNEL_VMEM),
    )(*table_list, own, near)


def middle(table_list, left, far, far_more):
    parts = len(far_more) + 1
    chans, length = far.shape[0], far.shape[1] // SEGS_DEV
    share = chans // parts
    return pl.pallas_call(
        functools.partial(far_kernel, parts),
        out_shape=jax.ShapeDtypeStruct((share, chans, LAGS), jnp.float32),
        in_specs=[VMEM] * (len(table_list) + 1 + parts),
        out_specs=VMEM,
        scratch_shapes=spectra_scratch(1, parts, chans, length, share),
        compiler_params=pltpu.CompilerParams(vmem_limit_bytes=KERNEL_VMEM),
    )(*table_list, left, far, *far_more)


def late(plan, table_list, near_corr, far_corr, left, low, high, last_mask):
    share, chans, _ = near_corr.shape
    parts = chans // share
    length = low.shape[1] // SEGS_DEV
    plan = pltpu.with_memory_space_constraint(plan, pltpu.HBM)
    return pl.pallas_call(
        functools.partial(late_kernel, parts, last_mask),
        out_shape=jax.ShapeDtypeStruct((ROUNDS, share, chans, LAGS), jnp.float32),
        in_specs=[SMEM] + [VMEM] * len(table_list) + [HBM] * 5,
        out_specs=HBM,
        scratch_shapes=[
            pltpu.VMEM((2, *low.shape), jnp.bfloat16),
            pltpu.VMEM(left.shape, jnp.float32),
            *spectra_scratch(2, parts, chans, length, share),
            pltpu.VMEM((2, share, chans, LAGS), jnp.float32),
            pltpu.SemaphoreType.DMA,
            pltpu.SemaphoreType.DMA((2,)),
            pltpu.SemaphoreType.DMA((2 * OUT_GROUPS,)),
            pltpu.SemaphoreType.DMA((2,)),
        ],
        compiler_params=pltpu.CompilerParams(vmem_limit_bytes=KERNEL_VMEM),
    )(plan, *table_list, near_corr, far_corr, left, low, high)


def from_partner(block, mask):
    chan_count = lax.axis_size("chan")
    return lax.ppermute(block, "chan", [(g, g ^ mask) for g in range(chan_count)])


def from_times(block):
    parts = lax.axis_size("tm")
    return [
        lax.ppermute(block, "tm", [(t, (t + j) % parts) for t in range(parts)])
        for j in range(1, parts)
    ]


def on_device(samples, fir_taps, plan):
    chan_count, parts = lax.axis_size("chan"), lax.axis_size("tm")
    chans = samples.shape[0]
    near_mask, far_mask = 1, chan_count - 1
    free_masks = range(2, far_mask)

    far = from_partner(samples, far_mask)
    others = from_times(samples)
    branch, own, table_list = prepare(plan, fir_taps, samples, far_mask, parts)
    for j, piece in enumerate(others):
        own = lax.dynamic_update_slice(own, piece, ((j + 1) * chans, 0))

    def fixed_work():
        near = from_partner(own, near_mask)
        far_more = from_times(far)
        self_corr, near_corr, left = early(table_list, own, near, parts)
        far_corr = middle(table_list, left, far, far_more)
        return self_corr, near_corr, far_corr, left

    def branch_of(low_mask, high_mask):
        def run():
            blocks = from_partner(own, low_mask), from_partner(own, high_mask)
            return *fixed_work(), *blocks

        return run

    pairs = [(low, high) for high in free_masks for low in free_masks if low < high]
    if len(pairs) <= MAX_BRANCHES:
        branches = [branch_of(*pair) for pair in pairs]
        self_corr, *corrs, left, low, high = lax.switch(branch.reshape(()), branches)
    else:
        sends = [functools.partial(from_partner, mask=mask) for mask in free_masks]
        low, high = (
            lax.switch(mask - free_masks[0], sends, own) for mask in free_masks_of(plan, far_mask)
        )
        self_corr, *corrs, left = fixed_work()
    return self_corr, late(plan, table_list, *corrs, left, low, high, far_mask)


def solution(mesh):
    in_specs = (P("chan", "tm"), P(), P())
    out_specs = (P(("chan", "tm"), None, None), P(None, ("chan", "tm"), None, None))
    return jax.shard_map(
        on_device, mesh=mesh, in_specs=in_specs, out_specs=out_specs, check_vma=False
    )
```

```python
import functools
import math

import jax
import jax.numpy as jnp
import ml_dtypes
import numpy as np
from jax import lax
from jax.experimental import pallas as pl
from jax.experimental.pallas import tpu as pltpu
from jax.sharding import PartitionSpec as P

SEGS_DEV = 2
LAGS = 129
ROUNDS = 4
LANE = 128
MAX_BRANCHES = 128
OUT_GROUPS = 2
VMEM_LIMIT = 8 * 1024 * 1024
KERNEL_VMEM = 24 * 1024 * 1024
VMEM = pl.BlockSpec(memory_space=pltpu.VMEM)
SMEM = pl.BlockSpec(memory_space=pltpu.SMEM)
HBM = pl.BlockSpec(memory_space=pl.ANY)


def split_table(table):
    high = table.astype(ml_dtypes.bfloat16)
    low = (table - high.astype(np.float64)).astype(ml_dtypes.bfloat16)
    return np.concatenate([high, high, low], axis=0)


def tables(length):
    half = length // 2
    quarter = length // 4
    sample = np.arange(half)[:, None]

    def columns(freqs):
        angle = 2.0 * math.pi / length * (sample * freqs[None, :] % length)
        return np.cos(angle), -np.sin(angle)

    even = 2 * np.arange(quarter)
    odd = even + 1
    even_re, even_im = columns(even)
    even_im[:, 0] = 1.0 - 2.0 * (np.arange(half) % 2)
    odd_re, odd_im = columns(odd)
    even_table = np.concatenate([even_re, even_im], axis=1)
    odd_table = np.concatenate([odd_re, odd_im], axis=1)

    freqs = np.concatenate([even, odd])[:, None]
    lag = (np.arange(LAGS) - LAGS // 2)[None, :]
    angle = 2.0 * math.pi / length * (lag * freqs % length)
    weight = np.where(freqs == 0, 1.0, 2.0) / length
    lag_cos = weight * np.cos(angle)
    lag_sin = weight * np.sin(angle)
    lag_sin[0] = (1.0 - 2.0 * (np.abs(lag[0]) % 2)) / length
    lag_table = np.zeros((length, 2 * LANE))
    lag_table[:, :LAGS] = np.concatenate([lag_cos, lag_sin], axis=0)
    return (
        split_table(even_table),
        split_table(odd_table),
        lag_table.astype(ml_dtypes.bfloat16),
    )


def dot(left, right):
    return jnp.dot(left, right, preferred_element_type=jnp.float32)


def free_masks_of(plan, last_mask):
    masks = [plan[r] for r in range(ROUNDS)]
    free = [(mask != 1) & (mask != last_mask) for mask in masks]
    low = functools.reduce(
        jnp.minimum, [jnp.where(ok, mask, last_mask) for ok, mask in zip(free, masks)]
    )
    high = functools.reduce(jnp.maximum, [jnp.where(ok, mask, 0) for ok, mask in zip(free, masks)])
    return low, high


def prepare_kernel(last_mask, plan, taps, samples, *refs):
    tables_hbm, (branch, record, toep), refs = refs[:2], refs[2:5], refs[5:]
    tables_vmem, (own_sem, table_sems) = refs[:2], refs[2:]
    chans = samples.shape[0]
    copies = [pltpu.make_async_copy(samples, record.at[pl.ds(0, chans)], own_sem)]
    copies += [
        pltpu.make_async_copy(table, table_vmem, table_sems.at[i])
        for i, (table, table_vmem) in enumerate(zip(tables_hbm, tables_vmem))
    ]
    for copy in copies:
        copy.start()
    low, high = (mask - 2 for mask in free_masks_of(plan, last_mask))
    branch[0] = high * (high - 1) // 2 + low

    lane = lax.broadcasted_iota(jnp.int32, (1, 2 * LANE), 1)
    base = jnp.zeros((1, 2 * LANE), jnp.float32)
    for j in range(taps.shape[0]):
        base = jnp.where(lane == j, taps[j], base)
    base = jnp.broadcast_to(base, (2 * LANE, 2 * LANE))
    toeplitz = pltpu.roll(base, LANE, 1, stride=1, stride_axis=0)[:, :LANE]
    toep_hi = toeplitz.astype(jnp.bfloat16)
    toep[:, :LANE] = toep_hi
    toep[:, LANE:] = (toeplitz - toep_hi.astype(jnp.float32)).astype(jnp.bfloat16)
    for copy in copies:
        copy.wait()


def prepare(plan, fir_taps, samples, last_mask, parts):
    chans, width = samples.shape
    *table_list, lag_table = tables(width // SEGS_DEV)
    plan, fir_taps, samples, *table_list = (
        pltpu.with_memory_space_constraint(jnp.asarray(array), pltpu.HBM)
        for array in (plan, fir_taps, samples, *table_list)
    )
    branch, record, toep, *table_list = pl.pallas_call(
        functools.partial(prepare_kernel, last_mask),
        out_shape=(
            jax.ShapeDtypeStruct((1,), jnp.int32),
            pltpu.VMEM((parts * chans, width), jnp.bfloat16),
            pltpu.VMEM((2 * LANE, 2 * LANE), jnp.bfloat16),
            *[pltpu.VMEM(table.shape, jnp.bfloat16) for table in table_list],
        ),
        in_specs=[SMEM, SMEM] + [HBM] * (1 + len(table_list)),
        out_specs=(SMEM,) + (VMEM,) * (2 + len(table_list)),
        scratch_shapes=[
            pltpu.SemaphoreType.DMA,
            pltpu.SemaphoreType.DMA((len(table_list),)),
        ],
        compiler_params=pltpu.CompilerParams(vmem_limit_bytes=VMEM_LIMIT),
    )(plan, fir_taps, samples, *table_list)
    return branch, record, (toep, *table_list, jnp.asarray(lag_table))


def add_spectra(columns_of, place, parts, shape, first_row, refs):
    chans, width = shape
    toep, sums, diffs = refs
    half = width // SEGS_DEV // 2
    tiles = half // LANE
    for piece in range(parts):
        tail = columns_of((piece + 1) % parts, width - LANE, width)
        has_before = jnp.where(lax.rem(place + parts - piece, parts) == 0, 0.0, 1.0)
        tail = (tail.astype(jnp.float32) * has_before).astype(jnp.bfloat16)
        windows = [jnp.concatenate([tail, columns_of(piece, 0, LANE)], axis=1)]
        windows += [
            columns_of(piece, LANE * (k - 1), LANE * (k + 1)) for k in range(1, width // LANE)
        ]
        both = dot(jnp.concatenate(windows, axis=0), toep[...])
        filtered = both[:, :LANE] + both[:, LANE:]
        for s in range(SEGS_DEV):
            row = first_row + (piece * SEGS_DEV + s) * chans
            for k in range(tiles):
                lo = (s * 2 * tiles + k) * chans
                hi = lo + tiles * chans
                first, second = filtered[lo : lo + chans], filtered[hi : hi + chans]
                for ref, value in ((sums, first + second), (diffs, first - second)):
                    high = value.astype(jnp.bfloat16)
                    low = (value - high.astype(jnp.float32)).astype(jnp.bfloat16)
                    for j, part in enumerate((high, low, high)):
                        at = half * j + LANE * k
                        ref[row : row + chans, at : at + LANE] = part


def whiten(sums, diffs, even_table, odd_table, real_ref, imag_ref):
    half = even_table.shape[1]
    quarter = half // 2
    even = dot(sums[...], even_table[...])
    odd = dot(diffs[...], odd_table[...])
    real = jnp.concatenate([even[:, :quarter], odd[:, :quarter]], axis=1)
    imag = jnp.concatenate([even[:, quarter:], odd[:, quarter:]], axis=1)
    edge = lax.broadcasted_iota(jnp.int32, real.shape, 1) == 0
    real_sq = real * real
    imag_sq = imag * imag
    level = 0.1 / (half + 1) * jnp.sum(real_sq + imag_sq, axis=1, keepdims=True) + 1e-06
    inv_real = lax.rsqrt(real_sq + jnp.where(edge, 0.0, imag_sq) + level)
    inv_imag = jnp.where(edge, lax.rsqrt(imag_sq + level), inv_real)
    real_ref[...] = (real * inv_real).astype(jnp.bfloat16).astype(jnp.float32)
    imag_ref[...] = (imag * inv_imag).astype(jnp.bfloat16).astype(jnp.float32)


def cross_spectra(first, count, chans, segs, left_ref, real_ref, imag_ref, cross):
    rows, half = real_ref.shape
    rows_blk = segs * chans
    sets = rows // rows_blk

    @pl.loop(0, count)
    def _(i):
        a = first + i
        at = pl.multiple_of(a * sets * chans, sets * chans)
        for c in range(half // LANE):
            cols = slice(LANE * c, LANE * (c + 1))
            left = [
                jnp.broadcast_to(left_ref[a, j : j + 1, cols], (chans, LANE))
                for j in range(3 * segs)
            ]
            for q in range(sets):
                cos_part = sin_part = 0.0
                for s in range(segs):
                    row_b = slice(q * rows_blk + s * chans, q * rows_blk + (s + 1) * chans)
                    re_b, im_b = real_ref[row_b, cols], imag_ref[row_b, cols]
                    re_a, im_a, x_a = (left[segs * j + s] for j in range(3))
                    cos_part += re_a * re_b + im_a * im_b
                    sin_part += x_a * im_b - im_a * re_b
                at_q = pl.ds(at + q * chans, chans)
                cross[at_q, cols] = cos_part.astype(jnp.bfloat16)
                cross[at_q, half + LANE * c : half + LANE * (c + 1)] = sin_part.astype(jnp.bfloat16)


def spectra_scratch(sets, parts, chans, length, share):
    rows, half = sets * parts * SEGS_DEV * chans, length // 2
    return [
        pltpu.VMEM((rows, 3 * half), jnp.bfloat16),
        pltpu.VMEM((rows, 3 * half), jnp.bfloat16),
        pltpu.VMEM((rows, half), jnp.float32),
        pltpu.VMEM((rows, half), jnp.float32),
        pltpu.VMEM((share * sets * chans, length), jnp.bfloat16),
    ]


def rows_of_block(block, chans):
    return lambda piece, lo, hi: block[piece * chans : (piece + 1) * chans, lo:hi]


def correlate_kernel(parts, last_mask, plan, toep, even_table, odd_table, lag_hbm, *refs):
    own, far, near, low, high, refs = *refs[:5], refs[5:]
    far_more, (self_out, pair_out), refs = refs[: parts - 1], refs[parts - 1 : parts + 1], refs[parts + 1 :]
    lag_table, arrived, far_arrived, left_ref, sums, diffs, real_ref, imag_ref, cross, staged = refs[:10]
    lag_sem, sems, far_sems, out_sems = refs[10:]

    chans, width = far.shape
    half = even_table.shape[1]
    share = left_ref.shape[0]
    segs = parts * SEGS_DEV
    sets = ROUNDS + 1
    place = lax.axis_index("tm")
    copies = [
        pltpu.make_async_copy(source, arrived.at[i], sems.at[i])
        for i, source in enumerate((near, low, high))
    ]
    far_copies = [
        pltpu.make_async_copy(source, far_arrived.at[i], far_sems.at[i])
        for i, source in enumerate(far_more)
    ]
    lag_copy = pltpu.make_async_copy(lag_hbm, lag_table, lag_sem)
    for copy in far_copies + copies + [lag_copy]:
        copy.start()

    def far_columns(piece, lo, hi):
        return far[:, lo:hi] if piece == 0 else far_arrived[piece - 1, :, lo:hi]

    blocks = [
        (rows_of_block(own, chans), []),
        (rows_of_block(arrived.at[0], chans), copies[:1]),
        (far_columns, far_copies),
        (rows_of_block(arrived.at[1], chans), copies[1:2]),
        (rows_of_block(arrived.at[2], chans), copies[2:]),
    ]
    for q in (0, 2, 1, 3, 4):
        columns_of, needs = blocks[q]
        for copy in needs:
            copy.wait()
        first_row = q * segs * chans
        add_spectra(columns_of, place, parts, far.shape, first_row, (toep, sums, diffs))
    whiten(sums, diffs, even_table, odd_table, real_ref, imag_ref)

    def picked(ref, s):
        value = ref[s * chans : s * chans + share, :]
        for owner in range(1, parts):
            at = s * chans + owner * share
            value = jnp.where(place == owner, ref[at : at + share, :], value)
        return value

    edge = lax.broadcasted_iota(jnp.int32, (share, half), 1) == 0
    for s in range(segs):
        real_s, imag_s = picked(real_ref, s), picked(imag_ref, s)
        lefts = (real_s, jnp.where(edge, 0.0, imag_s), jnp.where(edge, imag_s, real_s))
        for j, value in enumerate(lefts):
            for a in range(share):
                left_ref[a, segs * j + s : segs * j + s + 1, :] = value[a : a + 1]

    low_mask, high_mask = free_masks_of(plan, last_mask)
    slots = [
        sum(jnp.where(plan[r] == mask, r, 0) for r in range(ROUNDS))
        for mask in (1, last_mask, low_mask, high_mask)
    ]
    outs = [self_out, *(pair_out.at[slot] for slot in slots)]
    lag_copy.wait()
    out_copies = []
    groups = OUT_GROUPS if share % OUT_GROUPS == 0 else 1
    count = share // groups
    for group in range(groups):
        first = group * count
        cross_spectra(first, count, chans, segs, left_ref, real_ref, imag_ref, cross)
        rows = slice(first * sets * chans, (first + count) * sets * chans)
        result = dot(cross[rows, :], lag_table[...])
        for i in range(count):
            for q in range(sets):
                at = (i * sets + q) * chans
                staged[q, first + i] = result[at : at + chans, :LAGS]
        for q, out in enumerate(outs):
            piece = pl.ds(first, count)
            sem = out_sems.at[group * sets + q]
            out_copies.append(pltpu.make_async_copy(staged.at[q, piece], out.at[piece], sem))
            out_copies[-1].start()
    for copy in out_copies:
        copy.wait()


def correlate(plan, table_list, own, near, far, far_more, low, high, last_mask):
    chans, width = far.shape
    parts = len(far_more) + 1
    share = chans // parts
    length = width // SEGS_DEV
    sets = ROUNDS + 1
    *table_list, lag_table = table_list
    plan, lag_table = (
        pltpu.with_memory_space_constraint(array, pltpu.HBM) for array in (plan, lag_table)
    )
    return pl.pallas_call(
        functools.partial(correlate_kernel, parts, last_mask),
        out_shape=(
            jax.ShapeDtypeStruct((share, chans, LAGS), jnp.float32),
            jax.ShapeDtypeStruct((ROUNDS, share, chans, LAGS), jnp.float32),
        ),
        in_specs=[SMEM] + [VMEM] * len(table_list) + [HBM] + [VMEM] * 2 + [HBM] * (parts + 2),
        out_specs=(HBM, HBM),
        scratch_shapes=[
            pltpu.VMEM(lag_table.shape, jnp.bfloat16),
            pltpu.VMEM((3, *own.shape), jnp.bfloat16),
            pltpu.VMEM((parts - 1, chans, width), jnp.bfloat16),
            pltpu.VMEM((share, 3 * parts * SEGS_DEV, length // 2), jnp.float32),
            *spectra_scratch(sets, parts, chans, length, share),
            pltpu.VMEM((sets, share, chans, LAGS), jnp.float32),
            pltpu.SemaphoreType.DMA,
            pltpu.SemaphoreType.DMA((3,)),
            pltpu.SemaphoreType.DMA((parts - 1,)),
            pltpu.SemaphoreType.DMA((sets * OUT_GROUPS,)),
        ],
        compiler_params=pltpu.CompilerParams(vmem_limit_bytes=KERNEL_VMEM),
    )(plan, *table_list, lag_table, own, far, near, low, high, *far_more)


def from_partner(block, mask):
    chan_count = lax.axis_size("chan")
    return lax.ppermute(block, "chan", [(g, g ^ mask) for g in range(chan_count)])


def from_times(block):
    parts = lax.axis_size("tm")
    return [
        lax.ppermute(block, "tm", [(t, (t + j) % parts) for t in range(parts)])
        for j in range(1, parts)
    ]


def on_device(samples, fir_taps, plan):
    chan_count, parts = lax.axis_size("chan"), lax.axis_size("tm")
    chans = samples.shape[0]
    near_mask, far_mask = 1, chan_count - 1
    free_masks = range(2, far_mask)

    far = from_partner(samples, far_mask)
    others = from_times(samples)
    branch, own, table_list = prepare(plan, fir_taps, samples, far_mask, parts)
    for j, piece in enumerate(others):
        own = lax.dynamic_update_slice(own, piece, ((j + 1) * chans, 0))

    def send(masks, far, own):
        return from_partner(own, near_mask), from_times(far), *[from_partner(own, m) for m in masks]

    pairs = [(low, high) for high in free_masks for low in free_masks if low < high]
    if len(pairs) <= MAX_BRANCHES:
        branches = [functools.partial(send, pair) for pair in pairs]
        near, far_more, low, high = lax.switch(branch.reshape(()), branches, far, own)
    else:
        sends = [functools.partial(from_partner, mask=mask) for mask in free_masks]
        low, high = (
            lax.switch(mask - free_masks[0], sends, own) for mask in free_masks_of(plan, far_mask)
        )
        near, far_more = send((), far, own)
    return correlate(plan, table_list, own, near, far, far_more, low, high, far_mask)


def solution(mesh):
    in_specs = (P("chan", "tm"), P(), P())
    out_specs = (P(("chan", "tm"), None, None), P(None, ("chan", "tm"), None, None))
    return jax.shard_map(
        on_device, mesh=mesh, in_specs=in_specs, out_specs=out_specs, check_vma=False
    )
```

```python
import functools
import math

import jax
import jax.numpy as jnp
import ml_dtypes
import numpy as np
from jax import lax
from jax.experimental import pallas as pl
from jax.experimental.pallas import tpu as pltpu
from jax.sharding import PartitionSpec as P

SEGS_DEV = 2
LAGS = 129
ROUNDS = 4
LANE = 128
MAX_BRANCHES = 128
OUT_GROUPS = 4
VMEM_LIMIT = 8 * 1024 * 1024
KERNEL_VMEM = 24 * 1024 * 1024
VMEM = pl.BlockSpec(memory_space=pltpu.VMEM)
SMEM = pl.BlockSpec(memory_space=pltpu.SMEM)
HBM = pl.BlockSpec(memory_space=pl.ANY)


def split_table(table):
    high = table.astype(ml_dtypes.bfloat16)
    low = (table - high.astype(np.float64)).astype(ml_dtypes.bfloat16)
    return np.concatenate([high, high, low], axis=0)


def tables(length):
    quarter = length // 4

    def packed(freqs, count):
        angle = 2.0 * math.pi / length * (np.arange(count)[:, None] * freqs[None, :] % length)
        return np.concatenate([np.cos(angle), -np.sin(angle)], axis=1)

    fours = 4 * np.arange(quarter // 2)
    odds = 2 * np.arange(quarter) + 1
    sum_table = packed(fours, quarter)
    sum_table[:, quarter // 2] = 1.0 - 2.0 * (np.arange(quarter) % 2)
    fold_tables = sum_table, packed(fours + 2, quarter), packed(odds, 2 * quarter)

    freqs = np.concatenate([fours, fours + 2, odds])[:, None]
    lag = (np.arange(LAGS) - LAGS // 2)[None, :]
    angle = 2.0 * math.pi / length * (lag * freqs % length)
    weight = np.where(freqs == 0, 1.0, 2.0) / length
    lag_cos = weight * np.cos(angle)
    lag_sin = weight * np.sin(angle)
    lag_sin[0] = (1.0 - 2.0 * (np.abs(lag[0]) % 2)) / length
    lag_table = np.zeros((length, 2 * LANE))
    lag_table[:, :LAGS] = np.concatenate([lag_cos, lag_sin], axis=0)
    return (*map(split_table, fold_tables), lag_table.astype(ml_dtypes.bfloat16))


def dot(left, right):
    return jnp.dot(left, right, preferred_element_type=jnp.float32)


def free_masks_of(plan, last_mask):
    masks = [plan[r] for r in range(ROUNDS)]
    free = [(mask != 1) & (mask != last_mask) for mask in masks]
    low = functools.reduce(
        jnp.minimum, [jnp.where(ok, mask, last_mask) for ok, mask in zip(free, masks)]
    )
    high = functools.reduce(jnp.maximum, [jnp.where(ok, mask, 0) for ok, mask in zip(free, masks)])
    return low, high


def prepare_kernel(last_mask, plan, taps, samples, *refs):
    tables_hbm, (branch, record, toep), refs = refs[:3], refs[3:6], refs[6:]
    tables_vmem, (own_sem, table_sems) = refs[:3], refs[3:]
    chans = samples.shape[0]
    copies = [pltpu.make_async_copy(samples, record.at[pl.ds(0, chans)], own_sem)]
    copies += [
        pltpu.make_async_copy(table, table_vmem, table_sems.at[i])
        for i, (table, table_vmem) in enumerate(zip(tables_hbm, tables_vmem))
    ]
    for copy in copies:
        copy.start()
    low, high = (mask - 2 for mask in free_masks_of(plan, last_mask))
    branch[0] = high * (high - 1) // 2 + low

    lane = lax.broadcasted_iota(jnp.int32, (1, 2 * LANE), 1)
    base = jnp.zeros((1, 2 * LANE), jnp.float32)
    for j in range(taps.shape[0]):
        base = jnp.where(lane == j, taps[j], base)
    base = jnp.broadcast_to(base, (2 * LANE, 2 * LANE))
    toeplitz = pltpu.roll(base, LANE, 1, stride=1, stride_axis=0)[:, :LANE]
    toep_hi = toeplitz.astype(jnp.bfloat16)
    toep[:, :LANE] = toep_hi
    toep[:, LANE:] = (toeplitz - toep_hi.astype(jnp.float32)).astype(jnp.bfloat16)
    for copy in copies:
        copy.wait()


def prepare(plan, fir_taps, samples, last_mask, parts):
    chans, width = samples.shape
    *table_list, lag_table = tables(width // SEGS_DEV)
    plan, fir_taps, samples, *table_list = (
        pltpu.with_memory_space_constraint(jnp.asarray(array), pltpu.HBM)
        for array in (plan, fir_taps, samples, *table_list)
    )
    branch, record, toep, *table_list = pl.pallas_call(
        functools.partial(prepare_kernel, last_mask),
        out_shape=(
            jax.ShapeDtypeStruct((1,), jnp.int32),
            pltpu.VMEM((parts * chans, width), jnp.bfloat16),
            pltpu.VMEM((2 * LANE, 2 * LANE), jnp.bfloat16),
            *[pltpu.VMEM(table.shape, jnp.bfloat16) for table in table_list],
        ),
        in_specs=[SMEM, SMEM] + [HBM] * (1 + len(table_list)),
        out_specs=(SMEM,) + (VMEM,) * (2 + len(table_list)),
        scratch_shapes=[
            pltpu.SemaphoreType.DMA,
            pltpu.SemaphoreType.DMA((len(table_list),)),
        ],
        compiler_params=pltpu.CompilerParams(vmem_limit_bytes=VMEM_LIMIT),
    )(plan, fir_taps, samples, *table_list)
    return branch, record, (toep, *table_list, jnp.asarray(lag_table))


def add_spectra(columns_of, place, parts, shape, first_row, toep, folds):
    chans, width = shape
    tiles = width // SEGS_DEV // LANE
    quarter = tiles // 4
    for piece in range(parts):
        tail = columns_of((piece + 1) % parts, width - LANE, width)
        has_before = jnp.where(lax.rem(place + parts - piece, parts) == 0, 0.0, 1.0)
        tail = (tail.astype(jnp.float32) * has_before).astype(jnp.bfloat16)
        windows = [jnp.concatenate([tail, columns_of(piece, 0, LANE)], axis=1)]
        windows += [
            columns_of(piece, LANE * (k - 1), LANE * (k + 1)) for k in range(1, width // LANE)
        ]
        both = dot(jnp.concatenate(windows, axis=0), toep[...])
        filtered = both[:, :LANE] + both[:, LANE:]
        for s in range(SEGS_DEV):
            row = first_row + (piece * SEGS_DEV + s) * chans
            for k in range(quarter):
                at = [(s * tiles + j * quarter + k) * chans for j in range(4)]
                x = [filtered[lo : lo + chans] for lo in at]
                even, later = x[0] + x[2], x[1] + x[3]
                sums, diffs, odds = folds
                for ref, tile, value in (
                    (sums, k, even + later),
                    (diffs, k, even - later),
                    (odds, k, x[0] - x[2]),
                    (odds, k + quarter, x[1] - x[3]),
                ):
                    high = value.astype(jnp.bfloat16)
                    low = (value - high.astype(jnp.float32)).astype(jnp.bfloat16)
                    for j, part in enumerate((high, low, high)):
                        at = ref.shape[1] // 3 * j + LANE * tile
                        ref[row : row + chans, at : at + LANE] = part


def whiten(folds, fold_tables, real_ref, imag_ref):
    products = [dot(fold[...], table[...]) for fold, table in zip(folds, fold_tables)]
    real, imag = (
        jnp.concatenate(
            [p[:, p.shape[1] // 2 * j : p.shape[1] // 2 * (j + 1)] for p in products], axis=1
        )
        for j in range(2)
    )
    real_sq = real * real
    imag_sq = imag * imag
    energy = real_sq + imag_sq
    freqs = real.shape[1] + 1
    level = 0.1 / freqs * jnp.sum(energy, axis=1, keepdims=True) + 1e-06
    first, rest = slice(0, LANE), slice(LANE, freqs - 1)
    edge = lax.broadcasted_iota(jnp.int32, real[:, first].shape, 1) == 0
    inv_real = lax.rsqrt(jnp.where(edge, real_sq[:, first], energy[:, first]) + level)
    inv_imag = jnp.where(edge, lax.rsqrt(imag_sq[:, first] + level), inv_real)
    inverse = lax.rsqrt(energy[:, rest] + level)
    for ref, value, inv in ((real_ref, real, inv_real), (imag_ref, imag, inv_imag)):
        for lanes, factor in ((first, inv), (rest, inverse)):
            whitened = (value[:, lanes] * factor).astype(jnp.bfloat16)
            ref[:, lanes] = whitened.astype(jnp.float32)


def cross_spectra(first, count, chans, segs, left_ref, real_ref, imag_ref, cross):
    rows, half = real_ref.shape
    rows_blk = segs * chans
    sets = rows // rows_blk

    @pl.loop(0, count)
    def _(i):
        a = first + i
        at = pl.multiple_of(a * sets * chans, sets * chans)
        for c in range(half // LANE):
            cols = slice(LANE * c, LANE * (c + 1))
            left = [
                jnp.broadcast_to(left_ref[a, j : j + 1, cols], (chans, LANE))
                for j in range(3 * segs)
            ]
            for q in range(sets):
                cos_part = sin_part = 0.0
                for s in range(segs):
                    row_b = slice(q * rows_blk + s * chans, q * rows_blk + (s + 1) * chans)
                    re_b, im_b = real_ref[row_b, cols], imag_ref[row_b, cols]
                    re_a, im_a, x_a = (left[segs * j + s] for j in range(3))
                    cos_part += re_a * re_b + im_a * im_b
                    sin_part += x_a * im_b - im_a * re_b
                at_q = pl.ds(at + q * chans, chans)
                cross[at_q, cols] = cos_part.astype(jnp.bfloat16)
                cross[at_q, half + LANE * c : half + LANE * (c + 1)] = sin_part.astype(jnp.bfloat16)


def spectra_scratch(sets, parts, chans, length, share):
    rows, half = sets * parts * SEGS_DEV * chans, length // 2
    return [
        pltpu.VMEM((rows, 3 * length // 4), jnp.bfloat16),
        pltpu.VMEM((rows, 3 * length // 4), jnp.bfloat16),
        pltpu.VMEM((rows, 3 * half), jnp.bfloat16),
        pltpu.VMEM((rows, half), jnp.float32),
        pltpu.VMEM((rows, half), jnp.float32),
        pltpu.VMEM((share * sets * chans, length), jnp.bfloat16),
    ]


def rows_of_block(block, chans):
    return lambda piece, lo, hi: block[piece * chans : (piece + 1) * chans, lo:hi]


def correlate_kernel(parts, last_mask, plan_hbm, toep, *refs):
    fold_tables, lag_hbm, refs = refs[:3], refs[3], refs[4:]
    own, far, near, low, high, refs = *refs[:5], refs[5:]
    far_more, (self_out, pair_out), refs = refs[: parts - 1], refs[parts - 1 : parts + 1], refs[parts + 1 :]
    plan, lag_table, arrived, far_arrived, left_ref, *refs = refs
    folds, (real_ref, imag_ref, cross, staged), refs = refs[:3], refs[3:7], refs[7:]
    plan_sem, lag_sem, sems, far_sems, out_sems = refs

    chans, width = far.shape
    half = real_ref.shape[1]
    share = left_ref.shape[0]
    segs = parts * SEGS_DEV
    sets = ROUNDS + 1
    place = lax.axis_index("tm")
    copies = [
        pltpu.make_async_copy(source, arrived.at[i], sems.at[i])
        for i, source in enumerate((near, low, high))
    ]
    far_copies = [
        pltpu.make_async_copy(source, far_arrived.at[i], far_sems.at[i])
        for i, source in enumerate(far_more)
    ]
    lag_copy = pltpu.make_async_copy(lag_hbm, lag_table, lag_sem)
    plan_copy = pltpu.make_async_copy(plan_hbm, plan, plan_sem)
    for copy in far_copies + copies + [lag_copy, plan_copy]:
        copy.start()

    def far_columns(piece, lo, hi):
        return far[:, lo:hi] if piece == 0 else far_arrived[piece - 1, :, lo:hi]

    blocks = [
        (rows_of_block(own, chans), []),
        (rows_of_block(arrived.at[0], chans), copies[:1]),
        (far_columns, far_copies),
        (rows_of_block(arrived.at[1], chans), copies[1:2]),
        (rows_of_block(arrived.at[2], chans), copies[2:]),
    ]
    for q in (0, 2, 1, 3, 4):
        columns_of, needs = blocks[q]
        for copy in needs:
            copy.wait()
        first_row = q * segs * chans
        add_spectra(columns_of, place, parts, far.shape, first_row, toep, folds)
    whiten(folds, fold_tables, real_ref, imag_ref)

    def picked(ref, s):
        value = ref[s * chans : s * chans + share, :]
        for owner in range(1, parts):
            at = s * chans + owner * share
            value = jnp.where(place == owner, ref[at : at + share, :], value)
        return value

    edge = lax.broadcasted_iota(jnp.int32, (share, half), 1) == 0
    for s in range(segs):
        real_s, imag_s = picked(real_ref, s), picked(imag_ref, s)
        lefts = (real_s, jnp.where(edge, 0.0, imag_s), jnp.where(edge, imag_s, real_s))
        for j, value in enumerate(lefts):
            for a in range(share):
                left_ref[a, segs * j + s : segs * j + s + 1, :] = value[a : a + 1]

    plan_copy.wait()
    low_mask, high_mask = free_masks_of(plan, last_mask)
    slots = [
        sum(jnp.where(plan[r] == mask, r, 0) for r in range(ROUNDS))
        for mask in (1, last_mask, low_mask, high_mask)
    ]
    outs = [self_out, *(pair_out.at[slot] for slot in slots)]
    lag_copy.wait()
    out_copies = []
    groups = OUT_GROUPS if share % OUT_GROUPS == 0 else 1
    count = share // groups
    for group in range(groups):
        first = group * count
        cross_spectra(first, count, chans, segs, left_ref, real_ref, imag_ref, cross)
        rows = slice(first * sets * chans, (first + count) * sets * chans)
        result = dot(cross[rows, :], lag_table[...])
        for i in range(count):
            for q in range(sets):
                at = (i * sets + q) * chans
                staged[q, first + i] = result[at : at + chans, :LAGS]
        for q, out in enumerate(outs):
            piece = pl.ds(first, count)
            sem = out_sems.at[group * sets + q]
            out_copies.append(pltpu.make_async_copy(staged.at[q, piece], out.at[piece], sem))
            out_copies[-1].start()
    for copy in out_copies:
        copy.wait()


def correlate(plan, table_list, own, near, far, far_more, low, high, last_mask):
    chans, width = far.shape
    parts = len(far_more) + 1
    share = chans // parts
    length = width // SEGS_DEV
    sets = ROUNDS + 1
    *table_list, lag_table = table_list
    plan, lag_table = (
        pltpu.with_memory_space_constraint(array, pltpu.HBM) for array in (plan, lag_table)
    )
    return pl.pallas_call(
        functools.partial(correlate_kernel, parts, last_mask),
        out_shape=(
            jax.ShapeDtypeStruct((share, chans, LAGS), jnp.float32),
            jax.ShapeDtypeStruct((ROUNDS, share, chans, LAGS), jnp.float32),
        ),
        in_specs=[HBM] + [VMEM] * len(table_list) + [HBM] + [VMEM] * 2 + [HBM] * (parts + 2),
        out_specs=(HBM, HBM),
        scratch_shapes=[
            pltpu.SMEM(plan.shape, jnp.int32),
            pltpu.VMEM(lag_table.shape, jnp.bfloat16),
            pltpu.VMEM((3, *own.shape), jnp.bfloat16),
            pltpu.VMEM((parts - 1, chans, width), jnp.bfloat16),
            pltpu.VMEM((share, 3 * parts * SEGS_DEV, length // 2), jnp.float32),
            *spectra_scratch(sets, parts, chans, length, share),
            pltpu.VMEM((sets, share, chans, LAGS), jnp.float32),
            pltpu.SemaphoreType.DMA,
            pltpu.SemaphoreType.DMA,
            pltpu.SemaphoreType.DMA((3,)),
            pltpu.SemaphoreType.DMA((parts - 1,)),
            pltpu.SemaphoreType.DMA((sets * OUT_GROUPS,)),
        ],
        compiler_params=pltpu.CompilerParams(vmem_limit_bytes=KERNEL_VMEM),
    )(plan, *table_list, lag_table, own, far, near, low, high, *far_more)


def from_partner(block, mask):
    chan_count = lax.axis_size("chan")
    return lax.ppermute(block, "chan", [(g, g ^ mask) for g in range(chan_count)])


def from_times(block):
    parts = lax.axis_size("tm")
    return [
        lax.ppermute(block, "tm", [(t, (t + j) % parts) for t in range(parts)])
        for j in range(1, parts)
    ]


def on_device(samples, fir_taps, plan):
    chan_count, parts = lax.axis_size("chan"), lax.axis_size("tm")
    chans = samples.shape[0]
    near_mask, far_mask = 1, chan_count - 1
    free_masks = range(2, far_mask)

    far = from_partner(samples, far_mask)
    others = from_times(samples)
    branch, own, table_list = prepare(plan, fir_taps, samples, far_mask, parts)
    for j, piece in enumerate(others):
        own = lax.dynamic_update_slice(own, piece, ((j + 1) * chans, 0))

    def send(masks, far, own):
        return from_partner(own, near_mask), from_times(far), *[from_partner(own, m) for m in masks]

    pairs = [(low, high) for high in free_masks for low in free_masks if low < high]
    if len(pairs) <= MAX_BRANCHES:
        branches = [functools.partial(send, pair) for pair in pairs]
        near, far_more, low, high = lax.switch(branch.reshape(()), branches, far, own)
    else:
        sends = [functools.partial(from_partner, mask=mask) for mask in free_masks]
        low, high = (
            lax.switch(mask - free_masks[0], sends, own) for mask in free_masks_of(plan, far_mask)
        )
        near, far_more = send((), far, own)
    return correlate(plan, table_list, own, near, far, far_more, low, high, far_mask)


def solution(mesh):
    in_specs = (P("chan", "tm"), P(), P())
    out_specs = (P(("chan", "tm"), None, None), P(None, ("chan", "tm"), None, None))
    return jax.shard_map(
        on_device, mesh=mesh, in_specs=in_specs, out_specs=out_specs, check_vma=False
    )
```

```python
import functools
import math

import jax
import jax.numpy as jnp
import ml_dtypes
import numpy as np
from jax import lax
from jax.experimental import pallas as pl
from jax.experimental.pallas import tpu as pltpu
from jax.sharding import PartitionSpec as P

SEGS_DEV = 2
LAGS = 129
ROUNDS = 4
LANE = 128
MAX_BRANCHES = 128
OUT_GROUPS = 4
VMEM_LIMIT = 8 * 1024 * 1024
KERNEL_VMEM = 24 * 1024 * 1024
VMEM = pl.BlockSpec(memory_space=pltpu.VMEM)
SMEM = pl.BlockSpec(memory_space=pltpu.SMEM)
HBM = pl.BlockSpec(memory_space=pl.ANY)


def split_table(table):
    high = table.astype(ml_dtypes.bfloat16)
    low = (table - high.astype(np.float64)).astype(ml_dtypes.bfloat16)
    return np.concatenate([high, high, low], axis=0)


def tables(length):
    quarter = length // 4

    def packed(freqs, count):
        angle = 2.0 * math.pi / length * (np.arange(count)[:, None] * freqs[None, :] % length)
        return np.concatenate([np.cos(angle), -np.sin(angle)], axis=1)

    fours = 4 * np.arange(quarter // 2)
    odds = 2 * np.arange(quarter) + 1
    sum_table = packed(fours, quarter)
    sum_table[:, quarter // 2] = 1.0 - 2.0 * (np.arange(quarter) % 2)
    fold_tables = sum_table, packed(fours + 2, quarter), packed(odds, 2 * quarter)

    freqs = np.concatenate([fours, fours + 2, odds])[:, None]
    lag = (np.arange(LAGS) - LAGS // 2)[None, :]
    angle = 2.0 * math.pi / length * (lag * freqs % length)
    weight = np.where(freqs == 0, 1.0, 2.0) / length
    lag_cos = weight * np.cos(angle)
    lag_sin = weight * np.sin(angle)
    lag_sin[0] = (1.0 - 2.0 * (np.abs(lag[0]) % 2)) / length
    lag_table = np.zeros((length, 2 * LANE))
    lag_table[:, :LAGS] = np.concatenate([lag_cos, lag_sin], axis=0)
    return (*map(split_table, fold_tables), lag_table.astype(ml_dtypes.bfloat16))


def dot(left, right):
    return jnp.dot(left, right, preferred_element_type=jnp.float32)


def free_masks_of(plan, last_mask):
    masks = [plan[r] for r in range(ROUNDS)]
    free = [(mask != 1) & (mask != last_mask) for mask in masks]
    low = functools.reduce(
        jnp.minimum, [jnp.where(ok, mask, last_mask) for ok, mask in zip(free, masks)]
    )
    high = functools.reduce(jnp.maximum, [jnp.where(ok, mask, 0) for ok, mask in zip(free, masks)])
    return low, high


def prepare_kernel(last_mask, plan, taps, samples, *refs):
    tables_hbm, (branch, record, toep), refs = refs[:3], refs[3:6], refs[6:]
    tables_vmem, (own_sem, table_sems) = refs[:3], refs[3:]
    chans = samples.shape[0]
    copies = [pltpu.make_async_copy(samples, record.at[pl.ds(0, chans)], own_sem)]
    copies += [
        pltpu.make_async_copy(table, table_vmem, table_sems.at[i])
        for i, (table, table_vmem) in enumerate(zip(tables_hbm, tables_vmem))
    ]
    for copy in copies:
        copy.start()
    low, high = (mask - 2 for mask in free_masks_of(plan, last_mask))
    branch[0] = high * (high - 1) // 2 + low

    lane = lax.broadcasted_iota(jnp.int32, (1, 2 * LANE), 1)
    base = jnp.zeros((1, 2 * LANE), jnp.float32)
    for j in range(taps.shape[0]):
        base = jnp.where(lane == j, taps[j], base)
    base = jnp.broadcast_to(base, (2 * LANE, 2 * LANE))
    toeplitz = pltpu.roll(base, LANE, 1, stride=1, stride_axis=0)[:, :LANE]
    toep_hi = toeplitz.astype(jnp.bfloat16)
    toep[:, :LANE] = toep_hi
    toep[:, LANE:] = (toeplitz - toep_hi.astype(jnp.float32)).astype(jnp.bfloat16)
    for copy in copies:
        copy.wait()


def prepare(plan, fir_taps, samples, last_mask, parts):
    chans, width = samples.shape
    *table_list, lag_table = tables(width // SEGS_DEV)
    plan, fir_taps, samples, *table_list = (
        pltpu.with_memory_space_constraint(jnp.asarray(array), pltpu.HBM)
        for array in (plan, fir_taps, samples, *table_list)
    )
    branch, record, toep, *table_list = pl.pallas_call(
        functools.partial(prepare_kernel, last_mask),
        out_shape=(
            jax.ShapeDtypeStruct((1,), jnp.int32),
            pltpu.VMEM((parts * chans, width), jnp.bfloat16),
            pltpu.VMEM((2 * LANE, 2 * LANE), jnp.bfloat16),
            *[pltpu.VMEM(table.shape, jnp.bfloat16) for table in table_list],
        ),
        in_specs=[SMEM, SMEM] + [HBM] * (1 + len(table_list)),
        out_specs=(SMEM,) + (VMEM,) * (2 + len(table_list)),
        scratch_shapes=[
            pltpu.SemaphoreType.DMA,
            pltpu.SemaphoreType.DMA((len(table_list),)),
        ],
        compiler_params=pltpu.CompilerParams(vmem_limit_bytes=VMEM_LIMIT),
    )(plan, fir_taps, samples, *table_list)
    return branch, record, (toep, *table_list, jnp.asarray(lag_table))


def add_spectra(columns_of, place, parts, shape, first_row, toep, folds):
    chans, width = shape
    tiles = width // SEGS_DEV // LANE
    quarter = tiles // 4
    for piece in range(parts):
        tail = columns_of((piece + 1) % parts, width - LANE, width)
        has_before = jnp.where(lax.rem(place + parts - piece, parts) == 0, 0.0, 1.0)
        tail = (tail.astype(jnp.float32) * has_before).astype(jnp.bfloat16)
        windows = [jnp.concatenate([tail, columns_of(piece, 0, LANE)], axis=1)]
        windows += [
            columns_of(piece, LANE * (k - 1), LANE * (k + 1)) for k in range(1, width // LANE)
        ]
        both = dot(jnp.concatenate(windows, axis=0), toep[...])
        filtered = both[:, :LANE] + both[:, LANE:]
        for s in range(SEGS_DEV):
            row = first_row + (piece * SEGS_DEV + s) * chans
            for k in range(quarter):
                at = [(s * tiles + j * quarter + k) * chans for j in range(4)]
                x = [filtered[lo : lo + chans] for lo in at]
                even, later = x[0] + x[2], x[1] + x[3]
                sums, diffs, odds = folds
                for ref, tile, value in (
                    (sums, k, even + later),
                    (diffs, k, even - later),
                    (odds, k, x[0] - x[2]),
                    (odds, k + quarter, x[1] - x[3]),
                ):
                    high = value.astype(jnp.bfloat16)
                    low = (value - high.astype(jnp.float32)).astype(jnp.bfloat16)
                    for j, part in enumerate((high, low, high)):
                        at = ref.shape[1] // 3 * j + LANE * tile
                        ref[row : row + chans, at : at + LANE] = part


def whiten(folds, fold_tables, real_ref, imag_ref):
    products = [dot(fold[...], table[...]) for fold, table in zip(folds, fold_tables)]
    real, imag = (
        jnp.concatenate(
            [p[:, p.shape[1] // 2 * j : p.shape[1] // 2 * (j + 1)] for p in products], axis=1
        )
        for j in range(2)
    )
    real_sq = real * real
    imag_sq = imag * imag
    energy = real_sq + imag_sq
    freqs = real.shape[1] + 1
    level = 0.1 / freqs * jnp.sum(energy, axis=1, keepdims=True) + 1e-06
    first, rest = slice(0, LANE), slice(LANE, freqs - 1)
    edge = lax.broadcasted_iota(jnp.int32, real[:, first].shape, 1) == 0
    inv_real = lax.rsqrt(jnp.where(edge, real_sq[:, first], energy[:, first]) + level)
    inv_imag = jnp.where(edge, lax.rsqrt(imag_sq[:, first] + level), inv_real)
    inverse = lax.rsqrt(energy[:, rest] + level)
    for ref, value, inv in ((real_ref, real, inv_real), (imag_ref, imag, inv_imag)):
        for lanes, factor in ((first, inv), (rest, inverse)):
            whitened = (value[:, lanes] * factor).astype(jnp.bfloat16)
            ref[:, lanes] = whitened.astype(jnp.float32)


def cross_spectra(first, count, chans, segs, left_ref, real_ref, imag_ref, cross):
    rows, half = real_ref.shape
    rows_blk = segs * chans
    sets = rows // rows_blk

    @pl.loop(0, count)
    def _(i):
        a = first + i
        at = pl.multiple_of(a * sets * chans, sets * chans)
        for c in range(half // LANE):
            cols = slice(LANE * c, LANE * (c + 1))
            left = [
                jnp.broadcast_to(left_ref[a, j : j + 1, cols], (chans, LANE))
                for j in range(3 * segs)
            ]
            for q in range(sets):
                cos_part = sin_part = 0.0
                for s in range(segs):
                    row_b = slice(q * rows_blk + s * chans, q * rows_blk + (s + 1) * chans)
                    re_b, im_b = real_ref[row_b, cols], imag_ref[row_b, cols]
                    re_a, im_a, x_a = (left[segs * j + s] for j in range(3))
                    cos_part += re_a * re_b + im_a * im_b
                    sin_part += x_a * im_b - im_a * re_b
                at_q = pl.ds(at + q * chans, chans)
                cross[at_q, cols] = cos_part.astype(jnp.bfloat16)
                cross[at_q, half + LANE * c : half + LANE * (c + 1)] = sin_part.astype(jnp.bfloat16)


def spectra_scratch(sets, parts, chans, length, share):
    rows, half = sets * parts * SEGS_DEV * chans, length // 2
    return [
        pltpu.VMEM((rows, 3 * length // 4), jnp.bfloat16),
        pltpu.VMEM((rows, 3 * length // 4), jnp.bfloat16),
        pltpu.VMEM((rows, 3 * half), jnp.bfloat16),
        pltpu.VMEM((rows, half), jnp.float32),
        pltpu.VMEM((rows, half), jnp.float32),
        pltpu.VMEM((share * sets * chans, length), jnp.bfloat16),
    ]


def rows_of_block(block, chans):
    return lambda piece, lo, hi: block[piece * chans : (piece + 1) * chans, lo:hi]


def correlate_kernel(parts, last_mask, plan_hbm, toep, *refs):
    fold_tables, lag_hbm, refs = refs[:3], refs[3], refs[4:]
    own, far, near, low, high, refs = *refs[:5], refs[5:]
    far_more, (self_out, pair_out), refs = refs[: parts - 1], refs[parts - 1 : parts + 1], refs[parts + 1 :]
    plan, lag_table, arrived, left_ref, *refs = refs
    folds, (real_ref, imag_ref, cross, staged), refs = refs[:3], refs[3:7], refs[7:]
    plan_sem, lag_sem, sems, out_sems = refs

    chans, width = far.shape
    half = real_ref.shape[1]
    share = left_ref.shape[0]
    segs = parts * SEGS_DEV
    sets = ROUNDS + 1
    place = lax.axis_index("tm")
    copies = [
        pltpu.make_async_copy(source, arrived.at[i], sems.at[i])
        for i, source in enumerate((near, low, high))
    ]
    lag_copy = pltpu.make_async_copy(lag_hbm, lag_table, lag_sem)
    plan_copy = pltpu.make_async_copy(plan_hbm, plan, plan_sem)
    for copy in copies + [lag_copy, plan_copy]:
        copy.start()

    def far_columns(piece, lo, hi):
        return (far, *far_more)[piece][:, lo:hi]

    blocks = [
        (rows_of_block(own, chans), []),
        (rows_of_block(arrived.at[0], chans), copies[:1]),
        (far_columns, []),
        (rows_of_block(arrived.at[1], chans), copies[1:2]),
        (rows_of_block(arrived.at[2], chans), copies[2:]),
    ]
    for q in (0, 2, 1, 3, 4):
        columns_of, needs = blocks[q]
        for copy in needs:
            copy.wait()
        first_row = q * segs * chans
        add_spectra(columns_of, place, parts, far.shape, first_row, toep, folds)
    whiten(folds, fold_tables, real_ref, imag_ref)

    def picked(ref, s):
        value = ref[s * chans : s * chans + share, :]
        for owner in range(1, parts):
            at = s * chans + owner * share
            value = jnp.where(place == owner, ref[at : at + share, :], value)
        return value

    edge = lax.broadcasted_iota(jnp.int32, (share, half), 1) == 0
    for s in range(segs):
        real_s, imag_s = picked(real_ref, s), picked(imag_ref, s)
        lefts = (real_s, jnp.where(edge, 0.0, imag_s), jnp.where(edge, imag_s, real_s))
        for j, value in enumerate(lefts):
            for a in range(share):
                left_ref[a, segs * j + s : segs * j + s + 1, :] = value[a : a + 1]

    plan_copy.wait()
    low_mask, high_mask = free_masks_of(plan, last_mask)
    slots = [
        sum(jnp.where(plan[r] == mask, r, 0) for r in range(ROUNDS))
        for mask in (1, last_mask, low_mask, high_mask)
    ]
    outs = [self_out, *(pair_out.at[slot] for slot in slots)]
    lag_copy.wait()
    out_copies = []
    groups = OUT_GROUPS if share % OUT_GROUPS == 0 else 1
    count = share // groups
    for group in range(groups):
        first = group * count
        cross_spectra(first, count, chans, segs, left_ref, real_ref, imag_ref, cross)
        rows = slice(first * sets * chans, (first + count) * sets * chans)
        result = dot(cross[rows, :], lag_table[...])
        for i in range(count):
            for q in range(sets):
                at = (i * sets + q) * chans
                staged[q, first + i] = result[at : at + chans, :LAGS]
        for q, out in enumerate(outs):
            piece = pl.ds(first, count)
            sem = out_sems.at[group * sets + q]
            out_copies.append(pltpu.make_async_copy(staged.at[q, piece], out.at[piece], sem))
            out_copies[-1].start()
    for copy in out_copies:
        copy.wait()


def correlate(plan, table_list, own, near, far, far_more, low, high, last_mask):
    chans, width = far.shape
    parts = len(far_more) + 1
    share = chans // parts
    length = width // SEGS_DEV
    sets = ROUNDS + 1
    *table_list, lag_table = table_list
    plan, lag_table = (
        pltpu.with_memory_space_constraint(array, pltpu.HBM) for array in (plan, lag_table)
    )
    return pl.pallas_call(
        functools.partial(correlate_kernel, parts, last_mask),
        out_shape=(
            jax.ShapeDtypeStruct((share, chans, LAGS), jnp.float32),
            jax.ShapeDtypeStruct((ROUNDS, share, chans, LAGS), jnp.float32),
        ),
        in_specs=[HBM] + [VMEM] * len(table_list) + [HBM] + [VMEM] * 2 + [HBM] * 3 + [VMEM] * (parts - 1),
        out_specs=(HBM, HBM),
        scratch_shapes=[
            pltpu.SMEM(plan.shape, jnp.int32),
            pltpu.VMEM(lag_table.shape, jnp.bfloat16),
            pltpu.VMEM((3, *own.shape), jnp.bfloat16),
            pltpu.VMEM((share, 3 * parts * SEGS_DEV, length // 2), jnp.float32),
            *spectra_scratch(sets, parts, chans, length, share),
            pltpu.VMEM((sets, share, chans, LAGS), jnp.float32),
            pltpu.SemaphoreType.DMA,
            pltpu.SemaphoreType.DMA,
            pltpu.SemaphoreType.DMA((3,)),
            pltpu.SemaphoreType.DMA((sets * OUT_GROUPS,)),
        ],
        compiler_params=pltpu.CompilerParams(vmem_limit_bytes=KERNEL_VMEM),
    )(plan, *table_list, lag_table, own, far, near, low, high, *far_more)


def from_partner(block, mask):
    chan_count = lax.axis_size("chan")
    return lax.ppermute(block, "chan", [(g, g ^ mask) for g in range(chan_count)])


def from_times(block, mask=0):
    chan_count, parts = lax.axis_size("chan"), lax.axis_size("tm")
    routes = [
        [
            (g * parts + t, (g ^ mask) * parts + (t + j) % parts)
            for g in range(chan_count)
            for t in range(parts)
        ]
        for j in range(1, parts)
    ]
    return [lax.ppermute(block, ("chan", "tm"), route) for route in routes]


def on_device(samples, fir_taps, plan):
    chan_count, parts = lax.axis_size("chan"), lax.axis_size("tm")
    chans = samples.shape[0]
    near_mask, far_mask = 1, chan_count - 1
    free_masks = range(2, far_mask)

    far, far_more = from_partner(samples, far_mask), from_times(samples, far_mask)
    others = from_times(samples)
    branch, own, table_list = prepare(plan, fir_taps, samples, far_mask, parts)
    for j, piece in enumerate(others):
        own = lax.dynamic_update_slice(own, piece, ((j + 1) * chans, 0))

    def send(masks, own):
        return [from_partner(own, mask) for mask in (near_mask, *masks)]

    pairs = [(low, high) for high in free_masks for low in free_masks if low < high]
    if len(pairs) <= MAX_BRANCHES:
        branches = [functools.partial(send, pair) for pair in pairs]
        near, low, high = lax.switch(branch.reshape(()), branches, own)
    else:
        sends = [functools.partial(from_partner, mask=mask) for mask in free_masks]
        low, high = (
            lax.switch(mask - free_masks[0], sends, own) for mask in free_masks_of(plan, far_mask)
        )
        (near,) = send((), own)
    return correlate(plan, table_list, own, near, far, far_more, low, high, far_mask)


def solution(mesh):
    in_specs = (P("chan", "tm"), P(), P())
    out_specs = (P(("chan", "tm"), None, None), P(None, ("chan", "tm"), None, None))
    return jax.shard_map(
        on_device, mesh=mesh, in_specs=in_specs, out_specs=out_specs, check_vma=False
    )
```

```python
import functools
import math

import jax
import jax.numpy as jnp
import ml_dtypes
import numpy as np
from jax import lax
from jax.experimental import pallas as pl
from jax.experimental.pallas import tpu as pltpu
from jax.sharding import PartitionSpec as P

SEGS_DEV = 2
LAGS = 129
ROUNDS = 4
LANE = 128
MAX_BRANCHES = 128
OUT_GROUPS = 4
VMEM_LIMIT = 8 * 1024 * 1024
KERNEL_VMEM = 24 * 1024 * 1024
VMEM = pl.BlockSpec(memory_space=pltpu.VMEM)
SMEM = pl.BlockSpec(memory_space=pltpu.SMEM)
HBM = pl.BlockSpec(memory_space=pl.ANY)


def split_table(table):
    high = table.astype(ml_dtypes.bfloat16)
    low = (table - high.astype(np.float64)).astype(ml_dtypes.bfloat16)
    return np.concatenate([high, high, low], axis=0)


def tables(length):
    quarter = length // 4

    def packed(freqs, count):
        angle = 2.0 * math.pi / length * (np.arange(count)[:, None] * freqs[None, :] % length)
        return np.concatenate([np.cos(angle), -np.sin(angle)], axis=1)

    fours = 4 * np.arange(quarter // 2)
    odds = 2 * np.arange(quarter) + 1
    sum_table = packed(fours, quarter)
    sum_table[:, quarter // 2] = 1.0 - 2.0 * (np.arange(quarter) % 2)
    fold_tables = sum_table, packed(fours + 2, quarter), packed(odds, 2 * quarter)

    freqs = np.concatenate([fours, fours + 2, odds])[:, None]
    lag = (np.arange(LAGS) - LAGS // 2)[None, :]
    angle = 2.0 * math.pi / length * (lag * freqs % length)
    weight = np.where(freqs == 0, 1.0, 2.0) / length
    lag_cos = weight * np.cos(angle)
    lag_sin = weight * np.sin(angle)
    lag_sin[0] = (1.0 - 2.0 * (np.abs(lag[0]) % 2)) / length
    lag_table = np.zeros((length, 2 * LANE))
    lag_table[:, :LAGS] = np.concatenate([lag_cos, lag_sin], axis=0)
    return (*map(split_table, fold_tables), lag_table.astype(ml_dtypes.bfloat16))


def dot(left, right):
    return jnp.dot(left, right, preferred_element_type=jnp.float32)


def free_masks_of(plan, last_mask):
    masks = [plan[r] for r in range(ROUNDS)]
    free = [(mask != 1) & (mask != last_mask) for mask in masks]
    low = functools.reduce(
        jnp.minimum, [jnp.where(ok, mask, last_mask) for ok, mask in zip(free, masks)]
    )
    high = functools.reduce(jnp.maximum, [jnp.where(ok, mask, 0) for ok, mask in zip(free, masks)])
    return low, high


def prepare_kernel(last_mask, plan, taps, samples, *refs):
    tables_hbm, (branch, record, toep), refs = refs[:3], refs[3:6], refs[6:]
    tables_vmem, (own_sem, table_sems) = refs[:3], refs[3:]
    chans = samples.shape[0]
    copies = [pltpu.make_async_copy(samples, record.at[pl.ds(0, chans)], own_sem)]
    copies += [
        pltpu.make_async_copy(table, table_vmem, table_sems.at[i])
        for i, (table, table_vmem) in enumerate(zip(tables_hbm, tables_vmem))
    ]
    for copy in copies:
        copy.start()
    low, high = (mask - 2 for mask in free_masks_of(plan, last_mask))
    branch[0] = high * (high - 1) // 2 + low

    lane = lax.broadcasted_iota(jnp.int32, (1, 2 * LANE), 1)
    base = jnp.zeros((1, 2 * LANE), jnp.float32)
    for j in range(taps.shape[0]):
        base = jnp.where(lane == j, taps[j], base)
    base = jnp.broadcast_to(base, (2 * LANE, 2 * LANE))
    toeplitz = pltpu.roll(base, LANE, 1, stride=1, stride_axis=0)[:, :LANE]
    toep_hi = toeplitz.astype(jnp.bfloat16)
    toep[:, :LANE] = toep_hi
    toep[:, LANE:] = (toeplitz - toep_hi.astype(jnp.float32)).astype(jnp.bfloat16)
    for copy in copies:
        copy.wait()


def prepare(plan, fir_taps, samples, last_mask, parts):
    chans, width = samples.shape
    *table_list, lag_table = tables(width // SEGS_DEV)
    plan, fir_taps, samples, *table_list = (
        pltpu.with_memory_space_constraint(jnp.asarray(array), pltpu.HBM)
        for array in (plan, fir_taps, samples, *table_list)
    )
    branch, record, toep, *table_list = pl.pallas_call(
        functools.partial(prepare_kernel, last_mask),
        out_shape=(
            jax.ShapeDtypeStruct((1,), jnp.int32),
            pltpu.VMEM((parts * chans, width), jnp.bfloat16),
            pltpu.VMEM((2 * LANE, 2 * LANE), jnp.bfloat16),
            *[pltpu.VMEM(table.shape, jnp.bfloat16) for table in table_list],
        ),
        in_specs=[SMEM, SMEM] + [HBM] * (1 + len(table_list)),
        out_specs=(SMEM,) + (VMEM,) * (2 + len(table_list)),
        scratch_shapes=[
            pltpu.SemaphoreType.DMA,
            pltpu.SemaphoreType.DMA((len(table_list),)),
        ],
        compiler_params=pltpu.CompilerParams(vmem_limit_bytes=VMEM_LIMIT),
    )(plan, fir_taps, samples, *table_list)
    return branch, record, (toep, *table_list, jnp.asarray(lag_table))


def add_spectra(columns_of, place, parts, shape, first_row, toep, folds):
    chans, width = shape
    tiles = width // SEGS_DEV // LANE
    quarter = tiles // 4
    for piece in range(parts):
        tail = columns_of((piece + 1) % parts, width - LANE, width)
        has_before = jnp.where(lax.rem(place + parts - piece, parts) == 0, 0.0, 1.0)
        tail = (tail.astype(jnp.float32) * has_before).astype(jnp.bfloat16)
        windows = [jnp.concatenate([tail, columns_of(piece, 0, LANE)], axis=1)]
        windows += [
            columns_of(piece, LANE * (k - 1), LANE * (k + 1)) for k in range(1, width // LANE)
        ]
        both = dot(jnp.concatenate(windows, axis=0), toep[...])
        filtered = both[:, :LANE] + both[:, LANE:]
        for s in range(SEGS_DEV):
            row = first_row + (piece * SEGS_DEV + s) * chans
            for k in range(quarter):
                at = [(s * tiles + j * quarter + k) * chans for j in range(4)]
                x = [filtered[lo : lo + chans] for lo in at]
                even, later = x[0] + x[2], x[1] + x[3]
                sums, diffs, odds = folds
                for ref, tile, value in (
                    (sums, k, even + later),
                    (diffs, k, even - later),
                    (odds, k, x[0] - x[2]),
                    (odds, k + quarter, x[1] - x[3]),
                ):
                    high = value.astype(jnp.bfloat16)
                    low = (value - high.astype(jnp.float32)).astype(jnp.bfloat16)
                    for j, part in enumerate((high, low, high)):
                        at = ref.shape[1] // 3 * j + LANE * tile
                        ref[row : row + chans, at : at + LANE] = part


def whiten(folds, fold_tables, real_ref, imag_ref):
    products = [dot(fold[...], table[...]) for fold, table in zip(folds, fold_tables)]
    real, imag = (
        jnp.concatenate(
            [p[:, p.shape[1] // 2 * j : p.shape[1] // 2 * (j + 1)] for p in products], axis=1
        )
        for j in range(2)
    )
    real_sq = real * real
    imag_sq = imag * imag
    energy = real_sq + imag_sq
    freqs = real.shape[1] + 1
    level = 0.1 / freqs * jnp.sum(energy, axis=1, keepdims=True) + 1e-06
    first, rest = slice(0, LANE), slice(LANE, freqs - 1)
    edge = lax.broadcasted_iota(jnp.int32, real[:, first].shape, 1) == 0
    inv_real = lax.rsqrt(jnp.where(edge, real_sq[:, first], energy[:, first]) + level)
    inv_imag = jnp.where(edge, lax.rsqrt(imag_sq[:, first] + level), inv_real)
    inverse = lax.rsqrt(energy[:, rest] + level)
    for ref, value, inv in ((real_ref, real, inv_real), (imag_ref, imag, inv_imag)):
        for lanes, factor in ((first, inv), (rest, inverse)):
            whitened = (value[:, lanes] * factor).astype(jnp.bfloat16)
            ref[:, lanes] = whitened.astype(jnp.float32)


def cross_spectra(rows_a, chans, segs, left_ref, real_ref, imag_ref, cross):
    rows, half = real_ref.shape
    rows_blk = segs * chans
    sets = rows // rows_blk
    for i, a in enumerate(rows_a):
        for c in range(half // LANE):
            cols = slice(LANE * c, LANE * (c + 1))
            left = [
                jnp.broadcast_to(left_ref[a, j : j + 1, cols], (chans, LANE))
                for j in range(3 * segs)
            ]
            for q in range(sets):
                cos_part = sin_part = 0.0
                for s in range(segs):
                    row_b = slice(q * rows_blk + s * chans, q * rows_blk + (s + 1) * chans)
                    re_b, im_b = real_ref[row_b, cols], imag_ref[row_b, cols]
                    re_a, im_a, x_a = (left[segs * j + s] for j in range(3))
                    cos_part += re_a * re_b + im_a * im_b
                    sin_part += x_a * im_b - im_a * re_b
                at_q = slice((i * sets + q) * chans, (i * sets + q + 1) * chans)
                cross[at_q, cols] = cos_part.astype(jnp.bfloat16)
                cross[at_q, half + LANE * c : half + LANE * (c + 1)] = sin_part.astype(jnp.bfloat16)


def groups_of(share):
    return OUT_GROUPS if share % OUT_GROUPS == 0 else 1


def spectra_scratch(sets, parts, chans, length, share):
    rows, half = sets * parts * SEGS_DEV * chans, length // 2
    return [
        pltpu.VMEM((rows, 3 * length // 4), jnp.bfloat16),
        pltpu.VMEM((rows, 3 * length // 4), jnp.bfloat16),
        pltpu.VMEM((rows, 3 * half), jnp.bfloat16),
        pltpu.VMEM((rows, half), jnp.float32),
        pltpu.VMEM((rows, half), jnp.float32),
        *[
            pltpu.VMEM((share // groups_of(share) * sets * chans, length), jnp.bfloat16)
            for _ in range(groups_of(share))
        ],
    ]


def rows_of_block(block, chans):
    return lambda piece, lo, hi: block[piece * chans : (piece + 1) * chans, lo:hi]


def correlate_kernel(parts, last_mask, plan_hbm, toep, *refs):
    fold_tables, lag_hbm, refs = refs[:3], refs[3], refs[4:]
    own, far, near, low, high, refs = *refs[:5], refs[5:]
    far_more, (self_out, pair_out), refs = refs[: parts - 1], refs[parts - 1 : parts + 1], refs[parts + 1 :]
    plan, lag_table, arrived, far_arrived, left_ref, *refs = refs
    groups = groups_of(left_ref.shape[0])
    folds, (real_ref, imag_ref), refs = refs[:3], refs[3:5], refs[5:]
    crosses, staged, refs = refs[:groups], refs[groups], refs[groups + 1 :]
    plan_sem, lag_sem, sems, far_sems, out_sems = refs

    chans, width = far.shape
    half = real_ref.shape[1]
    share = left_ref.shape[0]
    segs = parts * SEGS_DEV
    sets = ROUNDS + 1
    place = lax.axis_index("tm")
    copies = [
        pltpu.make_async_copy(source, arrived.at[i], sems.at[i])
        for i, source in enumerate((near, low, high))
    ]
    far_copies = [
        pltpu.make_async_copy(source, far_arrived.at[i], far_sems.at[i])
        for i, source in enumerate(far_more)
    ]
    lag_copy = pltpu.make_async_copy(lag_hbm, lag_table, lag_sem)
    plan_copy = pltpu.make_async_copy(plan_hbm, plan, plan_sem)
    for copy in far_copies + copies + [lag_copy, plan_copy]:
        copy.start()

    def far_columns(piece, lo, hi):
        return far[:, lo:hi] if piece == 0 else far_arrived[piece - 1, :, lo:hi]

    blocks = [
        (rows_of_block(own, chans), []),
        (rows_of_block(arrived.at[0], chans), copies[:1]),
        (far_columns, far_copies),
        (rows_of_block(arrived.at[1], chans), copies[1:2]),
        (rows_of_block(arrived.at[2], chans), copies[2:]),
    ]
    for q in (0, 2, 1, 3, 4):
        columns_of, needs = blocks[q]
        for copy in needs:
            copy.wait()
        first_row = q * segs * chans
        add_spectra(columns_of, place, parts, far.shape, first_row, toep, folds)
    whiten(folds, fold_tables, real_ref, imag_ref)

    def picked(ref, s):
        value = ref[s * chans : s * chans + share, :]
        for owner in range(1, parts):
            at = s * chans + owner * share
            value = jnp.where(place == owner, ref[at : at + share, :], value)
        return value

    edge = lax.broadcasted_iota(jnp.int32, (share, half), 1) == 0
    for s in range(segs):
        real_s, imag_s = picked(real_ref, s), picked(imag_ref, s)
        lefts = (real_s, jnp.where(edge, 0.0, imag_s), jnp.where(edge, imag_s, real_s))
        for j, value in enumerate(lefts):
            for a in range(share):
                left_ref[a, segs * j + s : segs * j + s + 1, :] = value[a : a + 1]

    plan_copy.wait()
    low_mask, high_mask = free_masks_of(plan, last_mask)
    slots = [
        sum(jnp.where(plan[r] == mask, r, 0) for r in range(ROUNDS))
        for mask in (1, last_mask, low_mask, high_mask)
    ]
    outs = [self_out, *(pair_out.at[slot] for slot in slots)]
    lag_copy.wait()
    out_copies = []
    count = share // groups
    for group in range(groups + 1):
        if group < groups:
            rows_a = range(group * count, (group + 1) * count)
            cross_spectra(rows_a, chans, segs, left_ref, real_ref, imag_ref, crosses[group])
        if group == 0:
            continue
        first = (group - 1) * count
        result = dot(crosses[group - 1][...], lag_table[...])
        for i in range(count):
            for q in range(sets):
                at = (i * sets + q) * chans
                staged[q, first + i] = result[at : at + chans, :LAGS]
        for q, out in enumerate(outs):
            piece = pl.ds(first, count)
            sem = out_sems.at[first // count * sets + q]
            out_copies.append(pltpu.make_async_copy(staged.at[q, piece], out.at[piece], sem))
            out_copies[-1].start()
    for copy in out_copies:
        copy.wait()


def correlate(plan, table_list, own, near, far, far_more, low, high, last_mask):
    chans, width = far.shape
    parts = len(far_more) + 1
    share = chans // parts
    length = width // SEGS_DEV
    sets = ROUNDS + 1
    *table_list, lag_table = table_list
    plan, lag_table = (
        pltpu.with_memory_space_constraint(array, pltpu.HBM) for array in (plan, lag_table)
    )
    return pl.pallas_call(
        functools.partial(correlate_kernel, parts, last_mask),
        out_shape=(
            jax.ShapeDtypeStruct((share, chans, LAGS), jnp.float32),
            jax.ShapeDtypeStruct((ROUNDS, share, chans, LAGS), jnp.float32),
        ),
        in_specs=[HBM] + [VMEM] * len(table_list) + [HBM] + [VMEM] * 2 + [HBM] * (parts + 2),
        out_specs=(HBM, HBM),
        scratch_shapes=[
            pltpu.SMEM(plan.shape, jnp.int32),
            pltpu.VMEM(lag_table.shape, jnp.bfloat16),
            pltpu.VMEM((3, *own.shape), jnp.bfloat16),
            pltpu.VMEM((parts - 1, chans, width), jnp.bfloat16),
            pltpu.VMEM((share, 3 * parts * SEGS_DEV, length // 2), jnp.float32),
            *spectra_scratch(sets, parts, chans, length, share),
            pltpu.VMEM((sets, share, chans, LAGS), jnp.float32),
            pltpu.SemaphoreType.DMA,
            pltpu.SemaphoreType.DMA,
            pltpu.SemaphoreType.DMA((3,)),
            pltpu.SemaphoreType.DMA((parts - 1,)),
            pltpu.SemaphoreType.DMA((sets * OUT_GROUPS,)),
        ],
        compiler_params=pltpu.CompilerParams(vmem_limit_bytes=KERNEL_VMEM),
    )(plan, *table_list, lag_table, own, far, near, low, high, *far_more)


def from_partner(block, mask):
    chan_count = lax.axis_size("chan")
    return lax.ppermute(block, "chan", [(g, g ^ mask) for g in range(chan_count)])


def from_times(block):
    parts = lax.axis_size("tm")
    return [
        lax.ppermute(block, "tm", [(t, (t + j) % parts) for t in range(parts)])
        for j in range(1, parts)
    ]


def on_device(samples, fir_taps, plan):
    chan_count, parts = lax.axis_size("chan"), lax.axis_size("tm")
    chans = samples.shape[0]
    near_mask, far_mask = 1, chan_count - 1
    free_masks = range(2, far_mask)

    far = from_partner(samples, far_mask)
    others = from_times(samples)
    branch, own, table_list = prepare(plan, fir_taps, samples, far_mask, parts)
    for j, piece in enumerate(others):
        own = lax.dynamic_update_slice(own, piece, ((j + 1) * chans, 0))

    def send(masks, far, own):
        return from_partner(own, near_mask), from_times(far), *[from_partner(own, m) for m in masks]

    pairs = [(low, high) for high in free_masks for low in free_masks if low < high]
    if len(pairs) <= MAX_BRANCHES:
        branches = [functools.partial(send, pair) for pair in pairs]
        near, far_more, low, high = lax.switch(branch.reshape(()), branches, far, own)
    else:
        sends = [functools.partial(from_partner, mask=mask) for mask in free_masks]
        low, high = (
            lax.switch(mask - free_masks[0], sends, own) for mask in free_masks_of(plan, far_mask)
        )
        near, far_more = send((), far, own)
    return correlate(plan, table_list, own, near, far, far_more, low, high, far_mask)


def solution(mesh):
    in_specs = (P("chan", "tm"), P(), P())
    out_specs = (P(("chan", "tm"), None, None), P(None, ("chan", "tm"), None, None))
    return jax.shard_map(
        on_device, mesh=mesh, in_specs=in_specs, out_specs=out_specs, check_vma=False
    )
```

```python
import functools
import math

import jax
import jax.numpy as jnp
import ml_dtypes
import numpy as np
from jax import lax
from jax.experimental import pallas as pl
from jax.experimental.pallas import tpu as pltpu
from jax.sharding import PartitionSpec as P

SEGS_DEV = 2
LAGS = 129
ROUNDS = 4
LANE = 128
MAX_BRANCHES = 128
OUT_GROUPS = 4
VMEM_LIMIT = 8 * 1024 * 1024
KERNEL_VMEM = 24 * 1024 * 1024
VMEM = pl.BlockSpec(memory_space=pltpu.VMEM)
SMEM = pl.BlockSpec(memory_space=pltpu.SMEM)
HBM = pl.BlockSpec(memory_space=pl.ANY)


def split_table(table):
    high = table.astype(ml_dtypes.bfloat16)
    low = (table - high.astype(np.float64)).astype(ml_dtypes.bfloat16)
    return np.concatenate([high, high, low], axis=0)


def tables(length):
    quarter = length // 4

    def packed(freqs, count):
        angle = 2.0 * math.pi / length * (np.arange(count)[:, None] * freqs[None, :] % length)
        return np.concatenate([np.cos(angle), -np.sin(angle)], axis=1)

    fours = 4 * np.arange(quarter // 2)
    odds = 2 * np.arange(quarter) + 1
    sum_table = packed(fours, quarter)
    sum_table[:, quarter // 2] = 1.0 - 2.0 * (np.arange(quarter) % 2)
    fold_tables = sum_table, packed(fours + 2, quarter), packed(odds, 2 * quarter)

    freqs = np.concatenate([fours, fours + 2, odds])[:, None]
    lag = (np.arange(LAGS) - LAGS // 2)[None, :]
    angle = 2.0 * math.pi / length * (lag * freqs % length)
    weight = np.where(freqs == 0, 1.0, 2.0) / length
    lag_cos = weight * np.cos(angle)
    lag_sin = weight * np.sin(angle)
    lag_sin[0] = (1.0 - 2.0 * (np.abs(lag[0]) % 2)) / length
    lag_table = np.zeros((length, 2 * LANE))
    lag_table[:, :LAGS] = np.concatenate([lag_cos, lag_sin], axis=0)
    return (*map(split_table, fold_tables), lag_table.astype(ml_dtypes.bfloat16))


def dot(left, right):
    return jnp.dot(left, right, preferred_element_type=jnp.float32)


def free_masks_of(plan, last_mask):
    masks = [plan[r] for r in range(ROUNDS)]
    free = [(mask != 1) & (mask != last_mask) for mask in masks]
    low = functools.reduce(
        jnp.minimum, [jnp.where(ok, mask, last_mask) for ok, mask in zip(free, masks)]
    )
    high = functools.reduce(jnp.maximum, [jnp.where(ok, mask, 0) for ok, mask in zip(free, masks)])
    return low, high


def prepare_kernel(last_mask, plan, taps, samples, *refs):
    tables_hbm, (branch, record, toep), refs = refs[:3], refs[3:6], refs[6:]
    tables_vmem, (own_sem, table_sems) = refs[:3], refs[3:]
    chans = samples.shape[0]
    copies = [pltpu.make_async_copy(samples, record.at[pl.ds(0, chans)], own_sem)]
    copies += [
        pltpu.make_async_copy(table, table_vmem, table_sems.at[i])
        for i, (table, table_vmem) in enumerate(zip(tables_hbm, tables_vmem))
    ]
    for copy in copies:
        copy.start()
    low, high = (mask - 2 for mask in free_masks_of(plan, last_mask))
    branch[0] = high * (high - 1) // 2 + low

    lane = lax.broadcasted_iota(jnp.int32, (1, 2 * LANE), 1)
    base = jnp.zeros((1, 2 * LANE), jnp.float32)
    for j in range(taps.shape[0]):
        base = jnp.where(lane == j, taps[j], base)
    base = jnp.broadcast_to(base, (2 * LANE, 2 * LANE))
    toeplitz = pltpu.roll(base, LANE, 1, stride=1, stride_axis=0)[:, :LANE]
    toep_hi = toeplitz.astype(jnp.bfloat16)
    toep[:, :LANE] = toep_hi
    toep[:, LANE:] = (toeplitz - toep_hi.astype(jnp.float32)).astype(jnp.bfloat16)
    for copy in copies:
        copy.wait()


def prepare(plan, fir_taps, samples, last_mask, parts):
    chans, width = samples.shape
    *table_list, lag_table = tables(width // SEGS_DEV)
    plan, fir_taps, samples, *table_list = (
        pltpu.with_memory_space_constraint(jnp.asarray(array), pltpu.HBM)
        for array in (plan, fir_taps, samples, *table_list)
    )
    branch, record, toep, *table_list = pl.pallas_call(
        functools.partial(prepare_kernel, last_mask),
        out_shape=(
            jax.ShapeDtypeStruct((1,), jnp.int32),
            pltpu.VMEM((parts * chans, width), jnp.bfloat16),
            pltpu.VMEM((2 * LANE, 2 * LANE), jnp.bfloat16),
            *[pltpu.VMEM(table.shape, jnp.bfloat16) for table in table_list],
        ),
        in_specs=[SMEM, SMEM] + [HBM] * (1 + len(table_list)),
        out_specs=(SMEM,) + (VMEM,) * (2 + len(table_list)),
        scratch_shapes=[
            pltpu.SemaphoreType.DMA,
            pltpu.SemaphoreType.DMA((len(table_list),)),
        ],
        compiler_params=pltpu.CompilerParams(vmem_limit_bytes=VMEM_LIMIT),
    )(plan, fir_taps, samples, *table_list)
    return branch, record, (toep, *table_list, jnp.asarray(lag_table))


def add_spectra(columns_of, place, parts, shape, first_row, toep, folds):
    chans, width = shape
    tiles = width // SEGS_DEV // LANE
    quarter = tiles // 4
    for piece in range(parts):
        tail = columns_of((piece + 1) % parts, width - LANE, width)
        has_before = jnp.where(lax.rem(place + parts - piece, parts) == 0, 0.0, 1.0)
        tail = (tail.astype(jnp.float32) * has_before).astype(jnp.bfloat16)
        windows = [jnp.concatenate([tail, columns_of(piece, 0, LANE)], axis=1)]
        windows += [
            columns_of(piece, LANE * (k - 1), LANE * (k + 1)) for k in range(1, width // LANE)
        ]
        both = dot(jnp.concatenate(windows, axis=0), toep[...])
        filtered = both[:, :LANE] + both[:, LANE:]
        for s in range(SEGS_DEV):
            row = first_row + (piece * SEGS_DEV + s) * chans
            for k in range(quarter):
                at = [(s * tiles + j * quarter + k) * chans for j in range(4)]
                x = [filtered[lo : lo + chans] for lo in at]
                even, later = x[0] + x[2], x[1] + x[3]
                sums, diffs, odds = folds
                for ref, tile, value in (
                    (sums, k, even + later),
                    (diffs, k, even - later),
                    (odds, k, x[0] - x[2]),
                    (odds, k + quarter, x[1] - x[3]),
                ):
                    high = value.astype(jnp.bfloat16)
                    low = (value - high.astype(jnp.float32)).astype(jnp.bfloat16)
                    for j, part in enumerate((high, low, high)):
                        at = ref.shape[1] // 3 * j + LANE * tile
                        ref[row : row + chans, at : at + LANE] = part


def whiten(folds, fold_tables, real_ref, imag_ref):
    products = [dot(fold[...], table[...]) for fold, table in zip(folds, fold_tables)]
    real, imag = (
        jnp.concatenate(
            [p[:, p.shape[1] // 2 * j : p.shape[1] // 2 * (j + 1)] for p in products], axis=1
        )
        for j in range(2)
    )
    real_sq = real * real
    imag_sq = imag * imag
    energy = real_sq + imag_sq
    freqs = real.shape[1] + 1
    level = 0.1 / freqs * jnp.sum(energy, axis=1, keepdims=True) + 1e-06
    first, rest = slice(0, LANE), slice(LANE, freqs - 1)
    edge = lax.broadcasted_iota(jnp.int32, real[:, first].shape, 1) == 0
    inv_real = lax.rsqrt(jnp.where(edge, real_sq[:, first], energy[:, first]) + level)
    inv_imag = jnp.where(edge, lax.rsqrt(imag_sq[:, first] + level), inv_real)
    inverse = lax.rsqrt(energy[:, rest] + level)
    for ref, value, inv in ((real_ref, real, inv_real), (imag_ref, imag, inv_imag)):
        for lanes, factor in ((first, inv), (rest, inverse)):
            whitened = (value[:, lanes] * factor).astype(jnp.bfloat16)
            ref[:, lanes] = whitened.astype(jnp.float32)


def cross_spectra(rows_a, chans, segs, left_ref, real_ref, imag_ref, cross):
    rows, half = real_ref.shape
    rows_blk = segs * chans
    sets = rows // rows_blk
    for i, a in enumerate(rows_a):
        for c in range(half // LANE):
            cols = slice(LANE * c, LANE * (c + 1))
            left = [
                jnp.broadcast_to(left_ref[a, j : j + 1, cols], (chans, LANE))
                for j in range(3 * segs)
            ]
            for q in range(sets):
                cos_part = sin_part = 0.0
                for s in range(segs):
                    row_b = slice(q * rows_blk + s * chans, q * rows_blk + (s + 1) * chans)
                    re_b, im_b = real_ref[row_b, cols], imag_ref[row_b, cols]
                    re_a, im_a, x_a = (left[segs * j + s] for j in range(3))
                    cos_part += re_a * re_b + im_a * im_b
                    sin_part += x_a * im_b - im_a * re_b
                at_q = slice((i * sets + q) * chans, (i * sets + q + 1) * chans)
                cross[at_q, cols] = cos_part.astype(jnp.bfloat16)
                cross[at_q, half + LANE * c : half + LANE * (c + 1)] = sin_part.astype(jnp.bfloat16)


def groups_of(share):
    return OUT_GROUPS if share % OUT_GROUPS == 0 else 1


def spectra_scratch(sets, parts, chans, length, share):
    rows, half = sets * parts * SEGS_DEV * chans, length // 2
    return [
        pltpu.VMEM((rows, 3 * length // 4), jnp.bfloat16),
        pltpu.VMEM((rows, 3 * length // 4), jnp.bfloat16),
        pltpu.VMEM((rows, 3 * half), jnp.bfloat16),
        pltpu.VMEM((rows, half), jnp.float32),
        pltpu.VMEM((rows, half), jnp.float32),
        *[
            pltpu.VMEM((share // groups_of(share) * sets * chans, length), jnp.bfloat16)
            for _ in range(groups_of(share))
        ],
    ]


def rows_of_block(block, chans):
    return lambda piece, lo, hi: block[piece * chans : (piece + 1) * chans, lo:hi]


def correlate_kernel(parts, last_mask, plan_hbm, toep, *refs):
    fold_tables, lag_hbm, refs = refs[:3], refs[3], refs[4:]
    own, far, near, low, high, refs = *refs[:5], refs[5:]
    far_more, (self_out, pair_out), refs = refs[: parts - 1], refs[parts - 1 : parts + 1], refs[parts + 1 :]
    plan, lag_table, arrived, far_arrived, left_ref, *refs = refs
    groups = groups_of(left_ref.shape[0])
    folds, (real_ref, imag_ref), refs = refs[:3], refs[3:5], refs[5:]
    crosses, staged, refs = refs[:groups], refs[groups], refs[groups + 1 :]
    plan_sem, lag_sem, sems, far_sems, out_sems = refs

    chans, width = far.shape
    half = real_ref.shape[1]
    share = left_ref.shape[0]
    segs = parts * SEGS_DEV
    sets = ROUNDS + 1
    place = lax.axis_index("tm")
    copies = [
        pltpu.make_async_copy(source, arrived.at[i], sems.at[i])
        for i, source in enumerate((near, low, high))
    ]
    far_copies = [
        pltpu.make_async_copy(source, far_arrived.at[i], far_sems.at[i])
        for i, source in enumerate(far_more)
    ]
    lag_copy = pltpu.make_async_copy(lag_hbm, lag_table, lag_sem)
    plan_copy = pltpu.make_async_copy(plan_hbm, plan, plan_sem)
    for copy in far_copies + copies + [lag_copy, plan_copy]:
        copy.start()

    def far_columns(piece, lo, hi):
        return far[:, lo:hi] if piece == 0 else far_arrived[piece - 1, :, lo:hi]

    blocks = (
        rows_of_block(own, chans),
        rows_of_block(arrived.at[0], chans),
        far_columns,
        rows_of_block(arrived.at[1], chans),
        rows_of_block(arrived.at[2], chans),
    )
    for q, columns_of in enumerate(blocks):
        if q == 1:
            for copy in far_copies + copies + [plan_copy, lag_copy]:
                copy.wait()
        first_row = q * segs * chans
        add_spectra(columns_of, place, parts, far.shape, first_row, toep, folds)
    whiten(folds, fold_tables, real_ref, imag_ref)

    def picked(ref, s):
        value = ref[s * chans : s * chans + share, :]
        for owner in range(1, parts):
            at = s * chans + owner * share
            value = jnp.where(place == owner, ref[at : at + share, :], value)
        return value

    edge = lax.broadcasted_iota(jnp.int32, (share, half), 1) == 0
    for s in range(segs):
        real_s, imag_s = picked(real_ref, s), picked(imag_ref, s)
        lefts = (real_s, jnp.where(edge, 0.0, imag_s), jnp.where(edge, imag_s, real_s))
        for j, value in enumerate(lefts):
            for a in range(share):
                left_ref[a, segs * j + s : segs * j + s + 1, :] = value[a : a + 1]

    low_mask, high_mask = free_masks_of(plan, last_mask)
    slots = [
        sum(jnp.where(plan[r] == mask, r, 0) for r in range(ROUNDS))
        for mask in (1, last_mask, low_mask, high_mask)
    ]
    outs = [self_out, *(pair_out.at[slot] for slot in slots)]
    out_copies = []
    count = share // groups
    for group in range(groups + 1):
        if group < groups:
            rows_a = range(group * count, (group + 1) * count)
            cross_spectra(rows_a, chans, segs, left_ref, real_ref, imag_ref, crosses[group])
        if group == 0:
            continue
        first = (group - 1) * count
        result = dot(crosses[group - 1][...], lag_table[...])
        for i in range(count):
            for q in range(sets):
                at = (i * sets + q) * chans
                staged[q, first + i] = result[at : at + chans, :LAGS]
        for q, out in enumerate(outs):
            piece = pl.ds(first, count)
            sem = out_sems.at[first // count * sets + q]
            out_copies.append(pltpu.make_async_copy(staged.at[q, piece], out.at[piece], sem))
            out_copies[-1].start()
    for copy in out_copies:
        copy.wait()


def correlate(plan, table_list, own, near, far, far_more, low, high, last_mask):
    chans, width = far.shape
    parts = len(far_more) + 1
    share = chans // parts
    length = width // SEGS_DEV
    sets = ROUNDS + 1
    *table_list, lag_table = table_list
    plan, lag_table = (
        pltpu.with_memory_space_constraint(array, pltpu.HBM) for array in (plan, lag_table)
    )
    return pl.pallas_call(
        functools.partial(correlate_kernel, parts, last_mask),
        out_shape=(
            jax.ShapeDtypeStruct((share, chans, LAGS), jnp.float32),
            jax.ShapeDtypeStruct((ROUNDS, share, chans, LAGS), jnp.float32),
        ),
        in_specs=[HBM] + [VMEM] * len(table_list) + [HBM] + [VMEM] * 2 + [HBM] * (parts + 2),
        out_specs=(HBM, HBM),
        scratch_shapes=[
            pltpu.SMEM(plan.shape, jnp.int32),
            pltpu.VMEM(lag_table.shape, jnp.bfloat16),
            pltpu.VMEM((3, *own.shape), jnp.bfloat16),
            pltpu.VMEM((parts - 1, chans, width), jnp.bfloat16),
            pltpu.VMEM((share, 3 * parts * SEGS_DEV, length // 2), jnp.float32),
            *spectra_scratch(sets, parts, chans, length, share),
            pltpu.VMEM((sets, share, chans, LAGS), jnp.float32),
            pltpu.SemaphoreType.DMA,
            pltpu.SemaphoreType.DMA,
            pltpu.SemaphoreType.DMA((3,)),
            pltpu.SemaphoreType.DMA((parts - 1,)),
            pltpu.SemaphoreType.DMA((sets * OUT_GROUPS,)),
        ],
        compiler_params=pltpu.CompilerParams(vmem_limit_bytes=KERNEL_VMEM),
    )(plan, *table_list, lag_table, own, far, near, low, high, *far_more)


def from_partner(block, mask):
    chan_count = lax.axis_size("chan")
    return lax.ppermute(block, "chan", [(g, g ^ mask) for g in range(chan_count)])


def from_times(block):
    parts = lax.axis_size("tm")
    return [
        lax.ppermute(block, "tm", [(t, (t + j) % parts) for t in range(parts)])
        for j in range(1, parts)
    ]


def on_device(samples, fir_taps, plan):
    chan_count, parts = lax.axis_size("chan"), lax.axis_size("tm")
    chans = samples.shape[0]
    near_mask, far_mask = 1, chan_count - 1
    free_masks = range(2, far_mask)

    far = from_partner(samples, far_mask)
    others = from_times(samples)
    branch, own, table_list = prepare(plan, fir_taps, samples, far_mask, parts)
    for j, piece in enumerate(others):
        own = lax.dynamic_update_slice(own, piece, ((j + 1) * chans, 0))

    def send(masks, far, own):
        return from_partner(own, near_mask), from_times(far), *[from_partner(own, m) for m in masks]

    pairs = [(low, high) for high in free_masks for low in free_masks if low < high]
    if len(pairs) <= MAX_BRANCHES:
        branches = [functools.partial(send, pair) for pair in pairs]
        near, far_more, low, high = lax.switch(branch.reshape(()), branches, far, own)
    else:
        sends = [functools.partial(from_partner, mask=mask) for mask in free_masks]
        low, high = (
            lax.switch(mask - free_masks[0], sends, own) for mask in free_masks_of(plan, far_mask)
        )
        near, far_more = send((), far, own)
    return correlate(plan, table_list, own, near, far, far_more, low, high, far_mask)


def solution(mesh):
    in_specs = (P("chan", "tm"), P(), P())
    out_specs = (P(("chan", "tm"), None, None), P(None, ("chan", "tm"), None, None))
    return jax.shard_map(
        on_device, mesh=mesh, in_specs=in_specs, out_specs=out_specs, check_vma=False
    )
```

```python
import functools
import math

import jax
import jax.numpy as jnp
import ml_dtypes
import numpy as np
from jax import lax
from jax.experimental import pallas as pl
from jax.experimental.pallas import tpu as pltpu
from jax.sharding import PartitionSpec as P

SEGS_DEV = 2
LAGS = 129
ROUNDS = 4
LANE = 128
MAX_BRANCHES = 128
FIXED_SETS = 3
VMEM_LIMIT = 8 * 1024 * 1024
KERNEL_VMEM = 24 * 1024 * 1024
VMEM = pl.BlockSpec(memory_space=pltpu.VMEM)
SMEM = pl.BlockSpec(memory_space=pltpu.SMEM)
HBM = pl.BlockSpec(memory_space=pl.ANY)


def split_table(table):
    high = table.astype(ml_dtypes.bfloat16)
    low = (table - high.astype(np.float64)).astype(ml_dtypes.bfloat16)
    return np.concatenate([high, high, low], axis=0)


def tables(length):
    quarter = length // 4

    def packed(freqs, count):
        angle = 2.0 * math.pi / length * (np.arange(count)[:, None] * freqs[None, :] % length)
        return np.concatenate([np.cos(angle), -np.sin(angle)], axis=1)

    fours = 4 * np.arange(quarter // 2)
    odds = 2 * np.arange(quarter) + 1
    sum_table = packed(fours, quarter)
    sum_table[:, quarter // 2] = 1.0 - 2.0 * (np.arange(quarter) % 2)
    fold_tables = sum_table, packed(fours + 2, quarter), packed(odds, 2 * quarter)

    freqs = np.concatenate([fours, fours + 2, odds])[:, None]
    lag = (np.arange(LAGS) - LAGS // 2)[None, :]
    angle = 2.0 * math.pi / length * (lag * freqs % length)
    weight = np.where(freqs == 0, 1.0, 2.0) / length
    lag_cos = weight * np.cos(angle)
    lag_sin = weight * np.sin(angle)
    lag_sin[0] = (1.0 - 2.0 * (np.abs(lag[0]) % 2)) / length
    lag_table = np.zeros((length, 2 * LANE))
    lag_table[:, :LAGS] = np.concatenate([lag_cos, lag_sin], axis=0)
    return (*map(split_table, fold_tables), lag_table.astype(ml_dtypes.bfloat16))


def dot(left, right):
    return jnp.dot(left, right, preferred_element_type=jnp.float32)


def free_masks_of(plan, last_mask):
    masks = [plan[r] for r in range(ROUNDS)]
    free = [(mask != 1) & (mask != last_mask) for mask in masks]
    low = functools.reduce(
        jnp.minimum, [jnp.where(ok, mask, last_mask) for ok, mask in zip(free, masks)]
    )
    high = functools.reduce(jnp.maximum, [jnp.where(ok, mask, 0) for ok, mask in zip(free, masks)])
    return low, high


def prepare_kernel(last_mask, plan, taps, samples, *refs):
    tables_hbm, (branch, record, toep), refs = refs[:3], refs[3:6], refs[6:]
    tables_vmem, (own_sem, table_sems) = refs[:3], refs[3:]
    chans = samples.shape[0]
    copies = [pltpu.make_async_copy(samples, record.at[pl.ds(0, chans)], own_sem)]
    copies += [
        pltpu.make_async_copy(table, table_vmem, table_sems.at[i])
        for i, (table, table_vmem) in enumerate(zip(tables_hbm, tables_vmem))
    ]
    for copy in copies:
        copy.start()
    low, high = (mask - 2 for mask in free_masks_of(plan, last_mask))
    branch[0] = high * (high - 1) // 2 + low

    lane = lax.broadcasted_iota(jnp.int32, (1, 2 * LANE), 1)
    base = jnp.zeros((1, 2 * LANE), jnp.float32)
    for j in range(taps.shape[0]):
        base = jnp.where(lane == j, taps[j], base)
    base = jnp.broadcast_to(base, (2 * LANE, 2 * LANE))
    toeplitz = pltpu.roll(base, LANE, 1, stride=1, stride_axis=0)[:, :LANE]
    toep_hi = toeplitz.astype(jnp.bfloat16)
    toep[:, :LANE] = toep_hi
    toep[:, LANE:] = (toeplitz - toep_hi.astype(jnp.float32)).astype(jnp.bfloat16)
    for copy in copies:
        copy.wait()


def prepare(plan, fir_taps, samples, last_mask, parts):
    chans, width = samples.shape
    *table_list, lag_table = tables(width // SEGS_DEV)
    plan, fir_taps, samples, *table_list = (
        pltpu.with_memory_space_constraint(jnp.asarray(array), pltpu.HBM)
        for array in (plan, fir_taps, samples, *table_list)
    )
    branch, record, toep, *table_list = pl.pallas_call(
        functools.partial(prepare_kernel, last_mask),
        out_shape=(
            jax.ShapeDtypeStruct((1,), jnp.int32),
            pltpu.VMEM((parts * chans, width), jnp.bfloat16),
            pltpu.VMEM((2 * LANE, 2 * LANE), jnp.bfloat16),
            *[pltpu.VMEM(table.shape, jnp.bfloat16) for table in table_list],
        ),
        in_specs=[SMEM, SMEM] + [HBM] * (1 + len(table_list)),
        out_specs=(SMEM,) + (VMEM,) * (2 + len(table_list)),
        scratch_shapes=[
            pltpu.SemaphoreType.DMA,
            pltpu.SemaphoreType.DMA((len(table_list),)),
        ],
        compiler_params=pltpu.CompilerParams(vmem_limit_bytes=VMEM_LIMIT),
    )(plan, fir_taps, samples, *table_list)
    return branch, record, (toep, *table_list, jnp.asarray(lag_table))


def add_spectra(columns_of, place, parts, shape, first_row, toep, folds):
    chans, width = shape
    tiles = width // SEGS_DEV // LANE
    quarter = tiles // 4
    for piece in range(parts):
        tail = columns_of((piece + 1) % parts, width - LANE, width)
        has_before = jnp.where(lax.rem(place + parts - piece, parts) == 0, 0.0, 1.0)
        tail = (tail.astype(jnp.float32) * has_before).astype(jnp.bfloat16)
        windows = [jnp.concatenate([tail, columns_of(piece, 0, LANE)], axis=1)]
        windows += [
            columns_of(piece, LANE * (k - 1), LANE * (k + 1)) for k in range(1, width // LANE)
        ]
        both = dot(jnp.concatenate(windows, axis=0), toep[...])
        filtered = both[:, :LANE] + both[:, LANE:]
        for s in range(SEGS_DEV):
            row = first_row + (piece * SEGS_DEV + s) * chans
            for k in range(quarter):
                at = [(s * tiles + j * quarter + k) * chans for j in range(4)]
                x = [filtered[lo : lo + chans] for lo in at]
                even, later = x[0] + x[2], x[1] + x[3]
                sums, diffs, odds = folds
                for ref, tile, value in (
                    (sums, k, even + later),
                    (diffs, k, even - later),
                    (odds, k, x[0] - x[2]),
                    (odds, k + quarter, x[1] - x[3]),
                ):
                    high = value.astype(jnp.bfloat16)
                    low = (value - high.astype(jnp.float32)).astype(jnp.bfloat16)
                    for j, part in enumerate((high, low, high)):
                        at = ref.shape[1] // 3 * j + LANE * tile
                        ref[row : row + chans, at : at + LANE] = part


def transform(folds, fold_tables):
    return [dot(fold[...], table[...]) for fold, table in zip(folds, fold_tables)]


def whiten(products, real_ref, imag_ref):
    real, imag = (
        jnp.concatenate(
            [p[:, p.shape[1] // 2 * j : p.shape[1] // 2 * (j + 1)] for p in products], axis=1
        )
        for j in range(2)
    )
    real_sq = real * real
    imag_sq = imag * imag
    energy = real_sq + imag_sq
    freqs = real.shape[1] + 1
    level = 0.1 / freqs * jnp.sum(energy, axis=1, keepdims=True) + 1e-06
    first, rest = slice(0, LANE), slice(LANE, freqs - 1)
    edge = lax.broadcasted_iota(jnp.int32, real[:, first].shape, 1) == 0
    inv_real = lax.rsqrt(jnp.where(edge, real_sq[:, first], energy[:, first]) + level)
    inv_imag = jnp.where(edge, lax.rsqrt(imag_sq[:, first] + level), inv_real)
    inverse = lax.rsqrt(energy[:, rest] + level)
    for ref, value, inv in ((real_ref, real, inv_real), (imag_ref, imag, inv_imag)):
        for lanes, factor in ((first, inv), (rest, inverse)):
            whitened = (value[:, lanes] * factor).astype(jnp.bfloat16)
            ref[:, lanes] = whitened.astype(jnp.float32)


def cross_spectra(chans, segs, left_ref, spectra, cross):
    real_ref, imag_ref = spectra
    rows, half = real_ref.shape
    rows_blk = segs * chans
    sets = rows // rows_blk
    for a in range(left_ref.shape[0]):
        for c in range(half // LANE):
            cols = slice(LANE * c, LANE * (c + 1))
            left = [
                jnp.broadcast_to(left_ref[a, j : j + 1, cols], (chans, LANE))
                for j in range(3 * segs)
            ]
            for q in range(sets):
                cos_part = sin_part = 0.0
                for s in range(segs):
                    row_b = slice(q * rows_blk + s * chans, q * rows_blk + (s + 1) * chans)
                    re_b, im_b = real_ref[row_b, cols], imag_ref[row_b, cols]
                    re_a, im_a, x_a = (left[segs * j + s] for j in range(3))
                    cos_part += re_a * re_b + im_a * im_b
                    sin_part += x_a * im_b - im_a * re_b
                at = (q * left_ref.shape[0] + a) * chans
                at_q = slice(at, at + chans)
                cross[at_q, cols] = cos_part.astype(jnp.bfloat16)
                cross[at_q, half + LANE * c : half + LANE * (c + 1)] = sin_part.astype(jnp.bfloat16)


def spectra_scratch(sets, parts, chans, length):
    rows, half = sets * parts * SEGS_DEV * chans, length // 2
    return [
        pltpu.VMEM((rows, 3 * length // 4), jnp.bfloat16),
        pltpu.VMEM((rows, 3 * length // 4), jnp.bfloat16),
        pltpu.VMEM((rows, 3 * half), jnp.bfloat16),
        pltpu.VMEM((rows, half), jnp.float32),
        pltpu.VMEM((rows, half), jnp.float32),
    ]


def rows_of_block(block, chans):
    return lambda piece, lo, hi: block[piece * chans : (piece + 1) * chans, lo:hi]


def correlate_kernel(parts, last_mask, plan_hbm, toep, *refs):
    fold_tables, lag_hbm, refs = refs[:3], refs[3], refs[4:]
    own, far, near, low, high, refs = *refs[:5], refs[5:]
    far_more, (self_out, pair_out), refs = refs[: parts - 1], refs[parts - 1 : parts + 1], refs[parts + 1 :]
    plan, lag_table, arrived, far_arrived, left_ref, *refs = refs
    fixed_folds, fixed_spectra, refs = refs[:3], refs[3:5], refs[5:]
    free_folds, free_spectra, refs = refs[:3], refs[3:5], refs[5:]
    real_ref, imag_ref = fixed_spectra
    fixed_cross, free_cross, staged, *refs = refs
    plan_sem, lag_sem, sems, far_sems, out_sems = refs

    chans, width = far.shape
    half = real_ref.shape[1]
    share = left_ref.shape[0]
    segs = parts * SEGS_DEV
    sets = ROUNDS + 1
    place = lax.axis_index("tm")
    copies = [
        pltpu.make_async_copy(source, arrived.at[i], sems.at[i])
        for i, source in enumerate((near, low, high))
    ]
    far_copies = [
        pltpu.make_async_copy(source, far_arrived.at[i], far_sems.at[i])
        for i, source in enumerate(far_more)
    ]
    lag_copy = pltpu.make_async_copy(lag_hbm, lag_table, lag_sem)
    plan_copy = pltpu.make_async_copy(plan_hbm, plan, plan_sem)
    for copy in far_copies + copies + [lag_copy, plan_copy]:
        copy.start()

    def far_columns(piece, lo, hi):
        return far[:, lo:hi] if piece == 0 else far_arrived[piece - 1, :, lo:hi]

    blocks = (
        rows_of_block(own, chans),
        rows_of_block(arrived.at[0], chans),
        far_columns,
        rows_of_block(arrived.at[1], chans),
        rows_of_block(arrived.at[2], chans),
    )
    for q, columns_of in enumerate(blocks):
        if q == 1:
            for copy in far_copies + copies + [plan_copy, lag_copy]:
                copy.wait()
        if q == FIXED_SETS:
            fixed_products = transform(fixed_folds, fold_tables)
        folds, at = (fixed_folds, q) if q < FIXED_SETS else (free_folds, q - FIXED_SETS)
        first_row = at * segs * chans
        add_spectra(columns_of, place, parts, far.shape, first_row, toep, folds)
    whiten(fixed_products, real_ref, imag_ref)
    free_products = transform(free_folds, fold_tables)

    def picked(ref, s):
        value = ref[s * chans : s * chans + share, :]
        for owner in range(1, parts):
            at = s * chans + owner * share
            value = jnp.where(place == owner, ref[at : at + share, :], value)
        return value

    edge = lax.broadcasted_iota(jnp.int32, (share, half), 1) == 0
    for s in range(segs):
        real_s, imag_s = picked(real_ref, s), picked(imag_ref, s)
        lefts = (real_s, jnp.where(edge, 0.0, imag_s), jnp.where(edge, imag_s, real_s))
        for j, value in enumerate(lefts):
            for a in range(share):
                left_ref[a, segs * j + s : segs * j + s + 1, :] = value[a : a + 1]

    low_mask, high_mask = free_masks_of(plan, last_mask)
    slots = [
        sum(jnp.where(plan[r] == mask, r, 0) for r in range(ROUNDS))
        for mask in (1, last_mask, low_mask, high_mask)
    ]
    outs = [self_out, *(pair_out.at[slot] for slot in slots)]
    out_copies = []

    def lag_product(cross, first_set):
        result = dot(cross[...], lag_table[...])
        for row in range(cross.shape[0] // chans):
            q, a = divmod(row, share)
            staged[first_set + q, a] = result[row * chans : (row + 1) * chans, :LAGS]

    def copy_out(some):
        for q in some:
            copy = pltpu.make_async_copy(staged.at[q], outs[q], out_sems.at[q])
            copy.start()
            out_copies.append(copy)

    cross_spectra(chans, segs, left_ref, fixed_spectra, fixed_cross)
    whiten(free_products, *free_spectra)
    cross_spectra(chans, segs, left_ref, free_spectra, free_cross)
    lag_product(fixed_cross, 0)
    copy_out(range(FIXED_SETS))
    lag_product(free_cross, FIXED_SETS)
    copy_out(range(FIXED_SETS, sets))
    for copy in out_copies:
        copy.wait()


def correlate(plan, table_list, own, near, far, far_more, low, high, last_mask):
    chans, width = far.shape
    parts = len(far_more) + 1
    share = chans // parts
    length = width // SEGS_DEV
    sets = ROUNDS + 1
    *table_list, lag_table = table_list
    plan, lag_table = (
        pltpu.with_memory_space_constraint(array, pltpu.HBM) for array in (plan, lag_table)
    )
    return pl.pallas_call(
        functools.partial(correlate_kernel, parts, last_mask),
        out_shape=(
            jax.ShapeDtypeStruct((share, chans, LAGS), jnp.float32),
            jax.ShapeDtypeStruct((ROUNDS, share, chans, LAGS), jnp.float32),
        ),
        in_specs=[HBM] + [VMEM] * len(table_list) + [HBM] + [VMEM] * 2 + [HBM] * (parts + 2),
        out_specs=(HBM, HBM),
        scratch_shapes=[
            pltpu.SMEM(plan.shape, jnp.int32),
            pltpu.VMEM(lag_table.shape, jnp.bfloat16),
            pltpu.VMEM((3, *own.shape), jnp.bfloat16),
            pltpu.VMEM((parts - 1, chans, width), jnp.bfloat16),
            pltpu.VMEM((share, 3 * parts * SEGS_DEV, length // 2), jnp.float32),
            *spectra_scratch(FIXED_SETS, parts, chans, length),
            *spectra_scratch(sets - FIXED_SETS, parts, chans, length),
            pltpu.VMEM((FIXED_SETS * share * chans, length), jnp.bfloat16),
            pltpu.VMEM(((sets - FIXED_SETS) * share * chans, length), jnp.bfloat16),
            pltpu.VMEM((sets, share, chans, LAGS), jnp.float32),
            pltpu.SemaphoreType.DMA,
            pltpu.SemaphoreType.DMA,
            pltpu.SemaphoreType.DMA((3,)),
            pltpu.SemaphoreType.DMA((parts - 1,)),
            pltpu.SemaphoreType.DMA((sets,)),
        ],
        compiler_params=pltpu.CompilerParams(vmem_limit_bytes=KERNEL_VMEM),
    )(plan, *table_list, lag_table, own, far, near, low, high, *far_more)


def from_partner(block, mask):
    chan_count = lax.axis_size("chan")
    return lax.ppermute(block, "chan", [(g, g ^ mask) for g in range(chan_count)])


def from_times(block):
    parts = lax.axis_size("tm")
    return [
        lax.ppermute(block, "tm", [(t, (t + j) % parts) for t in range(parts)])
        for j in range(1, parts)
    ]


def on_device(samples, fir_taps, plan):
    chan_count, parts = lax.axis_size("chan"), lax.axis_size("tm")
    chans = samples.shape[0]
    near_mask, far_mask = 1, chan_count - 1
    free_masks = range(2, far_mask)

    far = from_partner(samples, far_mask)
    others = from_times(samples)
    branch, own, table_list = prepare(plan, fir_taps, samples, far_mask, parts)
    for j, piece in enumerate(others):
        own = lax.dynamic_update_slice(own, piece, ((j + 1) * chans, 0))

    def send(masks, far, own):
        return from_partner(own, near_mask), from_times(far), *[from_partner(own, m) for m in masks]

    pairs = [(low, high) for high in free_masks for low in free_masks if low < high]
    if len(pairs) <= MAX_BRANCHES:
        branches = [functools.partial(send, pair) for pair in pairs]
        near, far_more, low, high = lax.switch(branch.reshape(()), branches, far, own)
    else:
        sends = [functools.partial(from_partner, mask=mask) for mask in free_masks]
        low, high = (
            lax.switch(mask - free_masks[0], sends, own) for mask in free_masks_of(plan, far_mask)
        )
        near, far_more = send((), far, own)
    return correlate(plan, table_list, own, near, far, far_more, low, high, far_mask)


def solution(mesh):
    in_specs = (P("chan", "tm"), P(), P())
    out_specs = (P(("chan", "tm"), None, None), P(None, ("chan", "tm"), None, None))
    return jax.shard_map(
        on_device, mesh=mesh, in_specs=in_specs, out_specs=out_specs, check_vma=False
    )
```

```python
import functools
import math

import jax
import jax.numpy as jnp
import ml_dtypes
import numpy as np
from jax import lax
from jax.experimental import pallas as pl
from jax.experimental.pallas import tpu as pltpu
from jax.sharding import PartitionSpec as P

SEGS_DEV = 2
LAGS = 129
ROUNDS = 4
LANE = 128
MAX_BRANCHES = 128
FIXED_SETS = 3
VMEM_LIMIT = 8 * 1024 * 1024
KERNEL_VMEM = 24 * 1024 * 1024
VMEM = pl.BlockSpec(memory_space=pltpu.VMEM)
SMEM = pl.BlockSpec(memory_space=pltpu.SMEM)
HBM = pl.BlockSpec(memory_space=pl.ANY)


def split_table(table):
    high = table.astype(ml_dtypes.bfloat16)
    low = (table - high.astype(np.float64)).astype(ml_dtypes.bfloat16)
    return np.concatenate([high, high, low], axis=0)


def tables(length):
    quarter = length // 4

    def packed(freqs, count):
        angle = 2.0 * math.pi / length * (np.arange(count)[:, None] * freqs[None, :] % length)
        return np.concatenate([np.cos(angle), -np.sin(angle)], axis=1)

    fours = 4 * np.arange(quarter // 2)
    odds = 2 * np.arange(quarter) + 1
    sum_table = packed(fours, quarter)
    sum_table[:, quarter // 2] = 1.0 - 2.0 * (np.arange(quarter) % 2)
    fold_tables = sum_table, packed(fours + 2, quarter), packed(odds, 2 * quarter)

    freqs = np.concatenate([fours, fours + 2, odds])[:, None]
    lag = (np.arange(LAGS) - LAGS // 2)[None, :]
    angle = 2.0 * math.pi / length * (lag * freqs % length)
    weight = np.where(freqs == 0, 1.0, 2.0) / length
    lag_cos = weight * np.cos(angle)
    lag_sin = weight * np.sin(angle)
    lag_sin[0] = (1.0 - 2.0 * (np.abs(lag[0]) % 2)) / length
    lag_table = np.zeros((length, 2 * LANE))
    lag_table[:, :LAGS] = np.concatenate([lag_cos, lag_sin], axis=0)
    return (*map(split_table, fold_tables), lag_table.astype(ml_dtypes.bfloat16))


def dot(left, right):
    return jnp.dot(left, right, preferred_element_type=jnp.float32)


def free_masks_of(plan, last_mask):
    masks = [plan[r] for r in range(ROUNDS)]
    free = [(mask != 1) & (mask != last_mask) for mask in masks]
    low = functools.reduce(
        jnp.minimum, [jnp.where(ok, mask, last_mask) for ok, mask in zip(free, masks)]
    )
    high = functools.reduce(jnp.maximum, [jnp.where(ok, mask, 0) for ok, mask in zip(free, masks)])
    return low, high


def prepare_kernel(last_mask, plan, taps, samples, *refs):
    tables_hbm, (branch, record, toep), refs = refs[:3], refs[3:6], refs[6:]
    tables_vmem, (own_sem, table_sems) = refs[:3], refs[3:]
    chans = samples.shape[0]
    copies = [pltpu.make_async_copy(samples, record.at[pl.ds(0, chans)], own_sem)]
    copies += [
        pltpu.make_async_copy(table, table_vmem, table_sems.at[i])
        for i, (table, table_vmem) in enumerate(zip(tables_hbm, tables_vmem))
    ]
    for copy in copies:
        copy.start()
    low, high = (mask - 2 for mask in free_masks_of(plan, last_mask))
    branch[0] = high * (high - 1) // 2 + low

    lane = lax.broadcasted_iota(jnp.int32, (1, 2 * LANE), 1)
    base = jnp.zeros((1, 2 * LANE), jnp.float32)
    for j in range(taps.shape[0]):
        base = jnp.where(lane == j, taps[j], base)
    base = jnp.broadcast_to(base, (2 * LANE, 2 * LANE))
    toeplitz = pltpu.roll(base, LANE, 1, stride=1, stride_axis=0)[:, :LANE]
    toep_hi = toeplitz.astype(jnp.bfloat16)
    toep[:, :LANE] = toep_hi
    toep[:, LANE:] = (toeplitz - toep_hi.astype(jnp.float32)).astype(jnp.bfloat16)
    for copy in copies:
        copy.wait()


def prepare(plan, fir_taps, samples, last_mask, parts):
    chans, width = samples.shape
    *table_list, lag_table = tables(width // SEGS_DEV)
    plan, fir_taps, samples, *table_list = (
        pltpu.with_memory_space_constraint(jnp.asarray(array), pltpu.HBM)
        for array in (plan, fir_taps, samples, *table_list)
    )
    branch, record, toep, *table_list = pl.pallas_call(
        functools.partial(prepare_kernel, last_mask),
        out_shape=(
            jax.ShapeDtypeStruct((1,), jnp.int32),
            pltpu.VMEM((parts * chans, width), jnp.bfloat16),
            pltpu.VMEM((2 * LANE, 2 * LANE), jnp.bfloat16),
            *[pltpu.VMEM(table.shape, jnp.bfloat16) for table in table_list],
        ),
        in_specs=[SMEM, SMEM] + [HBM] * (1 + len(table_list)),
        out_specs=(SMEM,) + (VMEM,) * (2 + len(table_list)),
        scratch_shapes=[
            pltpu.SemaphoreType.DMA,
            pltpu.SemaphoreType.DMA((len(table_list),)),
        ],
        compiler_params=pltpu.CompilerParams(vmem_limit_bytes=VMEM_LIMIT),
    )(plan, fir_taps, samples, *table_list)
    return branch, record, (toep, *table_list, jnp.asarray(lag_table))


def add_spectra(columns_of, place, parts, shape, first_row, toep, folds):
    chans, width = shape
    tiles = width // SEGS_DEV // LANE
    quarter = tiles // 4
    for piece in range(parts):
        tail = columns_of((piece + 1) % parts, width - LANE, width)
        has_before = jnp.where(lax.rem(place + parts - piece, parts) == 0, 0.0, 1.0)
        tail = (tail.astype(jnp.float32) * has_before).astype(jnp.bfloat16)
        windows = [jnp.concatenate([tail, columns_of(piece, 0, LANE)], axis=1)]
        windows += [
            columns_of(piece, LANE * (k - 1), LANE * (k + 1)) for k in range(1, width // LANE)
        ]
        both = dot(jnp.concatenate(windows, axis=0), toep[...])
        filtered = both[:, :LANE] + both[:, LANE:]
        for s in range(SEGS_DEV):
            row = first_row + (piece * SEGS_DEV + s) * chans
            for k in range(quarter):
                at = [(s * tiles + j * quarter + k) * chans for j in range(4)]
                x = [filtered[lo : lo + chans] for lo in at]
                even, later = x[0] + x[2], x[1] + x[3]
                sums, diffs, odds = folds
                for ref, tile, value in (
                    (sums, k, even + later),
                    (diffs, k, even - later),
                    (odds, k, x[0] - x[2]),
                    (odds, k + quarter, x[1] - x[3]),
                ):
                    high = value.astype(jnp.bfloat16)
                    low = (value - high.astype(jnp.float32)).astype(jnp.bfloat16)
                    for j, part in enumerate((high, low, high)):
                        at = ref.shape[1] // 3 * j + LANE * tile
                        ref[row : row + chans, at : at + LANE] = part


def transform(folds, fold_tables):
    return [dot(fold[...], table[...]) for fold, table in zip(folds, fold_tables)]


def whiten(products, real_ref, imag_ref):
    real, imag = (
        jnp.concatenate(
            [p[:, p.shape[1] // 2 * j : p.shape[1] // 2 * (j + 1)] for p in products], axis=1
        )
        for j in range(2)
    )
    real_sq = real * real
    imag_sq = imag * imag
    energy = real_sq + imag_sq
    freqs = real.shape[1] + 1
    level = 0.1 / freqs * jnp.sum(energy, axis=1, keepdims=True) + 1e-06
    first, rest = slice(0, LANE), slice(LANE, freqs - 1)
    edge = lax.broadcasted_iota(jnp.int32, real[:, first].shape, 1) == 0
    inv_real = lax.rsqrt(jnp.where(edge, real_sq[:, first], energy[:, first]) + level)
    inv_imag = jnp.where(edge, lax.rsqrt(imag_sq[:, first] + level), inv_real)
    inverse = lax.rsqrt(energy[:, rest] + level)
    for ref, value, inv in ((real_ref, real, inv_real), (imag_ref, imag, inv_imag)):
        for lanes, factor in ((first, inv), (rest, inverse)):
            whitened = (value[:, lanes] * factor).astype(jnp.bfloat16)
            ref[:, lanes] = whitened.astype(jnp.float32)


def cross_spectra(chans, segs, left_ref, spectra, cross):
    real_ref, imag_ref = spectra
    rows, half = real_ref.shape
    rows_blk = segs * chans
    sets = rows // rows_blk
    for a in range(left_ref.shape[0]):
        for c in range(half // LANE):
            cols = slice(LANE * c, LANE * (c + 1))
            left = [
                jnp.broadcast_to(left_ref[a, j : j + 1, cols], (chans, LANE))
                for j in range(3 * segs)
            ]
            for q in range(sets):
                cos_part = sin_part = 0.0
                for s in range(segs):
                    row_b = slice(q * rows_blk + s * chans, q * rows_blk + (s + 1) * chans)
                    re_b, im_b = real_ref[row_b, cols], imag_ref[row_b, cols]
                    re_a, im_a, x_a = (left[segs * j + s] for j in range(3))
                    cos_part += re_a * re_b + im_a * im_b
                    sin_part += x_a * im_b - im_a * re_b
                at = (q * left_ref.shape[0] + a) * chans
                at_q = slice(at, at + chans)
                cross[at_q, cols] = cos_part.astype(jnp.bfloat16)
                cross[at_q, half + LANE * c : half + LANE * (c + 1)] = sin_part.astype(jnp.bfloat16)


def spectra_scratch(sets, parts, chans, length):
    rows, half = sets * parts * SEGS_DEV * chans, length // 2
    return [
        pltpu.VMEM((rows, 3 * length // 4), jnp.bfloat16),
        pltpu.VMEM((rows, 3 * length // 4), jnp.bfloat16),
        pltpu.VMEM((rows, 3 * half), jnp.bfloat16),
        pltpu.VMEM((rows, half), jnp.float32),
        pltpu.VMEM((rows, half), jnp.float32),
    ]


def rows_of_block(block, chans):
    return lambda piece, lo, hi: block[piece * chans : (piece + 1) * chans, lo:hi]


def correlate_kernel(parts, last_mask, plan_hbm, toep, *refs):
    fold_tables, lag_hbm, refs = refs[:3], refs[3], refs[4:]
    own, far, near, low, high, refs = *refs[:5], refs[5:]
    far_more, (self_out, pair_out), refs = refs[: parts - 1], refs[parts - 1 : parts + 1], refs[parts + 1 :]
    plan, lag_table, arrived, far_arrived, left_ref, *refs = refs
    fixed_folds, fixed_spectra, refs = refs[:3], refs[3:5], refs[5:]
    free_folds, free_spectra, refs = refs[:3], refs[3:5], refs[5:]
    real_ref, imag_ref = fixed_spectra
    fixed_cross, free_cross, staged, *refs = refs
    plan_sem, lag_sem, sems, far_sems, out_sems = refs

    chans, width = far.shape
    half = real_ref.shape[1]
    share = left_ref.shape[0]
    segs = parts * SEGS_DEV
    sets = ROUNDS + 1
    place = lax.axis_index("tm")
    copies = [
        pltpu.make_async_copy(source, arrived.at[i], sems.at[i])
        for i, source in enumerate((near, low, high))
    ]
    far_copies = [
        pltpu.make_async_copy(source, far_arrived.at[i], far_sems.at[i])
        for i, source in enumerate(far_more)
    ]
    lag_copy = pltpu.make_async_copy(lag_hbm, lag_table, lag_sem)
    plan_copy = pltpu.make_async_copy(plan_hbm, plan, plan_sem)
    for copy in far_copies + copies + [lag_copy, plan_copy]:
        copy.start()

    def far_columns(piece, lo, hi):
        return far[:, lo:hi] if piece == 0 else far_arrived[piece - 1, :, lo:hi]

    blocks = (
        rows_of_block(own, chans),
        rows_of_block(arrived.at[0], chans),
        far_columns,
        rows_of_block(arrived.at[1], chans),
        rows_of_block(arrived.at[2], chans),
    )
    for q, columns_of in enumerate(blocks):
        if q == 1:
            for copy in far_copies + copies + [plan_copy, lag_copy]:
                copy.wait()
        if q == FIXED_SETS:
            fixed_products = transform(fixed_folds, fold_tables)
        folds, at = (fixed_folds, q) if q < FIXED_SETS else (free_folds, q - FIXED_SETS)
        first_row = at * segs * chans
        add_spectra(columns_of, place, parts, far.shape, first_row, toep, folds)
    whiten(fixed_products, real_ref, imag_ref)
    free_products = transform(free_folds, fold_tables)

    def picked(ref, s):
        value = ref[s * chans : s * chans + share, :]
        for owner in range(1, parts):
            at = s * chans + owner * share
            value = jnp.where(place == owner, ref[at : at + share, :], value)
        return value

    edge = lax.broadcasted_iota(jnp.int32, (share, half), 1) == 0
    for s in range(segs):
        real_s, imag_s = picked(real_ref, s), picked(imag_ref, s)
        lefts = (real_s, jnp.where(edge, 0.0, imag_s), jnp.where(edge, imag_s, real_s))
        for j, value in enumerate(lefts):
            for a in range(share):
                left_ref[a, segs * j + s : segs * j + s + 1, :] = value[a : a + 1]

    low_mask, high_mask = free_masks_of(plan, last_mask)
    slots = [
        sum(jnp.where(plan[r] == mask, r, 0) for r in range(ROUNDS))
        for mask in (1, last_mask, low_mask, high_mask)
    ]
    outs = [self_out, *(pair_out.at[slot] for slot in slots)]
    out_copies = []

    def lag_product(cross, first_set):
        result = dot(cross[...], lag_table[...])
        for row in range(cross.shape[0] // chans):
            q, a = divmod(row, share)
            staged[first_set + q, a] = result[row * chans : (row + 1) * chans, :LAGS]

    def copy_out(some):
        for q in some:
            copy = pltpu.make_async_copy(staged.at[q], outs[q], out_sems.at[q])
            copy.start()
            out_copies.append(copy)

    cross_spectra(chans, segs, left_ref, fixed_spectra, fixed_cross)
    whiten(free_products, *free_spectra)
    cross_spectra(chans, segs, left_ref, free_spectra, free_cross)
    lag_product(fixed_cross, 0)
    copy_out(range(FIXED_SETS))
    lag_product(free_cross, FIXED_SETS)
    copy_out(range(FIXED_SETS, sets))
    for copy in out_copies:
        copy.wait()


def correlate(plan, table_list, own, near, far, far_more, low, high, last_mask):
    chans, width = far.shape
    parts = len(far_more) + 1
    share = chans // parts
    length = width // SEGS_DEV
    sets = ROUNDS + 1
    *table_list, lag_table = table_list
    plan, lag_table = (
        pltpu.with_memory_space_constraint(array, pltpu.HBM) for array in (plan, lag_table)
    )
    return pl.pallas_call(
        functools.partial(correlate_kernel, parts, last_mask),
        out_shape=(
            jax.ShapeDtypeStruct((share, chans, LAGS), jnp.float32),
            jax.ShapeDtypeStruct((ROUNDS, share, chans, LAGS), jnp.float32),
        ),
        in_specs=[HBM] + [VMEM] * len(table_list) + [HBM] + [VMEM] * 2 + [HBM] * (parts + 2),
        out_specs=(HBM, HBM),
        scratch_shapes=[
            pltpu.SMEM(plan.shape, jnp.int32),
            pltpu.VMEM(lag_table.shape, jnp.bfloat16),
            pltpu.VMEM((3, *own.shape), jnp.bfloat16),
            pltpu.VMEM((parts - 1, chans, width), jnp.bfloat16),
            pltpu.VMEM((share, 3 * parts * SEGS_DEV, length // 2), jnp.float32),
            *spectra_scratch(FIXED_SETS, parts, chans, length),
            *spectra_scratch(sets - FIXED_SETS, parts, chans, length),
            pltpu.VMEM((FIXED_SETS * share * chans, length), jnp.bfloat16),
            pltpu.VMEM(((sets - FIXED_SETS) * share * chans, length), jnp.bfloat16),
            pltpu.VMEM((sets, share, chans, LAGS), jnp.float32),
            pltpu.SemaphoreType.DMA,
            pltpu.SemaphoreType.DMA,
            pltpu.SemaphoreType.DMA((3,)),
            pltpu.SemaphoreType.DMA((parts - 1,)),
            pltpu.SemaphoreType.DMA((sets,)),
        ],
        compiler_params=pltpu.CompilerParams(vmem_limit_bytes=KERNEL_VMEM),
    )(plan, *table_list, lag_table, own, far, near, low, high, *far_more)


def from_partner(block, mask):
    chan_count = lax.axis_size("chan")
    return lax.ppermute(block, "chan", [(g, g ^ mask) for g in range(chan_count)])


def from_times(block):
    parts = lax.axis_size("tm")
    return [
        lax.ppermute(block, "tm", [(t, (t + j) % parts) for t in range(parts)])
        for j in range(1, parts)
    ]


def on_device(samples, fir_taps, plan):
    chan_count, parts = lax.axis_size("chan"), lax.axis_size("tm")
    chans = samples.shape[0]
    near_mask, far_mask = 1, chan_count - 1
    free_masks = range(2, far_mask)

    far = from_partner(samples, far_mask)
    others = from_times(samples)
    branch, own, table_list = prepare(plan, fir_taps, samples, far_mask, parts)
    for j, piece in enumerate(others):
        own = lax.dynamic_update_slice(own, piece, ((j + 1) * chans, 0))

    def send(masks, far, own):
        far_more = from_times(far)
        near = from_partner(own, near_mask)
        if len(masks) == 2 and min(masks) >= chan_count // 2:
            free = [
                [from_partner(piece, mask ^ far_mask) for piece in (far, *far_more)]
                for mask in masks
            ]
            return near, far_more, *[jnp.concatenate(pieces, axis=0) for pieces in free]
        return near, far_more, *[from_partner(own, mask) for mask in masks]

    pairs = [(low, high) for high in free_masks for low in free_masks if low < high]
    if len(pairs) <= MAX_BRANCHES:
        branches = [functools.partial(send, pair) for pair in pairs]
        near, far_more, low, high = lax.switch(branch.reshape(()), branches, far, own)
    else:
        sends = [functools.partial(from_partner, mask=mask) for mask in free_masks]
        low, high = (
            lax.switch(mask - free_masks[0], sends, own) for mask in free_masks_of(plan, far_mask)
        )
        near, far_more = send((), far, own)
    return correlate(plan, table_list, own, near, far, far_more, low, high, far_mask)


def solution(mesh):
    in_specs = (P("chan", "tm"), P(), P())
    out_specs = (P(("chan", "tm"), None, None), P(None, ("chan", "tm"), None, None))
    return jax.shard_map(
        on_device, mesh=mesh, in_specs=in_specs, out_specs=out_specs, check_vma=False
    )
```

```python
import functools
import math

import jax
import jax.numpy as jnp
import ml_dtypes
import numpy as np
from jax import lax
from jax.experimental import pallas as pl
from jax.experimental.pallas import tpu as pltpu
from jax.sharding import PartitionSpec as P

SEGS_DEV = 2
LAGS = 129
ROUNDS = 4
LANE = 128
MAX_BRANCHES = 128
FIXED_SETS = 3
VMEM_LIMIT = 8 * 1024 * 1024
KERNEL_VMEM = 24 * 1024 * 1024
VMEM = pl.BlockSpec(memory_space=pltpu.VMEM)
SMEM = pl.BlockSpec(memory_space=pltpu.SMEM)
HBM = pl.BlockSpec(memory_space=pl.ANY)


def split_table(table):
    high = table.astype(ml_dtypes.bfloat16)
    low = (table - high.astype(np.float64)).astype(ml_dtypes.bfloat16)
    return np.concatenate([high, high, low], axis=0)


def tables(length):
    quarter = length // 4

    def packed(freqs, count):
        angle = 2.0 * math.pi / length * (np.arange(count)[:, None] * freqs[None, :] % length)
        return np.concatenate([np.cos(angle), -np.sin(angle)], axis=1)

    fours = 4 * np.arange(quarter // 2)
    odds = 2 * np.arange(quarter) + 1
    sum_table = packed(fours, quarter)
    sum_table[:, quarter // 2] = 1.0 - 2.0 * (np.arange(quarter) % 2)
    fold_tables = sum_table, packed(fours + 2, quarter), packed(odds, 2 * quarter)

    freqs = np.concatenate([fours, fours + 2, odds])[:, None]
    lag = (np.arange(LAGS) - LAGS // 2)[None, :]
    angle = 2.0 * math.pi / length * (lag * freqs % length)
    weight = np.where(freqs == 0, 1.0, 2.0) / length
    lag_cos = weight * np.cos(angle)
    lag_sin = weight * np.sin(angle)
    lag_sin[0] = (1.0 - 2.0 * (np.abs(lag[0]) % 2)) / length
    lag_table = np.zeros((length, 2 * LANE))
    lag_table[:, :LAGS] = np.concatenate([lag_cos, lag_sin], axis=0)
    return (*map(split_table, fold_tables), lag_table.astype(ml_dtypes.bfloat16))


def dot(left, right):
    return jnp.dot(left, right, preferred_element_type=jnp.float32)


def free_masks_of(plan, last_mask):
    masks = [plan[r] for r in range(ROUNDS)]
    free = [(mask != 1) & (mask != last_mask) for mask in masks]
    low = functools.reduce(
        jnp.minimum, [jnp.where(ok, mask, last_mask) for ok, mask in zip(free, masks)]
    )
    high = functools.reduce(jnp.maximum, [jnp.where(ok, mask, 0) for ok, mask in zip(free, masks)])
    return low, high


def prepare_kernel(last_mask, plan_hbm, taps_hbm, samples, *refs):
    tables_hbm, (branch, record, toep), refs = refs[:3], refs[3:6], refs[6:]
    tables_vmem, (plan, taps, scalar_sems, own_sem, table_sems) = refs[:3], refs[3:]
    chans = samples.shape[0]
    scalar_copies = [
        pltpu.make_async_copy(source, target, scalar_sems.at[i])
        for i, (source, target) in enumerate(((plan_hbm, plan), (taps_hbm, taps)))
    ]
    copies = [pltpu.make_async_copy(samples, record.at[pl.ds(0, chans)], own_sem)]
    copies += [
        pltpu.make_async_copy(table, table_vmem, table_sems.at[i])
        for i, (table, table_vmem) in enumerate(zip(tables_hbm, tables_vmem))
    ]
    for copy in scalar_copies + copies:
        copy.start()
    for copy in scalar_copies:
        copy.wait()
    low, high = (mask - 2 for mask in free_masks_of(plan, last_mask))
    branch[0] = high * (high - 1) // 2 + low

    lane = lax.broadcasted_iota(jnp.int32, (1, 2 * LANE), 1)
    base = jnp.zeros((1, 2 * LANE), jnp.float32)
    for j in range(taps.shape[0]):
        base = jnp.where(lane == j, taps[j], base)
    base = jnp.broadcast_to(base, (2 * LANE, 2 * LANE))
    toeplitz = pltpu.roll(base, LANE, 1, stride=1, stride_axis=0)[:, :LANE]
    toep_hi = toeplitz.astype(jnp.bfloat16)
    toep[:, :LANE] = toep_hi
    toep[:, LANE:] = (toeplitz - toep_hi.astype(jnp.float32)).astype(jnp.bfloat16)
    for copy in copies:
        copy.wait()


def prepare(plan, fir_taps, samples, last_mask, parts):
    chans, width = samples.shape
    *table_list, lag_table = tables(width // SEGS_DEV)
    plan, fir_taps, samples, *table_list = (
        pltpu.with_memory_space_constraint(jnp.asarray(array), pltpu.HBM)
        for array in (plan, fir_taps, samples, *table_list)
    )
    branch, record, toep, *table_list = pl.pallas_call(
        functools.partial(prepare_kernel, last_mask),
        out_shape=(
            jax.ShapeDtypeStruct((1,), jnp.int32),
            pltpu.VMEM((parts * chans, width), jnp.bfloat16),
            pltpu.VMEM((2 * LANE, 2 * LANE), jnp.bfloat16),
            *[pltpu.VMEM(table.shape, jnp.bfloat16) for table in table_list],
        ),
        in_specs=[HBM] * (3 + len(table_list)),
        out_specs=(SMEM,) + (VMEM,) * (2 + len(table_list)),
        scratch_shapes=[
            pltpu.SMEM(plan.shape, jnp.int32),
            pltpu.SMEM(fir_taps.shape, jnp.float32),
            pltpu.SemaphoreType.DMA((2,)),
            pltpu.SemaphoreType.DMA,
            pltpu.SemaphoreType.DMA((len(table_list),)),
        ],
        compiler_params=pltpu.CompilerParams(vmem_limit_bytes=VMEM_LIMIT),
    )(plan, fir_taps, samples, *table_list)
    return branch, record, (toep, *table_list, jnp.asarray(lag_table))


def add_spectra(columns_of, place, parts, shape, first_row, toep, folds):
    chans, width = shape
    tiles = width // SEGS_DEV // LANE
    quarter = tiles // 4
    for piece in range(parts):
        tail = columns_of((piece + 1) % parts, width - LANE, width)
        has_before = jnp.where(lax.rem(place + parts - piece, parts) == 0, 0.0, 1.0)
        tail = (tail.astype(jnp.float32) * has_before).astype(jnp.bfloat16)
        windows = [jnp.concatenate([tail, columns_of(piece, 0, LANE)], axis=1)]
        windows += [
            columns_of(piece, LANE * (k - 1), LANE * (k + 1)) for k in range(1, width // LANE)
        ]
        both = dot(jnp.concatenate(windows, axis=0), toep[...])
        filtered = both[:, :LANE] + both[:, LANE:]
        for s in range(SEGS_DEV):
            row = first_row + (piece * SEGS_DEV + s) * chans
            for k in range(quarter):
                at = [(s * tiles + j * quarter + k) * chans for j in range(4)]
                x = [filtered[lo : lo + chans] for lo in at]
                even, later = x[0] + x[2], x[1] + x[3]
                sums, diffs, odds = folds
                for ref, tile, value in (
                    (sums, k, even + later),
                    (diffs, k, even - later),
                    (odds, k, x[0] - x[2]),
                    (odds, k + quarter, x[1] - x[3]),
                ):
                    high = value.astype(jnp.bfloat16)
                    low = (value - high.astype(jnp.float32)).astype(jnp.bfloat16)
                    for j, part in enumerate((high, low, high)):
                        at = ref.shape[1] // 3 * j + LANE * tile
                        ref[row : row + chans, at : at + LANE] = part


def transform(folds, fold_tables):
    return [dot(fold[...], table[...]) for fold, table in zip(folds, fold_tables)]


def whiten(products, real_ref, imag_ref):
    real, imag = (
        jnp.concatenate(
            [p[:, p.shape[1] // 2 * j : p.shape[1] // 2 * (j + 1)] for p in products], axis=1
        )
        for j in range(2)
    )
    real_sq = real * real
    imag_sq = imag * imag
    energy = real_sq + imag_sq
    freqs = real.shape[1] + 1
    level = 0.1 / freqs * jnp.sum(energy, axis=1, keepdims=True) + 1e-06
    first, rest = slice(0, LANE), slice(LANE, freqs - 1)
    edge = lax.broadcasted_iota(jnp.int32, real[:, first].shape, 1) == 0
    inv_real = lax.rsqrt(jnp.where(edge, real_sq[:, first], energy[:, first]) + level)
    inv_imag = jnp.where(edge, lax.rsqrt(imag_sq[:, first] + level), inv_real)
    inverse = lax.rsqrt(energy[:, rest] + level)
    for ref, value, inv in ((real_ref, real, inv_real), (imag_ref, imag, inv_imag)):
        for lanes, factor in ((first, inv), (rest, inverse)):
            whitened = (value[:, lanes] * factor).astype(jnp.bfloat16)
            ref[:, lanes] = whitened.astype(jnp.float32)


def cross_spectra(chans, segs, left_ref, spectra, cross):
    real_ref, imag_ref = spectra
    rows, half = real_ref.shape
    rows_blk = segs * chans
    sets = rows // rows_blk
    for a in range(left_ref.shape[0]):
        for c in range(half // LANE):
            cols = slice(LANE * c, LANE * (c + 1))
            left = [
                jnp.broadcast_to(left_ref[a, j : j + 1, cols], (chans, LANE))
                for j in range(3 * segs)
            ]
            for q in range(sets):
                cos_part = sin_part = 0.0
                for s in range(segs):
                    row_b = slice(q * rows_blk + s * chans, q * rows_blk + (s + 1) * chans)
                    re_b, im_b = real_ref[row_b, cols], imag_ref[row_b, cols]
                    re_a, im_a, x_a = (left[segs * j + s] for j in range(3))
                    cos_part += re_a * re_b + im_a * im_b
                    sin_part += x_a * im_b - im_a * re_b
                at = (q * left_ref.shape[0] + a) * chans
                at_q = slice(at, at + chans)
                cross[at_q, cols] = cos_part.astype(jnp.bfloat16)
                cross[at_q, half + LANE * c : half + LANE * (c + 1)] = sin_part.astype(jnp.bfloat16)


def spectra_scratch(sets, parts, chans, length):
    rows, half = sets * parts * SEGS_DEV * chans, length // 2
    return [
        pltpu.VMEM((rows, 3 * length // 4), jnp.bfloat16),
        pltpu.VMEM((rows, 3 * length // 4), jnp.bfloat16),
        pltpu.VMEM((rows, 3 * half), jnp.bfloat16),
        pltpu.VMEM((rows, half), jnp.float32),
        pltpu.VMEM((rows, half), jnp.float32),
    ]


def rows_of_block(block, chans):
    return lambda piece, lo, hi: block[piece * chans : (piece + 1) * chans, lo:hi]


def correlate_kernel(parts, last_mask, plan_hbm, toep, *refs):
    fold_tables, lag_hbm, refs = refs[:3], refs[3], refs[4:]
    own, far, near, low, high, refs = *refs[:5], refs[5:]
    far_more, (self_out, pair_out), refs = refs[: parts - 1], refs[parts - 1 : parts + 1], refs[parts + 1 :]
    plan, lag_table, arrived, far_arrived, left_ref, *refs = refs
    fixed_folds, fixed_spectra, refs = refs[:3], refs[3:5], refs[5:]
    free_folds, free_spectra, refs = refs[:3], refs[3:5], refs[5:]
    real_ref, imag_ref = fixed_spectra
    fixed_cross, free_cross, staged, *refs = refs
    plan_sem, lag_sem, sems, far_sems, out_sems = refs

    chans, width = far.shape
    half = real_ref.shape[1]
    share = left_ref.shape[0]
    segs = parts * SEGS_DEV
    sets = ROUNDS + 1
    place = lax.axis_index("tm")
    copies = [
        pltpu.make_async_copy(source, arrived.at[i], sems.at[i])
        for i, source in enumerate((near, low, high))
    ]
    far_copies = [
        pltpu.make_async_copy(source, far_arrived.at[i], far_sems.at[i])
        for i, source in enumerate(far_more)
    ]
    lag_copy = pltpu.make_async_copy(lag_hbm, lag_table, lag_sem)
    plan_copy = pltpu.make_async_copy(plan_hbm, plan, plan_sem)
    for copy in far_copies + copies + [lag_copy, plan_copy]:
        copy.start()

    def far_columns(piece, lo, hi):
        return far[:, lo:hi] if piece == 0 else far_arrived[piece - 1, :, lo:hi]

    blocks = (
        rows_of_block(own, chans),
        rows_of_block(arrived.at[0], chans),
        far_columns,
        rows_of_block(arrived.at[1], chans),
        rows_of_block(arrived.at[2], chans),
    )
    for q, columns_of in enumerate(blocks):
        if q == 1:
            for copy in far_copies + copies + [plan_copy, lag_copy]:
                copy.wait()
        if q == FIXED_SETS:
            fixed_products = transform(fixed_folds, fold_tables)
        folds, at = (fixed_folds, q) if q < FIXED_SETS else (free_folds, q - FIXED_SETS)
        first_row = at * segs * chans
        add_spectra(columns_of, place, parts, far.shape, first_row, toep, folds)
    whiten(fixed_products, real_ref, imag_ref)
    free_products = transform(free_folds, fold_tables)

    def picked(ref, s):
        value = ref[s * chans : s * chans + share, :]
        for owner in range(1, parts):
            at = s * chans + owner * share
            value = jnp.where(place == owner, ref[at : at + share, :], value)
        return value

    edge = lax.broadcasted_iota(jnp.int32, (share, half), 1) == 0
    for s in range(segs):
        real_s, imag_s = picked(real_ref, s), picked(imag_ref, s)
        lefts = (real_s, jnp.where(edge, 0.0, imag_s), jnp.where(edge, imag_s, real_s))
        for j, value in enumerate(lefts):
            for a in range(share):
                left_ref[a, segs * j + s : segs * j + s + 1, :] = value[a : a + 1]

    low_mask, high_mask = free_masks_of(plan, last_mask)
    slots = [
        sum(jnp.where(plan[r] == mask, r, 0) for r in range(ROUNDS))
        for mask in (1, last_mask, low_mask, high_mask)
    ]
    outs = [self_out, *(pair_out.at[slot] for slot in slots)]
    out_copies = []

    def lag_product(cross, first_set):
        result = dot(cross[...], lag_table[...])
        for row in range(cross.shape[0] // chans):
            q, a = divmod(row, share)
            staged[first_set + q, a] = result[row * chans : (row + 1) * chans, :LAGS]

    def copy_out(some):
        for q in some:
            copy = pltpu.make_async_copy(staged.at[q], outs[q], out_sems.at[q])
            copy.start()
            out_copies.append(copy)

    cross_spectra(chans, segs, left_ref, fixed_spectra, fixed_cross)
    whiten(free_products, *free_spectra)
    cross_spectra(chans, segs, left_ref, free_spectra, free_cross)
    lag_product(fixed_cross, 0)
    copy_out(range(FIXED_SETS))
    lag_product(free_cross, FIXED_SETS)
    copy_out(range(FIXED_SETS, sets))
    for copy in out_copies:
        copy.wait()


def correlate(plan, table_list, own, near, far, far_more, low, high, last_mask):
    chans, width = far.shape
    parts = len(far_more) + 1
    share = chans // parts
    length = width // SEGS_DEV
    sets = ROUNDS + 1
    *table_list, lag_table = table_list
    plan, lag_table = (
        pltpu.with_memory_space_constraint(array, pltpu.HBM) for array in (plan, lag_table)
    )
    return pl.pallas_call(
        functools.partial(correlate_kernel, parts, last_mask),
        out_shape=(
            jax.ShapeDtypeStruct((share, chans, LAGS), jnp.float32),
            jax.ShapeDtypeStruct((ROUNDS, share, chans, LAGS), jnp.float32),
        ),
        in_specs=[HBM] + [VMEM] * len(table_list) + [HBM] + [VMEM] * 2 + [HBM] * (parts + 2),
        out_specs=(HBM, HBM),
        scratch_shapes=[
            pltpu.SMEM(plan.shape, jnp.int32),
            pltpu.VMEM(lag_table.shape, jnp.bfloat16),
            pltpu.VMEM((3, *own.shape), jnp.bfloat16),
            pltpu.VMEM((parts - 1, chans, width), jnp.bfloat16),
            pltpu.VMEM((share, 3 * parts * SEGS_DEV, length // 2), jnp.float32),
            *spectra_scratch(FIXED_SETS, parts, chans, length),
            *spectra_scratch(sets - FIXED_SETS, parts, chans, length),
            pltpu.VMEM((FIXED_SETS * share * chans, length), jnp.bfloat16),
            pltpu.VMEM(((sets - FIXED_SETS) * share * chans, length), jnp.bfloat16),
            pltpu.VMEM((sets, share, chans, LAGS), jnp.float32),
            pltpu.SemaphoreType.DMA,
            pltpu.SemaphoreType.DMA,
            pltpu.SemaphoreType.DMA((3,)),
            pltpu.SemaphoreType.DMA((parts - 1,)),
            pltpu.SemaphoreType.DMA((sets,)),
        ],
        compiler_params=pltpu.CompilerParams(vmem_limit_bytes=KERNEL_VMEM),
    )(plan, *table_list, lag_table, own, far, near, low, high, *far_more)


def from_partner(block, mask):
    chan_count = lax.axis_size("chan")
    return lax.ppermute(block, "chan", [(g, g ^ mask) for g in range(chan_count)])


def from_times(block):
    parts = lax.axis_size("tm")
    return [
        lax.ppermute(block, "tm", [(t, (t + j) % parts) for t in range(parts)])
        for j in range(1, parts)
    ]


def on_device(samples, fir_taps, plan):
    chan_count, parts = lax.axis_size("chan"), lax.axis_size("tm")
    chans = samples.shape[0]
    near_mask, far_mask = 1, chan_count - 1
    free_masks = range(2, far_mask)

    far = from_partner(samples, far_mask)
    others = from_times(samples)
    branch, own, table_list = prepare(plan, fir_taps, samples, far_mask, parts)
    for j, piece in enumerate(others):
        own = lax.dynamic_update_slice(own, piece, ((j + 1) * chans, 0))

    def send(masks, far, own):
        return from_partner(own, near_mask), from_times(far), *[from_partner(own, m) for m in masks]

    pairs = [(low, high) for high in free_masks for low in free_masks if low < high]
    if len(pairs) <= MAX_BRANCHES:
        branches = [functools.partial(send, pair) for pair in pairs]
        near, far_more, low, high = lax.switch(branch.reshape(()), branches, far, own)
    else:
        sends = [functools.partial(from_partner, mask=mask) for mask in free_masks]
        low, high = (
            lax.switch(mask - free_masks[0], sends, own) for mask in free_masks_of(plan, far_mask)
        )
        near, far_more = send((), far, own)
    return correlate(plan, table_list, own, near, far, far_more, low, high, far_mask)


def solution(mesh):
    in_specs = (P("chan", "tm"), P(), P())
    out_specs = (P(("chan", "tm"), None, None), P(None, ("chan", "tm"), None, None))
    return jax.shard_map(
        on_device, mesh=mesh, in_specs=in_specs, out_specs=out_specs, check_vma=False
    )
```

```python
import functools
import math

import jax
import jax.numpy as jnp
import ml_dtypes
import numpy as np
from jax import lax
from jax.experimental import pallas as pl
from jax.experimental.pallas import tpu as pltpu
from jax.sharding import PartitionSpec as P

SEGS_DEV = 2
LAGS = 129
ROUNDS = 4
LANE = 128
MAX_BRANCHES = 128
FIXED_SETS = 3
VMEM_LIMIT = 8 * 1024 * 1024
KERNEL_VMEM = 24 * 1024 * 1024
VMEM = pl.BlockSpec(memory_space=pltpu.VMEM)
SMEM = pl.BlockSpec(memory_space=pltpu.SMEM)
HBM = pl.BlockSpec(memory_space=pl.ANY)


def split_table(table):
    high = table.astype(ml_dtypes.bfloat16)
    low = (table - high.astype(np.float64)).astype(ml_dtypes.bfloat16)
    return np.concatenate([high, high, low], axis=0)


def tables(length):
    quarter = length // 4

    def packed(freqs, count):
        angle = 2.0 * math.pi / length * (np.arange(count)[:, None] * freqs[None, :] % length)
        return np.concatenate([np.cos(angle), -np.sin(angle)], axis=1)

    fours = 4 * np.arange(quarter // 2)
    odds = 2 * np.arange(quarter) + 1
    sum_table = packed(fours, quarter)
    sum_table[:, quarter // 2] = 1.0 - 2.0 * (np.arange(quarter) % 2)
    fold_tables = sum_table, packed(fours + 2, quarter), packed(odds, 2 * quarter)

    freqs = np.concatenate([fours, fours + 2, odds])[:, None]
    lag = (np.arange(LAGS) - LAGS // 2)[None, :]
    angle = 2.0 * math.pi / length * (lag * freqs % length)
    weight = np.where(freqs == 0, 1.0, 2.0) / length
    lag_cos = weight * np.cos(angle)
    lag_sin = weight * np.sin(angle)
    lag_sin[0] = (1.0 - 2.0 * (np.abs(lag[0]) % 2)) / length
    lag_table = np.zeros((length, 2 * LANE))
    lag_table[:, :LAGS] = np.concatenate([lag_cos, lag_sin], axis=0)
    return (*map(split_table, fold_tables), lag_table.astype(ml_dtypes.bfloat16))


def dot(left, right):
    return jnp.dot(left, right, preferred_element_type=jnp.float32)


def free_masks_of(plan, last_mask):
    masks = [plan[r] for r in range(ROUNDS)]
    free = [(mask != 1) & (mask != last_mask) for mask in masks]
    low = functools.reduce(
        jnp.minimum, [jnp.where(ok, mask, last_mask) for ok, mask in zip(free, masks)]
    )
    high = functools.reduce(jnp.maximum, [jnp.where(ok, mask, 0) for ok, mask in zip(free, masks)])
    return low, high


def prepare_kernel(last_mask, plan_hbm, taps_hbm, samples, *refs):
    tables_hbm, (branch, record, toep), refs = refs[:3], refs[3:6], refs[6:]
    tables_vmem, (plan, taps, scalar_sems, own_sem, table_sems) = refs[:3], refs[3:]
    chans = samples.shape[0]
    scalar_copies = [
        pltpu.make_async_copy(source, target, scalar_sems.at[i])
        for i, (source, target) in enumerate(((plan_hbm, plan), (taps_hbm, taps)))
    ]
    copies = [pltpu.make_async_copy(samples, record.at[pl.ds(0, chans)], own_sem)]
    copies += [
        pltpu.make_async_copy(table, table_vmem, table_sems.at[i])
        for i, (table, table_vmem) in enumerate(zip(tables_hbm, tables_vmem))
    ]
    for copy in scalar_copies + copies:
        copy.start()
    for copy in scalar_copies:
        copy.wait()
    low, high = (mask - 2 for mask in free_masks_of(plan, last_mask))
    branch[0] = high * (high - 1) // 2 + low

    lane = lax.broadcasted_iota(jnp.int32, (1, 2 * LANE), 1)
    base = jnp.zeros((1, 2 * LANE), jnp.float32)
    for j in range(taps.shape[0]):
        base = jnp.where(lane == j, taps[j], base)
    base = jnp.broadcast_to(base, (2 * LANE, 2 * LANE))
    toeplitz = pltpu.roll(base, LANE, 1, stride=1, stride_axis=0)[:, :LANE]
    toep_hi = toeplitz.astype(jnp.bfloat16)
    toep[:, :LANE] = toep_hi
    toep[:, LANE:] = (toeplitz - toep_hi.astype(jnp.float32)).astype(jnp.bfloat16)
    for copy in copies:
        copy.wait()


def prepare(plan, fir_taps, samples, last_mask, parts):
    chans, width = samples.shape
    *table_list, lag_table = tables(width // SEGS_DEV)
    plan, fir_taps, samples, *table_list = (
        pltpu.with_memory_space_constraint(jnp.asarray(array), pltpu.HBM)
        for array in (plan, fir_taps, samples, *table_list)
    )
    branch, record, toep, *table_list = pl.pallas_call(
        functools.partial(prepare_kernel, last_mask),
        out_shape=(
            jax.ShapeDtypeStruct((1,), jnp.int32),
            pltpu.VMEM((parts * chans, width), jnp.bfloat16),
            pltpu.VMEM((2 * LANE, 2 * LANE), jnp.bfloat16),
            *[pltpu.VMEM(table.shape, jnp.bfloat16) for table in table_list],
        ),
        in_specs=[HBM] * (3 + len(table_list)),
        out_specs=(SMEM,) + (VMEM,) * (2 + len(table_list)),
        scratch_shapes=[
            pltpu.SMEM(plan.shape, jnp.int32),
            pltpu.SMEM(fir_taps.shape, jnp.float32),
            pltpu.SemaphoreType.DMA((2,)),
            pltpu.SemaphoreType.DMA,
            pltpu.SemaphoreType.DMA((len(table_list),)),
        ],
        compiler_params=pltpu.CompilerParams(vmem_limit_bytes=VMEM_LIMIT),
    )(plan, fir_taps, samples, *table_list)
    return branch, record, (toep, *table_list, jnp.asarray(lag_table))


def add_spectra(columns_of, place, parts, shape, first_row, toep, folds):
    chans, width = shape
    tiles = width // SEGS_DEV // LANE
    quarter = tiles // 4
    for piece in range(parts):
        tail = columns_of((piece + 1) % parts, width - LANE, width)
        has_before = jnp.where(lax.rem(place + parts - piece, parts) == 0, 0.0, 1.0)
        tail = (tail.astype(jnp.float32) * has_before).astype(jnp.bfloat16)
        windows = [jnp.concatenate([tail, columns_of(piece, 0, LANE)], axis=1)]
        windows += [
            columns_of(piece, LANE * (k - 1), LANE * (k + 1)) for k in range(1, width // LANE)
        ]
        both = dot(jnp.concatenate(windows, axis=0), toep[...])
        filtered = both[:, :LANE] + both[:, LANE:]
        for s in range(SEGS_DEV):
            row = first_row + (piece * SEGS_DEV + s) * chans
            for k in range(quarter):
                at = [(s * tiles + j * quarter + k) * chans for j in range(4)]
                x = [filtered[lo : lo + chans] for lo in at]
                even, later = x[0] + x[2], x[1] + x[3]
                sums, diffs, odds = folds
                for ref, tile, value in (
                    (sums, k, even + later),
                    (diffs, k, even - later),
                    (odds, k, x[0] - x[2]),
                    (odds, k + quarter, x[1] - x[3]),
                ):
                    high = value.astype(jnp.bfloat16)
                    low = (value - high.astype(jnp.float32)).astype(jnp.bfloat16)
                    for j, part in enumerate((high, low, high)):
                        at = ref.shape[1] // 3 * j + LANE * tile
                        ref[row : row + chans, at : at + LANE] = part


def transform(folds, fold_tables):
    return [dot(fold[...], table[...]) for fold, table in zip(folds, fold_tables)]


def whiten(products, real_ref, imag_ref):
    real, imag = (
        jnp.concatenate(
            [p[:, p.shape[1] // 2 * j : p.shape[1] // 2 * (j + 1)] for p in products], axis=1
        )
        for j in range(2)
    )
    real_sq = real * real
    imag_sq = imag * imag
    energy = real_sq + imag_sq
    freqs = real.shape[1] + 1
    level = 0.1 / freqs * jnp.sum(energy, axis=1, keepdims=True) + 1e-06
    first, rest = slice(0, LANE), slice(LANE, freqs - 1)
    edge = lax.broadcasted_iota(jnp.int32, real[:, first].shape, 1) == 0
    inv_real = lax.rsqrt(jnp.where(edge, real_sq[:, first], energy[:, first]) + level)
    inv_imag = jnp.where(edge, lax.rsqrt(imag_sq[:, first] + level), inv_real)
    inverse = lax.rsqrt(energy[:, rest] + level)
    for ref, value, inv in ((real_ref, real, inv_real), (imag_ref, imag, inv_imag)):
        for lanes, factor in ((first, inv), (rest, inverse)):
            whitened = (value[:, lanes] * factor).astype(jnp.bfloat16)
            ref[:, lanes] = whitened.astype(jnp.float32)


def cross_spectra(chans, segs, left_ref, spectra, cross):
    real_ref, imag_ref = spectra
    rows, half = real_ref.shape
    rows_blk = segs * chans
    sets = rows // rows_blk
    for a in range(left_ref.shape[0]):
        for c in range(half // LANE):
            cols = slice(LANE * c, LANE * (c + 1))
            left = [
                jnp.broadcast_to(left_ref[a, j : j + 1, cols], (chans, LANE))
                for j in range(3 * segs)
            ]
            for q in range(sets):
                cos_part = sin_part = 0.0
                for s in range(segs):
                    row_b = slice(q * rows_blk + s * chans, q * rows_blk + (s + 1) * chans)
                    re_b, im_b = real_ref[row_b, cols], imag_ref[row_b, cols]
                    re_a, im_a, x_a = (left[segs * j + s] for j in range(3))
                    cos_part += re_a * re_b + im_a * im_b
                    sin_part += x_a * im_b - im_a * re_b
                at = (q * left_ref.shape[0] + a) * chans
                at_q = slice(at, at + chans)
                cross[at_q, cols] = cos_part.astype(jnp.bfloat16)
                cross[at_q, half + LANE * c : half + LANE * (c + 1)] = sin_part.astype(jnp.bfloat16)


def spectra_scratch(sets, parts, chans, length):
    rows, half = sets * parts * SEGS_DEV * chans, length // 2
    return [
        pltpu.VMEM((rows, 3 * length // 4), jnp.bfloat16),
        pltpu.VMEM((rows, 3 * length // 4), jnp.bfloat16),
        pltpu.VMEM((rows, 3 * half), jnp.bfloat16),
        pltpu.VMEM((rows, half), jnp.float32),
        pltpu.VMEM((rows, half), jnp.float32),
    ]


def rows_of_block(block, chans):
    return lambda piece, lo, hi: block[piece * chans : (piece + 1) * chans, lo:hi]


def correlate_kernel(parts, last_mask, plan_hbm, toep, *refs):
    fold_tables, lag_hbm, refs = refs[:3], refs[3], refs[4:]
    own, far, near, low, high, refs = *refs[:5], refs[5:]
    far_more, (self_out, pair_out), refs = refs[: parts - 1], refs[parts - 1 : parts + 1], refs[parts + 1 :]
    plan, lag_table, arrived, far_arrived, left_ref, *refs = refs
    fixed_folds, fixed_spectra, refs = refs[:3], refs[3:5], refs[5:]
    free_folds, free_spectra, refs = refs[:3], refs[3:5], refs[5:]
    real_ref, imag_ref = fixed_spectra
    fixed_cross, free_cross, staged, *refs = refs
    plan_sem, lag_sem, sems, far_sems, out_sems = refs

    chans, width = far.shape
    half = real_ref.shape[1]
    share = left_ref.shape[0]
    segs = parts * SEGS_DEV
    sets = ROUNDS + 1
    place = lax.axis_index("tm")
    copies = [
        pltpu.make_async_copy(source, arrived.at[i], sems.at[i])
        for i, source in enumerate((near, low, high))
    ]
    far_copies = [
        pltpu.make_async_copy(source, far_arrived.at[i], far_sems.at[i])
        for i, source in enumerate(far_more)
    ]
    lag_copy = pltpu.make_async_copy(lag_hbm, lag_table, lag_sem)
    plan_copy = pltpu.make_async_copy(plan_hbm, plan, plan_sem)
    for copy in far_copies + copies + [lag_copy, plan_copy]:
        copy.start()

    def far_columns(piece, lo, hi):
        return far[:, lo:hi] if piece == 0 else far_arrived[piece - 1, :, lo:hi]

    blocks = (
        rows_of_block(own, chans),
        rows_of_block(arrived.at[0], chans),
        far_columns,
        rows_of_block(arrived.at[1], chans),
        rows_of_block(arrived.at[2], chans),
    )
    for q, columns_of in enumerate(blocks):
        if q == 1:
            for copy in far_copies + copies + [plan_copy, lag_copy]:
                copy.wait()
        if q == FIXED_SETS:
            fixed_products = transform(fixed_folds, fold_tables)
        folds, at = (fixed_folds, q) if q < FIXED_SETS else (free_folds, q - FIXED_SETS)
        first_row = at * segs * chans
        add_spectra(columns_of, place, parts, far.shape, first_row, toep, folds)
    whiten(fixed_products, real_ref, imag_ref)
    free_products = transform(free_folds, fold_tables)

    def picked(ref, s):
        value = ref[s * chans : s * chans + share, :]
        for owner in range(1, parts):
            at = s * chans + owner * share
            value = jnp.where(place == owner, ref[at : at + share, :], value)
        return value

    edge = lax.broadcasted_iota(jnp.int32, (share, half), 1) == 0
    for s in range(segs):
        real_s, imag_s = picked(real_ref, s), picked(imag_ref, s)
        lefts = (real_s, jnp.where(edge, 0.0, imag_s), jnp.where(edge, imag_s, real_s))
        for j, value in enumerate(lefts):
            for a in range(share):
                left_ref[a, segs * j + s : segs * j + s + 1, :] = value[a : a + 1]

    low_mask, high_mask = free_masks_of(plan, last_mask)
    slots = [
        sum(jnp.where(plan[r] == mask, r, 0) for r in range(ROUNDS))
        for mask in (1, last_mask, low_mask, high_mask)
    ]
    outs = [self_out, *(pair_out.at[slot] for slot in slots)]
    out_copies = []

    def lag_product(cross, first_set):
        result = dot(cross[...], lag_table[...])
        for row in range(cross.shape[0] // chans):
            q, a = divmod(row, share)
            staged[first_set + q, a] = result[row * chans : (row + 1) * chans, :LAGS]

    def copy_out(some):
        for q in some:
            copy = pltpu.make_async_copy(staged.at[q], outs[q], out_sems.at[q])
            copy.start()
            out_copies.append(copy)

    cross_spectra(chans, segs, left_ref, fixed_spectra, fixed_cross)
    whiten(free_products, *free_spectra)
    cross_spectra(chans, segs, left_ref, free_spectra, free_cross)
    lag_product(fixed_cross, 0)
    copy_out(range(FIXED_SETS))
    lag_product(free_cross, FIXED_SETS)
    copy_out(range(FIXED_SETS, sets))
    for copy in out_copies:
        copy.wait()


def correlate(plan, table_list, own, near, far, far_more, low, high, last_mask):
    chans, width = far.shape
    parts = len(far_more) + 1
    share = chans // parts
    length = width // SEGS_DEV
    sets = ROUNDS + 1
    *table_list, lag_table = table_list
    plan, lag_table = (
        pltpu.with_memory_space_constraint(array, pltpu.HBM) for array in (plan, lag_table)
    )
    return pl.pallas_call(
        functools.partial(correlate_kernel, parts, last_mask),
        out_shape=(
            jax.ShapeDtypeStruct((share, chans, LAGS), jnp.float32),
            jax.ShapeDtypeStruct((ROUNDS, share, chans, LAGS), jnp.float32),
        ),
        in_specs=[HBM] + [VMEM] * len(table_list) + [HBM] + [VMEM] * 2 + [HBM] * (parts + 2),
        out_specs=(HBM, HBM),
        scratch_shapes=[
            pltpu.SMEM(plan.shape, jnp.int32),
            pltpu.VMEM(lag_table.shape, jnp.bfloat16),
            pltpu.VMEM((3, *own.shape), jnp.bfloat16),
            pltpu.VMEM((parts - 1, chans, width), jnp.bfloat16),
            pltpu.VMEM((share, 3 * parts * SEGS_DEV, length // 2), jnp.float32),
            *spectra_scratch(FIXED_SETS, parts, chans, length),
            *spectra_scratch(sets - FIXED_SETS, parts, chans, length),
            pltpu.VMEM((FIXED_SETS * share * chans, length), jnp.bfloat16),
            pltpu.VMEM(((sets - FIXED_SETS) * share * chans, length), jnp.bfloat16),
            pltpu.VMEM((sets, share, chans, LAGS), jnp.float32),
            pltpu.SemaphoreType.DMA,
            pltpu.SemaphoreType.DMA,
            pltpu.SemaphoreType.DMA((3,)),
            pltpu.SemaphoreType.DMA((parts - 1,)),
            pltpu.SemaphoreType.DMA((sets,)),
        ],
        compiler_params=pltpu.CompilerParams(vmem_limit_bytes=KERNEL_VMEM),
    )(plan, *table_list, lag_table, own, far, near, low, high, *far_more)


def from_partner(block, mask):
    chan_count = lax.axis_size("chan")
    return lax.ppermute(block, "chan", [(g, g ^ mask) for g in range(chan_count)])


def from_times(block):
    parts = lax.axis_size("tm")
    return [
        lax.ppermute(block, "tm", [(t, (t + j) % parts) for t in range(parts)])
        for j in range(1, parts)
    ]


def on_device(samples, fir_taps, plan):
    chan_count, parts = lax.axis_size("chan"), lax.axis_size("tm")
    chans = samples.shape[0]
    near_mask, far_mask = 1, chan_count - 1
    free_masks = range(2, far_mask)

    far = from_partner(samples, far_mask)
    others = from_times(samples)
    branch, own, table_list = prepare(plan, fir_taps, samples, far_mask, parts)
    *others, far = lax.optimization_barrier((*others, far))
    for j, piece in enumerate(others):
        own = lax.dynamic_update_slice(own, piece, ((j + 1) * chans, 0))

    def send(masks, far, own):
        return from_partner(own, near_mask), from_times(far), *[from_partner(own, m) for m in masks]

    pairs = [(low, high) for high in free_masks for low in free_masks if low < high]
    if len(pairs) <= MAX_BRANCHES:
        branches = [functools.partial(send, pair) for pair in pairs]
        near, far_more, low, high = lax.switch(branch.reshape(()), branches, far, own)
    else:
        sends = [functools.partial(from_partner, mask=mask) for mask in free_masks]
        low, high = (
            lax.switch(mask - free_masks[0], sends, own) for mask in free_masks_of(plan, far_mask)
        )
        near, far_more = send((), far, own)
    return correlate(plan, table_list, own, near, far, far_more, low, high, far_mask)


def solution(mesh):
    in_specs = (P("chan", "tm"), P(), P())
    out_specs = (P(("chan", "tm"), None, None), P(None, ("chan", "tm"), None, None))
    return jax.shard_map(
        on_device, mesh=mesh, in_specs=in_specs, out_specs=out_specs, check_vma=False
    )
```

```python
import functools
import math

import jax
import jax.numpy as jnp
import ml_dtypes
import numpy as np
from jax import lax
from jax.experimental import pallas as pl
from jax.experimental.pallas import tpu as pltpu
from jax.sharding import PartitionSpec as P

SEGS_DEV = 2
LAGS = 129
ROUNDS = 4
LANE = 128
MAX_BRANCHES = 128
FIXED_SETS = 3
VMEM_LIMIT = 8 * 1024 * 1024
KERNEL_VMEM = 24 * 1024 * 1024
VMEM = pl.BlockSpec(memory_space=pltpu.VMEM)
SMEM = pl.BlockSpec(memory_space=pltpu.SMEM)
HBM = pl.BlockSpec(memory_space=pl.ANY)


def split_table(table):
    high = table.astype(ml_dtypes.bfloat16)
    low = (table - high.astype(np.float64)).astype(ml_dtypes.bfloat16)
    return np.concatenate([high, high, low], axis=0)


def tables(length):
    quarter = length // 4

    def packed(freqs, count):
        angle = 2.0 * math.pi / length * (np.arange(count)[:, None] * freqs[None, :] % length)
        return np.concatenate([np.cos(angle), -np.sin(angle)], axis=1)

    fours = 4 * np.arange(quarter // 2)
    odds = 2 * np.arange(quarter) + 1
    sum_table = packed(fours, quarter)
    sum_table[:, quarter // 2] = 1.0 - 2.0 * (np.arange(quarter) % 2)
    fold_tables = sum_table, packed(fours + 2, quarter), packed(odds, 2 * quarter)

    freqs = np.concatenate([fours, fours + 2, odds])[:, None]
    lag = (np.arange(LAGS) - LAGS // 2)[None, :]
    angle = 2.0 * math.pi / length * (lag * freqs % length)
    weight = np.where(freqs == 0, 1.0, 2.0) / length
    lag_cos = weight * np.cos(angle)
    lag_sin = weight * np.sin(angle)
    lag_sin[0] = (1.0 - 2.0 * (np.abs(lag[0]) % 2)) / length
    lag_table = np.zeros((length, 2 * LANE))
    lag_table[:, :LAGS] = np.concatenate([lag_cos, lag_sin], axis=0)
    return (*map(split_table, fold_tables), lag_table.astype(ml_dtypes.bfloat16))


def dot(left, right):
    return jnp.dot(left, right, preferred_element_type=jnp.float32)


def free_masks_of(plan, last_mask):
    masks = [plan[r] for r in range(ROUNDS)]
    free = [(mask != 1) & (mask != last_mask) for mask in masks]
    low = functools.reduce(
        jnp.minimum, [jnp.where(ok, mask, last_mask) for ok, mask in zip(free, masks)]
    )
    high = functools.reduce(jnp.maximum, [jnp.where(ok, mask, 0) for ok, mask in zip(free, masks)])
    return low, high


def prepare_kernel(last_mask, plan_hbm, taps_hbm, samples, *refs):
    tables_hbm, (branch, record, toep), refs = refs[:3], refs[3:6], refs[6:]
    tables_vmem, (plan, taps, scalar_sems, own_sem, table_sems) = refs[:3], refs[3:]
    chans = samples.shape[0]
    scalar_copies = [
        pltpu.make_async_copy(source, target, scalar_sems.at[i])
        for i, (source, target) in enumerate(((plan_hbm, plan), (taps_hbm, taps)))
    ]
    copies = [pltpu.make_async_copy(samples, record.at[pl.ds(0, chans)], own_sem)]
    copies += [
        pltpu.make_async_copy(table, table_vmem, table_sems.at[i])
        for i, (table, table_vmem) in enumerate(zip(tables_hbm, tables_vmem))
    ]
    for copy in scalar_copies + copies:
        copy.start()
    for copy in scalar_copies:
        copy.wait()
    low, high = (mask - 2 for mask in free_masks_of(plan, last_mask))
    branch[0] = high * (high - 1) // 2 + low

    lane = lax.broadcasted_iota(jnp.int32, (1, 2 * LANE), 1)
    base = jnp.zeros((1, 2 * LANE), jnp.float32)
    for j in range(taps.shape[0]):
        base = jnp.where(lane == j, taps[j], base)
    base = jnp.broadcast_to(base, (2 * LANE, 2 * LANE))
    toeplitz = pltpu.roll(base, LANE, 1, stride=1, stride_axis=0)[:, :LANE]
    toep_hi = toeplitz.astype(jnp.bfloat16)
    toep[:, :LANE] = toep_hi
    toep[:, LANE:] = (toeplitz - toep_hi.astype(jnp.float32)).astype(jnp.bfloat16)
    for copy in copies:
        copy.wait()


def prepare(plan, fir_taps, samples, last_mask, parts):
    chans, width = samples.shape
    *table_list, lag_table = tables(width // SEGS_DEV)
    plan, fir_taps, samples, *table_list = (
        pltpu.with_memory_space_constraint(jnp.asarray(array), pltpu.HBM)
        for array in (plan, fir_taps, samples, *table_list)
    )
    branch, record, toep, *table_list = pl.pallas_call(
        functools.partial(prepare_kernel, last_mask),
        out_shape=(
            jax.ShapeDtypeStruct((1,), jnp.int32),
            pltpu.VMEM((parts * chans, width), jnp.bfloat16),
            pltpu.VMEM((2 * LANE, 2 * LANE), jnp.bfloat16),
            *[pltpu.VMEM(table.shape, jnp.bfloat16) for table in table_list],
        ),
        in_specs=[HBM] * (3 + len(table_list)),
        out_specs=(SMEM,) + (VMEM,) * (2 + len(table_list)),
        scratch_shapes=[
            pltpu.SMEM(plan.shape, jnp.int32),
            pltpu.SMEM(fir_taps.shape, jnp.float32),
            pltpu.SemaphoreType.DMA((2,)),
            pltpu.SemaphoreType.DMA,
            pltpu.SemaphoreType.DMA((len(table_list),)),
        ],
        compiler_params=pltpu.CompilerParams(vmem_limit_bytes=VMEM_LIMIT),
    )(plan, fir_taps, samples, *table_list)
    return branch, record, (toep, *table_list, jnp.asarray(lag_table))


def add_spectra(columns_of, place, parts, shape, first_row, toep, folds):
    chans, width = shape
    tiles = width // SEGS_DEV // LANE
    quarter = tiles // 4
    for piece in range(parts):
        tail = columns_of((piece + 1) % parts, width - LANE, width)
        has_before = jnp.where(lax.rem(place + parts - piece, parts) == 0, 0.0, 1.0)
        tail = (tail.astype(jnp.float32) * has_before).astype(jnp.bfloat16)
        windows = [jnp.concatenate([tail, columns_of(piece, 0, LANE)], axis=1)]
        windows += [
            columns_of(piece, LANE * (k - 1), LANE * (k + 1)) for k in range(1, width // LANE)
        ]
        both = dot(jnp.concatenate(windows, axis=0), toep[...])
        filtered = both[:, :LANE] + both[:, LANE:]
        for s in range(SEGS_DEV):
            row = first_row + (piece * SEGS_DEV + s) * chans
            for k in range(quarter):
                at = [(s * tiles + j * quarter + k) * chans for j in range(4)]
                x = [filtered[lo : lo + chans] for lo in at]
                even, later = x[0] + x[2], x[1] + x[3]
                sums, diffs, odds = folds
                for ref, tile, value in (
                    (sums, k, even + later),
                    (diffs, k, even - later),
                    (odds, k, x[0] - x[2]),
                    (odds, k + quarter, x[1] - x[3]),
                ):
                    high = value.astype(jnp.bfloat16)
                    low = (value - high.astype(jnp.float32)).astype(jnp.bfloat16)
                    for j, part in enumerate((high, low, high)):
                        at = ref.shape[1] // 3 * j + LANE * tile
                        ref[row : row + chans, at : at + LANE] = part


def transform(folds, fold_tables):
    return [dot(fold[...], table[...]) for fold, table in zip(folds, fold_tables)]


def whiten(products, real_ref, imag_ref):
    real, imag = (
        jnp.concatenate(
            [p[:, p.shape[1] // 2 * j : p.shape[1] // 2 * (j + 1)] for p in products], axis=1
        )
        for j in range(2)
    )
    real_sq = real * real
    imag_sq = imag * imag
    energy = real_sq + imag_sq
    freqs = real.shape[1] + 1
    level = 0.1 / freqs * jnp.sum(energy, axis=1, keepdims=True) + 1e-06
    first, rest = slice(0, LANE), slice(LANE, freqs - 1)
    edge = lax.broadcasted_iota(jnp.int32, real[:, first].shape, 1) == 0
    inv_real = lax.rsqrt(jnp.where(edge, real_sq[:, first], energy[:, first]) + level)
    inv_imag = jnp.where(edge, lax.rsqrt(imag_sq[:, first] + level), inv_real)
    inverse = lax.rsqrt(energy[:, rest] + level)
    for ref, value, inv in ((real_ref, real, inv_real), (imag_ref, imag, inv_imag)):
        for lanes, factor in ((first, inv), (rest, inverse)):
            whitened = (value[:, lanes] * factor).astype(jnp.bfloat16)
            ref[:, lanes] = whitened.astype(jnp.float32)


def cross_spectra(chans, segs, left_ref, spectra, cross, first_set=0):
    real_ref, imag_ref = spectra
    rows, half = real_ref.shape
    rows_blk = segs * chans
    sets = rows // rows_blk
    for a in range(left_ref.shape[0]):
        for c in range(half // LANE):
            cols = slice(LANE * c, LANE * (c + 1))
            left = [
                jnp.broadcast_to(left_ref[a, j : j + 1, cols], (chans, LANE))
                for j in range(3 * segs)
            ]
            for q in range(sets):
                cos_part = sin_part = 0.0
                for s in range(segs):
                    row_b = slice(q * rows_blk + s * chans, q * rows_blk + (s + 1) * chans)
                    re_b, im_b = real_ref[row_b, cols], imag_ref[row_b, cols]
                    re_a, im_a, x_a = (left[segs * j + s] for j in range(3))
                    cos_part += re_a * re_b + im_a * im_b
                    sin_part += x_a * im_b - im_a * re_b
                at = ((first_set + q) * left_ref.shape[0] + a) * chans
                at_q = slice(at, at + chans)
                cross[at_q, cols] = cos_part.astype(jnp.bfloat16)
                cross[at_q, half + LANE * c : half + LANE * (c + 1)] = sin_part.astype(jnp.bfloat16)


def spectra_scratch(sets, parts, chans, length):
    rows, half = sets * parts * SEGS_DEV * chans, length // 2
    return [
        pltpu.VMEM((rows, 3 * length // 4), jnp.bfloat16),
        pltpu.VMEM((rows, 3 * length // 4), jnp.bfloat16),
        pltpu.VMEM((rows, 3 * half), jnp.bfloat16),
        pltpu.VMEM((rows, half), jnp.float32),
        pltpu.VMEM((rows, half), jnp.float32),
    ]


def rows_of_block(block, chans):
    return lambda piece, lo, hi: block[piece * chans : (piece + 1) * chans, lo:hi]


def correlate_kernel(parts, last_mask, plan_hbm, toep, *refs):
    fold_tables, lag_hbm, refs = refs[:3], refs[3], refs[4:]
    own, far, near, low, high, refs = *refs[:5], refs[5:]
    far_more, (self_out, pair_out), refs = refs[: parts - 1], refs[parts - 1 : parts + 1], refs[parts + 1 :]
    plan, lag_table, arrived, far_arrived, left_ref, *refs = refs
    (own_folds, own_spectra), (fixed_folds, fixed_spectra), (free_folds, free_spectra) = (
        (refs[at : at + 3], refs[at + 3 : at + 5]) for at in (0, 5, 10)
    )
    refs = refs[15:]
    real_ref, imag_ref = own_spectra
    fixed_cross, free_cross, staged, *refs = refs
    plan_sem, lag_sem, sems, far_sems, out_sems = refs

    chans, width = far.shape
    half = real_ref.shape[1]
    share = left_ref.shape[0]
    segs = parts * SEGS_DEV
    sets = ROUNDS + 1
    place = lax.axis_index("tm")
    copies = [
        pltpu.make_async_copy(source, arrived.at[i], sems.at[i])
        for i, source in enumerate((near, low, high))
    ]
    far_copies = [
        pltpu.make_async_copy(source, far_arrived.at[i], far_sems.at[i])
        for i, source in enumerate(far_more)
    ]
    lag_copy = pltpu.make_async_copy(lag_hbm, lag_table, lag_sem)
    plan_copy = pltpu.make_async_copy(plan_hbm, plan, plan_sem)
    for copy in far_copies + copies + [lag_copy, plan_copy]:
        copy.start()

    def far_columns(piece, lo, hi):
        return far[:, lo:hi] if piece == 0 else far_arrived[piece - 1, :, lo:hi]

    blocks = (
        rows_of_block(own, chans),
        rows_of_block(arrived.at[0], chans),
        far_columns,
        rows_of_block(arrived.at[1], chans),
        rows_of_block(arrived.at[2], chans),
    )

    def add_all(first, last, folds):
        for q in range(first, last):
            row = (q - first) * segs * chans
            add_spectra(blocks[q], place, parts, far.shape, row, toep, folds)

    add_all(0, 1, own_folds)
    whiten(transform(own_folds, fold_tables), real_ref, imag_ref)

    def picked(ref, s):
        value = ref[s * chans : s * chans + share, :]
        for owner in range(1, parts):
            at = s * chans + owner * share
            value = jnp.where(place == owner, ref[at : at + share, :], value)
        return value

    edge = lax.broadcasted_iota(jnp.int32, (share, half), 1) == 0
    for s in range(segs):
        real_s, imag_s = picked(real_ref, s), picked(imag_ref, s)
        lefts = (real_s, jnp.where(edge, 0.0, imag_s), jnp.where(edge, imag_s, real_s))
        for j, value in enumerate(lefts):
            for a in range(share):
                left_ref[a, segs * j + s : segs * j + s + 1, :] = value[a : a + 1]

    for copy in far_copies + copies + [plan_copy, lag_copy]:
        copy.wait()
    add_all(1, FIXED_SETS, fixed_folds)
    fixed_products = transform(fixed_folds, fold_tables)
    add_all(FIXED_SETS, sets, free_folds)
    whiten(fixed_products, *fixed_spectra)
    free_products = transform(free_folds, fold_tables)

    low_mask, high_mask = free_masks_of(plan, last_mask)
    slots = [
        sum(jnp.where(plan[r] == mask, r, 0) for r in range(ROUNDS))
        for mask in (1, last_mask, low_mask, high_mask)
    ]
    outs = [self_out, *(pair_out.at[slot] for slot in slots)]
    out_copies = []

    def lag_product(cross, first_set):
        result = dot(cross[...], lag_table[...])
        for row in range(cross.shape[0] // chans):
            q, a = divmod(row, share)
            staged[first_set + q, a] = result[row * chans : (row + 1) * chans, :LAGS]

    def copy_out(some):
        for q in some:
            copy = pltpu.make_async_copy(staged.at[q], outs[q], out_sems.at[q])
            copy.start()
            out_copies.append(copy)

    cross_spectra(chans, segs, left_ref, own_spectra, fixed_cross)
    cross_spectra(chans, segs, left_ref, fixed_spectra, fixed_cross, 1)
    whiten(free_products, *free_spectra)
    cross_spectra(chans, segs, left_ref, free_spectra, free_cross)
    lag_product(fixed_cross, 0)
    copy_out(range(FIXED_SETS))
    lag_product(free_cross, FIXED_SETS)
    copy_out(range(FIXED_SETS, sets))
    for copy in out_copies:
        copy.wait()


def correlate(plan, table_list, own, near, far, far_more, low, high, last_mask):
    chans, width = far.shape
    parts = len(far_more) + 1
    share = chans // parts
    length = width // SEGS_DEV
    sets = ROUNDS + 1
    *table_list, lag_table = table_list
    plan, lag_table = (
        pltpu.with_memory_space_constraint(array, pltpu.HBM) for array in (plan, lag_table)
    )
    return pl.pallas_call(
        functools.partial(correlate_kernel, parts, last_mask),
        out_shape=(
            jax.ShapeDtypeStruct((share, chans, LAGS), jnp.float32),
            jax.ShapeDtypeStruct((ROUNDS, share, chans, LAGS), jnp.float32),
        ),
        in_specs=[HBM] + [VMEM] * len(table_list) + [HBM] + [VMEM] * 2 + [HBM] * (parts + 2),
        out_specs=(HBM, HBM),
        scratch_shapes=[
            pltpu.SMEM(plan.shape, jnp.int32),
            pltpu.VMEM(lag_table.shape, jnp.bfloat16),
            pltpu.VMEM((3, *own.shape), jnp.bfloat16),
            pltpu.VMEM((parts - 1, chans, width), jnp.bfloat16),
            pltpu.VMEM((share, 3 * parts * SEGS_DEV, length // 2), jnp.float32),
            *spectra_scratch(1, parts, chans, length),
            *spectra_scratch(FIXED_SETS - 1, parts, chans, length),
            *spectra_scratch(sets - FIXED_SETS, parts, chans, length),
            pltpu.VMEM((FIXED_SETS * share * chans, length), jnp.bfloat16),
            pltpu.VMEM(((sets - FIXED_SETS) * share * chans, length), jnp.bfloat16),
            pltpu.VMEM((sets, share, chans, LAGS), jnp.float32),
            pltpu.SemaphoreType.DMA,
            pltpu.SemaphoreType.DMA,
            pltpu.SemaphoreType.DMA((3,)),
            pltpu.SemaphoreType.DMA((parts - 1,)),
            pltpu.SemaphoreType.DMA((sets,)),
        ],
        compiler_params=pltpu.CompilerParams(vmem_limit_bytes=KERNEL_VMEM),
    )(plan, *table_list, lag_table, own, far, near, low, high, *far_more)


def from_partner(block, mask):
    chan_count = lax.axis_size("chan")
    return lax.ppermute(block, "chan", [(g, g ^ mask) for g in range(chan_count)])


def from_times(block):
    parts = lax.axis_size("tm")
    return [
        lax.ppermute(block, "tm", [(t, (t + j) % parts) for t in range(parts)])
        for j in range(1, parts)
    ]


def on_device(samples, fir_taps, plan):
    chan_count, parts = lax.axis_size("chan"), lax.axis_size("tm")
    chans = samples.shape[0]
    near_mask, far_mask = 1, chan_count - 1
    free_masks = range(2, far_mask)

    far = from_partner(samples, far_mask)
    others = from_times(samples)
    branch, own, table_list = prepare(plan, fir_taps, samples, far_mask, parts)
    for j, piece in enumerate(others):
        own = lax.dynamic_update_slice(own, piece, ((j + 1) * chans, 0))

    def send(masks, far, own):
        return from_partner(own, near_mask), from_times(far), *[from_partner(own, m) for m in masks]

    pairs = [(low, high) for high in free_masks for low in free_masks if low < high]
    if len(pairs) <= MAX_BRANCHES:
        branches = [functools.partial(send, pair) for pair in pairs]
        near, far_more, low, high = lax.switch(branch.reshape(()), branches, far, own)
    else:
        sends = [functools.partial(from_partner, mask=mask) for mask in free_masks]
        low, high = (
            lax.switch(mask - free_masks[0], sends, own) for mask in free_masks_of(plan, far_mask)
        )
        near, far_more = send((), far, own)
    return correlate(plan, table_list, own, near, far, far_more, low, high, far_mask)


def solution(mesh):
    in_specs = (P("chan", "tm"), P(), P())
    out_specs = (P(("chan", "tm"), None, None), P(None, ("chan", "tm"), None, None))
    return jax.shard_map(
        on_device, mesh=mesh, in_specs=in_specs, out_specs=out_specs, check_vma=False
    )
```

```python
import functools
import math

import jax
import jax.numpy as jnp
import ml_dtypes
import numpy as np
from jax import lax
from jax.experimental import pallas as pl
from jax.experimental.pallas import tpu as pltpu
from jax.sharding import PartitionSpec as P

SEGS_DEV = 2
LAGS = 129
ROUNDS = 4
LANE = 128
MAX_BRANCHES = 128
FIXED_SETS = 3
VMEM_LIMIT = 8 * 1024 * 1024
KERNEL_VMEM = 24 * 1024 * 1024
VMEM = pl.BlockSpec(memory_space=pltpu.VMEM)
SMEM = pl.BlockSpec(memory_space=pltpu.SMEM)
HBM = pl.BlockSpec(memory_space=pl.ANY)


def split_table(table):
    high = table.astype(ml_dtypes.bfloat16)
    low = (table - high.astype(np.float64)).astype(ml_dtypes.bfloat16)
    return np.concatenate([high, high, low], axis=0)


def tables(length):
    quarter = length // 4

    def packed(freqs, count):
        angle = 2.0 * math.pi / length * (np.arange(count)[:, None] * freqs[None, :] % length)
        return np.concatenate([np.cos(angle), -np.sin(angle)], axis=1)

    fours = 4 * np.arange(quarter // 2)
    odds = 2 * np.arange(quarter) + 1
    sum_table = packed(fours, quarter)
    sum_table[:, quarter // 2] = 1.0 - 2.0 * (np.arange(quarter) % 2)
    fold_tables = sum_table, packed(fours + 2, quarter), packed(odds, 2 * quarter)

    freqs = np.concatenate([fours, fours + 2, odds])[:, None]
    lag = (np.arange(LAGS) - LAGS // 2)[None, :]
    angle = 2.0 * math.pi / length * (lag * freqs % length)
    weight = np.where(freqs == 0, 1.0, 2.0) / length
    lag_cos = weight * np.cos(angle)
    lag_sin = weight * np.sin(angle)
    lag_sin[0] = (1.0 - 2.0 * (np.abs(lag[0]) % 2)) / length
    lag_table = np.zeros((length, 2 * LANE))
    lag_table[:, :LAGS] = np.concatenate([lag_cos, lag_sin], axis=0)
    return (*map(split_table, fold_tables), lag_table.astype(ml_dtypes.bfloat16))


def dot(left, right):
    return jnp.dot(left, right, preferred_element_type=jnp.float32)


def free_masks_of(plan, last_mask):
    masks = [plan[r] for r in range(ROUNDS)]
    free = [(mask != 1) & (mask != last_mask) for mask in masks]
    low = functools.reduce(
        jnp.minimum, [jnp.where(ok, mask, last_mask) for ok, mask in zip(free, masks)]
    )
    high = functools.reduce(jnp.maximum, [jnp.where(ok, mask, 0) for ok, mask in zip(free, masks)])
    return low, high


def prepare_kernel(last_mask, plan_hbm, taps_hbm, samples, *refs):
    tables_hbm, (branch, record, toep), refs = refs[:3], refs[3:6], refs[6:]
    tables_vmem, (plan, taps, scalar_sems, own_sem, table_sems) = refs[:3], refs[3:]
    chans = samples.shape[0]
    scalar_copies = [
        pltpu.make_async_copy(source, target, scalar_sems.at[i])
        for i, (source, target) in enumerate(((plan_hbm, plan), (taps_hbm, taps)))
    ]
    copies = [pltpu.make_async_copy(samples, record.at[pl.ds(0, chans)], own_sem)]
    copies += [
        pltpu.make_async_copy(table, table_vmem, table_sems.at[i])
        for i, (table, table_vmem) in enumerate(zip(tables_hbm, tables_vmem))
    ]
    for copy in scalar_copies + copies:
        copy.start()
    for copy in scalar_copies:
        copy.wait()
    low, high = (mask - 2 for mask in free_masks_of(plan, last_mask))
    branch[0] = high * (high - 1) // 2 + low

    lane = lax.broadcasted_iota(jnp.int32, (1, 2 * LANE), 1)
    base = jnp.zeros((1, 2 * LANE), jnp.float32)
    for j in range(taps.shape[0]):
        base = jnp.where(lane == j, taps[j], base)
    base = jnp.broadcast_to(base, (2 * LANE, 2 * LANE))
    toeplitz = pltpu.roll(base, LANE, 1, stride=1, stride_axis=0)[:, :LANE]
    toep_hi = toeplitz.astype(jnp.bfloat16)
    toep[:, :LANE] = toep_hi
    toep[:, LANE:] = (toeplitz - toep_hi.astype(jnp.float32)).astype(jnp.bfloat16)
    for copy in copies:
        copy.wait()


def prepare(plan, fir_taps, samples, last_mask, parts):
    chans, width = samples.shape
    *table_list, lag_table = tables(width // SEGS_DEV)
    plan, fir_taps, samples, *table_list = (
        pltpu.with_memory_space_constraint(jnp.asarray(array), pltpu.HBM)
        for array in (plan, fir_taps, samples, *table_list)
    )
    branch, record, toep, *table_list = pl.pallas_call(
        functools.partial(prepare_kernel, last_mask),
        out_shape=(
            jax.ShapeDtypeStruct((1,), jnp.int32),
            pltpu.VMEM((parts * chans, width), jnp.bfloat16),
            pltpu.VMEM((2 * LANE, 2 * LANE), jnp.bfloat16),
            *[pltpu.VMEM(table.shape, jnp.bfloat16) for table in table_list],
        ),
        in_specs=[HBM] * (3 + len(table_list)),
        out_specs=(SMEM,) + (VMEM,) * (2 + len(table_list)),
        scratch_shapes=[
            pltpu.SMEM(plan.shape, jnp.int32),
            pltpu.SMEM(fir_taps.shape, jnp.float32),
            pltpu.SemaphoreType.DMA((2,)),
            pltpu.SemaphoreType.DMA,
            pltpu.SemaphoreType.DMA((len(table_list),)),
        ],
        compiler_params=pltpu.CompilerParams(vmem_limit_bytes=VMEM_LIMIT),
    )(plan, fir_taps, samples, *table_list)
    return branch, record, (toep, *table_list, jnp.asarray(lag_table))


def add_spectra(columns_of, place, parts, shape, first_row, toep, folds):
    chans, width = shape
    tiles = width // SEGS_DEV // LANE
    quarter = tiles // 4
    for piece in range(parts):
        tail = columns_of((piece + 1) % parts, width - LANE, width)
        has_before = jnp.where(lax.rem(place + parts - piece, parts) == 0, 0.0, 1.0)
        tail = (tail.astype(jnp.float32) * has_before).astype(jnp.bfloat16)
        windows = [jnp.concatenate([tail, columns_of(piece, 0, LANE)], axis=1)]
        windows += [
            columns_of(piece, LANE * (k - 1), LANE * (k + 1)) for k in range(1, width // LANE)
        ]
        both = dot(jnp.concatenate(windows, axis=0), toep[...])
        filtered = both[:, :LANE] + both[:, LANE:]
        for s in range(SEGS_DEV):
            row = first_row + (piece * SEGS_DEV + s) * chans
            for k in range(quarter):
                at = [(s * tiles + j * quarter + k) * chans for j in range(4)]
                x = [filtered[lo : lo + chans] for lo in at]
                even, later = x[0] + x[2], x[1] + x[3]
                sums, diffs, odds = folds
                for ref, tile, value in (
                    (sums, k, even + later),
                    (diffs, k, even - later),
                    (odds, k, x[0] - x[2]),
                    (odds, k + quarter, x[1] - x[3]),
                ):
                    high = value.astype(jnp.bfloat16)
                    low = (value - high.astype(jnp.float32)).astype(jnp.bfloat16)
                    for j, part in enumerate((high, low, high)):
                        at = ref.shape[1] // 3 * j + LANE * tile
                        ref[row : row + chans, at : at + LANE] = part


def transform(folds, fold_tables):
    return [dot(fold[...], table[...]) for fold, table in zip(folds, fold_tables)]


def whiten(products, real_ref, imag_ref):
    real, imag = (
        jnp.concatenate(
            [p[:, p.shape[1] // 2 * j : p.shape[1] // 2 * (j + 1)] for p in products], axis=1
        )
        for j in range(2)
    )
    real_sq = real * real
    imag_sq = imag * imag
    energy = real_sq + imag_sq
    freqs = real.shape[1] + 1
    level = 0.1 / freqs * jnp.sum(energy, axis=1, keepdims=True) + 1e-06
    first, rest = slice(0, LANE), slice(LANE, freqs - 1)
    edge = lax.broadcasted_iota(jnp.int32, real[:, first].shape, 1) == 0
    inv_real = lax.rsqrt(jnp.where(edge, real_sq[:, first], energy[:, first]) + level)
    inv_imag = jnp.where(edge, lax.rsqrt(imag_sq[:, first] + level), inv_real)
    inverse = lax.rsqrt(energy[:, rest] + level)
    for ref, value, inv in ((real_ref, real, inv_real), (imag_ref, imag, inv_imag)):
        for lanes, factor in ((first, inv), (rest, inverse)):
            whitened = (value[:, lanes] * factor).astype(jnp.bfloat16)
            ref[:, lanes] = whitened.astype(jnp.float32)


def cross_spectra(chans, segs, left_ref, spectra, cross, first_set=0):
    real_ref, imag_ref = spectra
    rows, half = real_ref.shape
    rows_blk = segs * chans
    sets = rows // rows_blk
    for a in range(left_ref.shape[0]):
        for c in range(half // LANE):
            cols = slice(LANE * c, LANE * (c + 1))
            kinds = 3 if c == 0 else 2
            left = [
                jnp.broadcast_to(left_ref[a, j : j + 1, cols], (chans, LANE))
                for j in range(kinds * segs)
            ]
            for q in range(sets):
                cos_part = sin_part = 0.0
                for s in range(segs):
                    row_b = slice(q * rows_blk + s * chans, q * rows_blk + (s + 1) * chans)
                    re_b, im_b = real_ref[row_b, cols], imag_ref[row_b, cols]
                    re_a, im_a, x_a = (left[segs * (j % kinds) + s] for j in range(3))
                    cos_part += re_a * re_b + im_a * im_b
                    sin_part += x_a * im_b - im_a * re_b
                at = ((first_set + q) * left_ref.shape[0] + a) * chans
                at_q = slice(at, at + chans)
                cross[at_q, cols] = cos_part.astype(jnp.bfloat16)
                cross[at_q, half + LANE * c : half + LANE * (c + 1)] = sin_part.astype(jnp.bfloat16)


def spectra_scratch(sets, parts, chans, length):
    rows, half = sets * parts * SEGS_DEV * chans, length // 2
    return [
        pltpu.VMEM((rows, 3 * length // 4), jnp.bfloat16),
        pltpu.VMEM((rows, 3 * length // 4), jnp.bfloat16),
        pltpu.VMEM((rows, 3 * half), jnp.bfloat16),
        pltpu.VMEM((rows, half), jnp.float32),
        pltpu.VMEM((rows, half), jnp.float32),
    ]


def rows_of_block(block, chans):
    return lambda piece, lo, hi: block[piece * chans : (piece + 1) * chans, lo:hi]


def correlate_kernel(parts, last_mask, plan_hbm, toep, *refs):
    fold_tables, lag_hbm, refs = refs[:3], refs[3], refs[4:]
    own, far, near, low, high, refs = *refs[:5], refs[5:]
    far_more, (self_out, pair_out), refs = refs[: parts - 1], refs[parts - 1 : parts + 1], refs[parts + 1 :]
    plan, lag_table, arrived, far_arrived, left_ref, *refs = refs
    (own_folds, own_spectra), (fixed_folds, fixed_spectra), (free_folds, free_spectra) = (
        (refs[at : at + 3], refs[at + 3 : at + 5]) for at in (0, 5, 10)
    )
    refs = refs[15:]
    real_ref, imag_ref = own_spectra
    fixed_cross, free_cross, staged, *refs = refs
    plan_sem, lag_sem, sems, far_sems, out_sems = refs

    chans, width = far.shape
    half = real_ref.shape[1]
    share = left_ref.shape[0]
    segs = parts * SEGS_DEV
    sets = ROUNDS + 1
    place = lax.axis_index("tm")
    copies = [
        pltpu.make_async_copy(source, arrived.at[i], sems.at[i])
        for i, source in enumerate((near, low, high))
    ]
    far_copies = [
        pltpu.make_async_copy(source, far_arrived.at[i], far_sems.at[i])
        for i, source in enumerate(far_more)
    ]
    lag_copy = pltpu.make_async_copy(lag_hbm, lag_table, lag_sem)
    plan_copy = pltpu.make_async_copy(plan_hbm, plan, plan_sem)
    for copy in far_copies + copies + [lag_copy, plan_copy]:
        copy.start()

    def far_columns(piece, lo, hi):
        return far[:, lo:hi] if piece == 0 else far_arrived[piece - 1, :, lo:hi]

    blocks = (
        rows_of_block(own, chans),
        rows_of_block(arrived.at[0], chans),
        far_columns,
        rows_of_block(arrived.at[1], chans),
        rows_of_block(arrived.at[2], chans),
    )

    def add_all(first, last, folds):
        for q in range(first, last):
            row = (q - first) * segs * chans
            add_spectra(blocks[q], place, parts, far.shape, row, toep, folds)

    add_all(0, 1, own_folds)
    whiten(transform(own_folds, fold_tables), real_ref, imag_ref)

    def picked(ref, s):
        value = ref[s * chans : s * chans + share, :]
        for owner in range(1, parts):
            at = s * chans + owner * share
            value = jnp.where(place == owner, ref[at : at + share, :], value)
        return value

    edge = lax.broadcasted_iota(jnp.int32, (share, half), 1) == 0
    for s in range(segs):
        real_s, imag_s = picked(real_ref, s), picked(imag_ref, s)
        lefts = (real_s, jnp.where(edge, 0.0, imag_s), jnp.where(edge, imag_s, real_s))
        for j, value in enumerate(lefts):
            for a in range(share):
                left_ref[a, segs * j + s : segs * j + s + 1, :] = value[a : a + 1]

    for copy in far_copies + copies + [plan_copy, lag_copy]:
        copy.wait()
    add_all(1, FIXED_SETS, fixed_folds)
    fixed_products = transform(fixed_folds, fold_tables)
    add_all(FIXED_SETS, sets, free_folds)
    whiten(fixed_products, *fixed_spectra)
    free_products = transform(free_folds, fold_tables)

    low_mask, high_mask = free_masks_of(plan, last_mask)
    slots = [
        sum(jnp.where(plan[r] == mask, r, 0) for r in range(ROUNDS))
        for mask in (1, last_mask, low_mask, high_mask)
    ]
    outs = [self_out, *(pair_out.at[slot] for slot in slots)]
    out_copies = []

    def lag_product(cross, first_set):
        result = dot(cross[...], lag_table[...])
        for row in range(cross.shape[0] // chans):
            q, a = divmod(row, share)
            staged[first_set + q, a] = result[row * chans : (row + 1) * chans, :LAGS]

    def copy_out(some):
        for q in some:
            copy = pltpu.make_async_copy(staged.at[q], outs[q], out_sems.at[q])
            copy.start()
            out_copies.append(copy)

    cross_spectra(chans, segs, left_ref, own_spectra, fixed_cross)
    cross_spectra(chans, segs, left_ref, fixed_spectra, fixed_cross, 1)
    whiten(free_products, *free_spectra)
    cross_spectra(chans, segs, left_ref, free_spectra, free_cross)
    lag_product(fixed_cross, 0)
    copy_out(range(FIXED_SETS))
    lag_product(free_cross, FIXED_SETS)
    copy_out(range(FIXED_SETS, sets))
    for copy in out_copies:
        copy.wait()


def correlate(plan, table_list, own, near, far, far_more, low, high, last_mask):
    chans, width = far.shape
    parts = len(far_more) + 1
    share = chans // parts
    length = width // SEGS_DEV
    sets = ROUNDS + 1
    *table_list, lag_table = table_list
    plan, lag_table = (
        pltpu.with_memory_space_constraint(array, pltpu.HBM) for array in (plan, lag_table)
    )
    return pl.pallas_call(
        functools.partial(correlate_kernel, parts, last_mask),
        out_shape=(
            jax.ShapeDtypeStruct((share, chans, LAGS), jnp.float32),
            jax.ShapeDtypeStruct((ROUNDS, share, chans, LAGS), jnp.float32),
        ),
        in_specs=[HBM] + [VMEM] * len(table_list) + [HBM] + [VMEM] * 2 + [HBM] * (parts + 2),
        out_specs=(HBM, HBM),
        scratch_shapes=[
            pltpu.SMEM(plan.shape, jnp.int32),
            pltpu.VMEM(lag_table.shape, jnp.bfloat16),
            pltpu.VMEM((3, *own.shape), jnp.bfloat16),
            pltpu.VMEM((parts - 1, chans, width), jnp.bfloat16),
            pltpu.VMEM((share, 3 * parts * SEGS_DEV, length // 2), jnp.float32),
            *spectra_scratch(1, parts, chans, length),
            *spectra_scratch(FIXED_SETS - 1, parts, chans, length),
            *spectra_scratch(sets - FIXED_SETS, parts, chans, length),
            pltpu.VMEM((FIXED_SETS * share * chans, length), jnp.bfloat16),
            pltpu.VMEM(((sets - FIXED_SETS) * share * chans, length), jnp.bfloat16),
            pltpu.VMEM((sets, share, chans, LAGS), jnp.float32),
            pltpu.SemaphoreType.DMA,
            pltpu.SemaphoreType.DMA,
            pltpu.SemaphoreType.DMA((3,)),
            pltpu.SemaphoreType.DMA((parts - 1,)),
            pltpu.SemaphoreType.DMA((sets,)),
        ],
        compiler_params=pltpu.CompilerParams(vmem_limit_bytes=KERNEL_VMEM),
    )(plan, *table_list, lag_table, own, far, near, low, high, *far_more)


def from_partner(block, mask):
    chan_count = lax.axis_size("chan")
    return lax.ppermute(block, "chan", [(g, g ^ mask) for g in range(chan_count)])


def from_times(block):
    parts = lax.axis_size("tm")
    return [
        lax.ppermute(block, "tm", [(t, (t + j) % parts) for t in range(parts)])
        for j in range(1, parts)
    ]


def on_device(samples, fir_taps, plan):
    chan_count, parts = lax.axis_size("chan"), lax.axis_size("tm")
    chans = samples.shape[0]
    near_mask, far_mask = 1, chan_count - 1
    free_masks = range(2, far_mask)

    far = from_partner(samples, far_mask)
    others = from_times(samples)
    branch, own, table_list = prepare(plan, fir_taps, samples, far_mask, parts)
    for j, piece in enumerate(others):
        own = lax.dynamic_update_slice(own, piece, ((j + 1) * chans, 0))

    def send(masks, far, own):
        return from_partner(own, near_mask), from_times(far), *[from_partner(own, m) for m in masks]

    pairs = [(low, high) for high in free_masks for low in free_masks if low < high]
    if len(pairs) <= MAX_BRANCHES:
        branches = [functools.partial(send, pair) for pair in pairs]
        near, far_more, low, high = lax.switch(branch.reshape(()), branches, far, own)
    else:
        sends = [functools.partial(from_partner, mask=mask) for mask in free_masks]
        low, high = (
            lax.switch(mask - free_masks[0], sends, own) for mask in free_masks_of(plan, far_mask)
        )
        near, far_more = send((), far, own)
    return correlate(plan, table_list, own, near, far, far_more, low, high, far_mask)


def solution(mesh):
    in_specs = (P("chan", "tm"), P(), P())
    out_specs = (P(("chan", "tm"), None, None), P(None, ("chan", "tm"), None, None))
    return jax.shard_map(
        on_device, mesh=mesh, in_specs=in_specs, out_specs=out_specs, check_vma=False
    )
```
